32 devices in a mesh: dp: 4 (over y, x), ctx: 4 (over z), tensor: 2 (over core).
Axes of the slice: x: 2, y: 2, z: 4, core: 2. Of those that a mesh axis runs over, the one named last changes fastest.
Arguments:
- inputs: bfloat16 [2048, 2304], P(('dp', 'ctx')), may hold values from -6 to 6
- cotangent: bfloat16 [2048, 2304], P(('dp', 'ctx')), may hold values from -6 to 6
- lengths: int32 [4], replicated, may hold values from 256 to 512
- dealing: int32 [4], replicated, may hold values from 0 to 3, each once
- span_table: int32 [4, 8], replicated, may hold values from 0 to 7, as said below
- prenorm_gain: bfloat16 [2, 2304], P(None, ('dp', 'ctx')), may hold values from 0.5 to 1.5
- query_weight: bfloat16 [2, 2304, 2304], P(None, ('dp', 'ctx'), 'tensor'), may hold values from -0.125 to 0.125
- keys_weight: bfloat16 [2, 2304, 2304], P(None, ('dp', 'ctx'), 'tensor'), may hold values from -0.125 to 0.125
- values_weight: bfloat16 [2, 2304, 2304], P(None, ('dp', 'ctx'), 'tensor'), may hold values from -0.125 to 0.125
- project_weight: bfloat16 [2, 2304, 2304], P(None, 'tensor', ('dp', 'ctx')), may hold values from -2.5 to 2.5
- postnorm_gain: bfloat16 [2, 2304], P(None, ('dp', 'ctx')), may hold values from 0.5 to 1.5
- gating_weight: bfloat16 [2, 2304, 5760], P(None, ('dp', 'ctx'), 'tensor'), may hold values from -0.125 to 0.125
- upward_weight: bfloat16 [2, 2304, 5760], P(None, ('dp', 'ctx'), 'tensor'), may hold values from -0.125 to 0.125
- downward_weight: bfloat16 [2, 5760, 2304], P(None, 'tensor', ('dp', 'ctx')), may hold values from -0.5 to 0.5
Outputs:
- output: bfloat16 [2048, 2304], P(('dp', 'ctx'))
- grad_inputs: float32 [2048, 2304], P(('dp', 'ctx'))
- grad_prenorm: float32 [2, 2304], P(None, ('dp', 'ctx'))
- grad_query: float32 [2, 2304, 2304], P(None, ('dp', 'ctx'), 'tensor')
- grad_keys: float32 [2, 2304, 2304], P(None, ('dp', 'ctx'), 'tensor')
- grad_values: float32 [2, 2304, 2304], P(None, ('dp', 'ctx'), 'tensor')
- grad_project: float32 [2, 2304, 2304], P(None, 'tensor', ('dp', 'ctx'))
- grad_postnorm: float32 [2, 2304], P(None, ('dp', 'ctx'))
- grad_gating: float32 [2, 2304, 5760], P(None, ('dp', 'ctx'), 'tensor')
- grad_upward: float32 [2, 2304, 5760], P(None, ('dp', 'ctx'), 'tensor')
- grad_downward: float32 [2, 5760, 2304], P(None, 'tensor', ('dp', 'ctx'))
The draws below stay inside these ranges and needn't reach their ends.
Inputs may be any that keep to these rules, and one draw needn't show every extreme that they name: For each group g and each index c of ctx, span_table[g, 2 c] and span_table[g, 2 c + 1] are some j and 7 - j, in either order; every j below 4 appears once in a group.
All inputs are finite; a program needn't handle non-finite values.
Results may differ from the reference program's by a relative error of at most 0.035.
Values may be sent and summed in bfloat16 or wider, within the bound.
A program may use at most 448 MiB of HBM per device.

```python
import math
import jax
import jax.numpy as jnp
from jax import lax

D = 2304
HEADS = 36
FF = 5760
HEAD_DIM = 64
TOK_DEV = 128
LAYERS = 2
BLOCK = 128
MAX_LEN = 512
SEQS = 1
TOKENS = 2048
N_DP = 4
N_CTX = 4


def draw_lengths(key, part):
    key = jax.random.fold_in(key, 11)
    number = N_DP * SEQS
    values = jax.random.randint(key, (number,), MAX_LEN // 2, MAX_LEN + 1)
    values = values.at[0].set(MAX_LEN)
    values = values.at[1].set(MAX_LEN // 2)
    return values.astype(jnp.int32)


def draw_span_table(key, part):
    key = jax.random.fold_in(key, 23)

    def one_group(group_key):
        order_key, flip_key = jax.random.split(group_key)
        lower_half = jax.random.permutation(order_key, N_CTX).astype(jnp.int32)
        flip_bits = jax.random.randint(flip_key, (N_CTX,), 0, 2)
        upper_half = 2 * N_CTX - 1 - lower_half
        leading = jnp.where(flip_bits == 1, upper_half, lower_half)
        trailing = jnp.where(flip_bits == 1, lower_half, upper_half)
        return jnp.stack([leading, trailing], axis=1).reshape(2 * N_CTX)
    return jax.vmap(one_group)(jax.random.split(key, N_DP)).astype(jnp.int32)


def block_scale(rng, dims, shards, smallest, top_value):
    level = 1.0
    for dim, shards_of in shards:
        steps = jax.random.uniform(jax.random.fold_in(jax.random.fold_in(rng, 6), dim), (shards_of,), jnp.float32, smallest / len(shards), top_value / len(shards))
        level = level * jnp.repeat(jnp.exp(steps), dims[dim] // shards_of).reshape((-1,) + (1,) * (len(dims) - 1 - dim))
    return level


def bell_draw(stream_key, shape, scale, reach, pieces=(), kind=jnp.bfloat16):
    loudness = block_scale(stream_key, shape, pieces, -0.22, 0.18) if pieces else 1.0
    array = jax.random.normal(stream_key, shape, jnp.float32) * scale * loudness
    return jnp.minimum(jnp.maximum(array, -reach), reach).astype(kind)


def setup_inputs(seed: int = 0) -> dict:
    key_of = jax.random.split(jax.random.key(seed), 15)
    return {
        "inputs": bell_draw(key_of[0], (TOKENS, D), 1.0, 6.0, ((0, 16),)),
        "cotangent": bell_draw(key_of[1], (TOKENS, D), 1.0, 6.0, ((0, 16),)),
        "lengths": draw_lengths(jax.random.fold_in(key_of[14], 71), 0),
        "dealing": jax.random.permutation(key_of[3], N_DP * SEQS).astype(jnp.int32),
        "span_table": draw_span_table(jax.random.fold_in(key_of[14], 71), 0),
        "prenorm_gain": jnp.clip(1.0 + 0.1 * jax.random.normal(key_of[5], (LAYERS, D), jnp.float32), 0.5, 1.5).astype(jnp.bfloat16),
        "query_weight": bell_draw(key_of[6], (LAYERS, D, D), D ** -0.5, 0.125, ((1, 16), (2, 2))),
        "keys_weight": bell_draw(key_of[7], (LAYERS, D, D), D ** -0.5, 0.125, ((1, 16), (2, 2))),
        "values_weight": bell_draw(key_of[8], (LAYERS, D, D), D ** -0.5, 0.125, ((1, 16), (2, 2))),
        "project_weight": bell_draw(key_of[9], (LAYERS, D, D), 6 ** -0.5, 2.5, ((1, 2), (2, 16))),
        "postnorm_gain": jnp.clip(1.0 + 0.1 * jax.random.normal(key_of[10], (LAYERS, D), jnp.float32), 0.5, 1.5).astype(jnp.bfloat16),
        "gating_weight": bell_draw(key_of[11], (LAYERS, D, FF), D ** -0.5, 0.125, ((1, 16), (2, 2))),
        "upward_weight": bell_draw(key_of[12], (LAYERS, D, FF), D ** -0.5, 0.125, ((1, 16), (2, 2))),
        "downward_weight": bell_draw(key_of[13], (LAYERS, FF, D), 128 ** -0.5, 0.5, ((1, 2), (2, 16))),
    }


eps_norm = 1e-05
depth_scale = 1.4 / math.sqrt(40.0)
rope_base = 10000.0
masked_score = -1e+30

@jax.custom_vjp
def low(v):
    return lax.optimization_barrier(v.astype(jnp.bfloat16)).astype(jnp.float32)

@jax.custom_vjp
def low_back(v):
    return v

def low_keep(v):
    return (low(v), None)

def low_pass(kept, grad):
    return (grad,)

def back_keep(v):
    return (v, None)

def back_low(kept, grad):
    return (low(grad),)
low.defvjp(low_keep, low_pass)
low_back.defvjp(back_keep, back_low)

def matmul(left, right):
    return jnp.dot(left, right, precision=lax.Precision.HIGHEST)

def rms_norm(values, gain):
    return values * lax.rsqrt(lax.optimization_barrier(jnp.mean(values * values, axis=-1, keepdims=True)) + eps_norm) * gain

def rotate(values, position):
    half_dim = values.shape[-1] // 2
    inverse = rope_base ** (-jnp.arange(half_dim).astype(jnp.float32) / half_dim)
    angles = position.astype(jnp.float32)[:, None] * inverse[None, :]
    cosine = jnp.cos(angles)[:, None, :]
    sine_table = jnp.sin(angles)[:, None, :]
    front_half = values[..., :half_dim]
    back_half = values[..., half_dim:]
    return jnp.concatenate([front_half * cosine - back_half * sine_table, back_half * cosine + front_half * sine_table], axis=-1)

def group_layout(lengths, dealing, group_index, seq_count):
    chosen = lax.dynamic_slice_in_dim(dealing, (group_index * seq_count).astype(jnp.int32), seq_count)
    matches = chosen[:, None] == jnp.arange(lengths.shape[0], dtype=jnp.int32)[None, :]
    seq_lens = lax.optimization_barrier(jnp.sum(jnp.where(matches, lengths[None, :], 0), axis=1)).astype(jnp.int32)
    padded = ((seq_lens + BLOCK - 1) // BLOCK * BLOCK).astype(jnp.int32)
    starts = (jnp.cumsum(padded) - padded).astype(jnp.int32)
    return (starts, seq_lens)

def slot_facts(slots, starts, seq_lens):
    member = (lax.optimization_barrier(jnp.sum((slots[:, None] >= starts[None, :]).astype(jnp.int32), axis=1)) - 1).astype(jnp.int32)
    matches = member[:, None] == jnp.arange(starts.shape[0], dtype=jnp.int32)[None, :]
    anchor = lax.optimization_barrier(jnp.sum(jnp.where(matches, starts[None, :], 0), axis=1)).astype(jnp.int32)
    extent = lax.optimization_barrier(jnp.sum(jnp.where(matches, seq_lens[None, :], 0), axis=1)).astype(jnp.int32)
    position = (slots - anchor).astype(jnp.int32)
    return (slots, member, position, (position < extent).astype(jnp.int32))

def allowed(query_facts, key_facts):
    query_slot, query_member, query_position, query_valid = query_facts
    key_slot, key_member, key_position, key_valid = key_facts
    same_slot = query_slot[:, None] == key_slot[None, :]
    both_valid = (query_valid[:, None] == 1) & (key_valid[None, :] == 1)
    causal = (query_member[:, None] == key_member[None, :]) & (key_position[None, :] <= query_position[:, None])
    return same_slot | both_valid & causal

def attend(query, key, value, facts):
    group_rows = query.shape[0]
    block_size = 512 if group_rows % 512 == 0 else group_rows
    score_scale = 1.0 / math.sqrt(HEAD_DIM)

    def one_block(first_row):
        query_block = lax.dynamic_slice_in_dim(query, first_row, block_size)
        block_facts = tuple((lax.dynamic_slice_in_dim(fact_array, first_row, block_size) for fact_array in facts))
        scores = low_back(jnp.einsum('qhd,khd->hqk', query_block, key, precision=lax.Precision.HIGHEST)) * score_scale
        allowed_pairs = allowed(block_facts, facts)
        scores = jnp.where(allowed_pairs[None], scores, masked_score)
        shifted = scores - lax.optimization_barrier(jnp.max(scores, axis=-1, keepdims=True))
        softmax_terms = jnp.exp(shifted)
        softmax_terms = softmax_terms / lax.optimization_barrier(jnp.sum(softmax_terms, axis=-1, keepdims=True))
        return jnp.einsum('hqk,khd->qhd', low(softmax_terms), value, precision=lax.Precision.HIGHEST)
    firsts = jnp.arange(group_rows // block_size, dtype=jnp.int32) * block_size
    return lax.map(jax.checkpoint(one_block), firsts).reshape(group_rows, -1)

def layer(values, params, facts):
    gain_front, query_full, keys_full, values_full, project_full, gain_back, gating_full, upward_full, downward_full = params
    group_rows = values.shape[0]
    position = facts[2]
    head_shape = (group_rows, HEADS, HEAD_DIM)
    normed = low(rms_norm(values, gain_front))
    query = low(rotate(low_back(matmul(normed, query_full)).reshape(head_shape), position))
    key = low(rotate(low_back(matmul(normed, keys_full)).reshape(head_shape), position))
    value = low(low_back(matmul(normed, values_full))).reshape(head_shape)
    mixed_heads = low(low_back(attend(query, key, value, facts)))
    hidden = values + depth_scale * low_back(matmul(mixed_heads, project_full))
    normed_two = low(rms_norm(hidden, gain_back))
    gating = low_back(matmul(normed_two, gating_full))
    upward = low_back(matmul(normed_two, upward_full))
    activated = low(jax.nn.silu(gating) * upward)
    return hidden + depth_scale * low_back(matmul(activated, downward_full))

def reference(inputs, cotangent, lengths, dealing, span_table, prenorm_gain, query_weight, keys_weight, values_weight, project_weight, postnorm_gain, gating_weight, upward_weight, downward_weight):
    params = tuple((weight.astype(jnp.float32) for weight in (prenorm_gain, query_weight, keys_weight, values_weight, project_weight, postnorm_gain, gating_weight, upward_weight, downward_weight)))
    group_rows = inputs.shape[0] // N_DP
    seq_count = lengths.shape[0] // N_DP
    half_span = TOK_DEV // 2
    row_index = jnp.arange(group_rows, dtype=jnp.int32)
    rows_in = inputs.astype(jnp.float32).reshape(N_DP, group_rows, -1)
    rows_cot = cotangent.astype(jnp.float32).reshape(N_DP, group_rows, -1)

    def per_group(totals, members):
        group_in, group_cot, group_index = members
        starts, seq_lens = group_layout(lengths, dealing, group_index, seq_count)
        span_row = lax.dynamic_index_in_dim(span_table, group_index, 0, keepdims=False)
        matches = (row_index // half_span)[:, None] == jnp.arange(span_row.shape[0], dtype=jnp.int32)[None, :]
        span_of = lax.optimization_barrier(jnp.sum(jnp.where(matches, span_row[None, :], 0), axis=1)).astype(jnp.int32)
        slots = (span_of * half_span + row_index % half_span).astype(jnp.int32)
        facts = slot_facts(slots, starts, seq_lens)

        def forward(values, weights):
            for layer_index in range(LAYERS):
                values = layer(values, tuple((weight[layer_index] for weight in weights)), facts)
            return values
        result, pull = jax.vjp(forward, group_in, params)
        grad_rows, grad_params = pull(group_cot)
        totals = jax.tree.map(jnp.add, totals, grad_params)
        return (totals, (result, grad_rows))
    zeros = jax.tree.map(jnp.zeros_like, params)
    totals, (results, grads) = lax.scan(per_group, zeros, (rows_in, rows_cot, jnp.arange(N_DP, dtype=jnp.int32)))
    width = inputs.shape[1]
    return (results.reshape(-1, width).astype(jnp.bfloat16), grads.reshape(-1, width), totals[0], totals[1], totals[2], totals[3], totals[4], totals[5], totals[6], totals[7], totals[8])
```

```python
import math

import functools

import jax
import jax.numpy as jnp
from jax import lax
from jax.experimental import pallas as pl
from jax.experimental.pallas import tpu as pltpu
from jax.sharding import PartitionSpec as P

MESH = pl.DeviceIdType.MESH

HEAD_DIM = 64
LAYERS = 2
BLOCK = 128
LANES = 128

eps_norm = 1e-05
depth_scale = 1.4 / math.sqrt(40.0)
rope_base = 10000.0
masked_score = -1e30
score_scale = 1.0 / math.sqrt(HEAD_DIM)


def times(left, right):
    return jnp.dot(left, right, preferred_element_type=jnp.float32)


def times_transposed(left, right):
    return lax.dot_general(
        left, right, (((1,), (1,)), ((), ())), preferred_element_type=jnp.float32
    )


def outer_rows(left, right):
    return lax.dot_general(
        left, right, (((0,), (0,)), ((), ())), preferred_element_type=jnp.float32
    )


def rms_parts(values):
    inverse = lax.rsqrt(jnp.mean(values * values, axis=-1, keepdims=True) + eps_norm)
    return (values * inverse, inverse)


def norm_backward(values, gain, grad_normed):
    scaled, inverse = rms_parts(values)
    gain_grad = jnp.sum(grad_normed * scaled, axis=0, keepdims=True)
    grad_scaled = grad_normed * gain
    return (
        gain_grad,
        inverse * (grad_scaled - scaled * jnp.mean(grad_scaled * scaled, axis=-1, keepdims=True)),
    )


def rope_tables(position, half_dim):
    inverse = rope_base ** (-jnp.arange(half_dim).astype(jnp.float32) / half_dim)
    angles = position.astype(jnp.float32)[:, None] * inverse[None, :]
    return (jnp.cos(angles)[:, None, :], jnp.sin(angles)[:, None, :])


def rotate(values, tables, direction):
    cosine, sine_table = tables
    half_dim = values.shape[-1] // 2
    front_half = values[..., :half_dim]
    back_half = values[..., half_dim:]
    return jnp.concatenate(
        [
            front_half * cosine - direction * back_half * sine_table,
            back_half * cosine + direction * front_half * sine_table,
        ],
        axis=-1,
    )


def group_layout(lengths, dealing, group_index, seq_count):
    chosen = lax.dynamic_slice_in_dim(dealing, group_index * seq_count, seq_count)
    matches = chosen[:, None] == jnp.arange(lengths.shape[0], dtype=jnp.int32)[None, :]
    seq_lens = jnp.sum(jnp.where(matches, lengths[None, :], 0), axis=1)
    padded = (seq_lens + BLOCK - 1) // BLOCK * BLOCK
    starts = jnp.cumsum(padded) - padded
    return (starts, seq_lens)


def slots_for(number, span_row, half_span):
    rows = jnp.arange(number, dtype=jnp.int32)
    matches = (rows // half_span)[:, None] == jnp.arange(span_row.shape[0], dtype=jnp.int32)[None, :]
    span_of = jnp.sum(jnp.where(matches, span_row[None, :], 0), axis=1)
    return span_of * half_span + rows % half_span


def slot_facts(slots, starts, seq_lens):
    member = jnp.sum((slots[:, None] >= starts[None, :]).astype(jnp.int32), axis=1) - 1
    matches = member[:, None] == jnp.arange(starts.shape[0], dtype=jnp.int32)[None, :]
    anchor = jnp.sum(jnp.where(matches, starts[None, :], 0), axis=1)
    extent = jnp.sum(jnp.where(matches, seq_lens[None, :], 0), axis=1)
    position = slots - anchor
    return (slots, member, position, (position < extent).astype(jnp.int32))


def allowed(query_facts, key_facts):
    query_slot, query_member, query_position, query_valid = query_facts
    key_slot, key_member, key_position, key_valid = key_facts
    same_slot = query_slot[:, None] == key_slot[None, :]
    both_valid = (query_valid[:, None] == 1) & (key_valid[None, :] == 1)
    causal = (query_member[:, None] == key_member[None, :]) & (
        key_position[None, :] <= query_position[:, None]
    )
    return same_slot | both_valid & causal


class Plan:
    def __init__(self, n_dp, n_ctx, columns, hidden):
        self.n_dp, self.n_ctx = n_dp, n_ctx
        heads = columns // HEAD_DIM
        self.head_cuts = [i * heads // n_ctx for i in range(n_ctx + 1)]
        self.head_count = max(b - a for a, b in zip(self.head_cuts, self.head_cuts[1:]))
        self.head_width = self.head_count * HEAD_DIM
        self.unit_cuts = [i * hidden // n_ctx for i in range(n_ctx + 1)]
        units = max(b - a for a, b in zip(self.unit_cuts, self.unit_cuts[1:]))
        self.unit_width = (units + LANES - 1) // LANES * LANES


def cut_windows(weight, cuts, width):
    pieces = []
    for first, last in zip(cuts, cuts[1:]):
        pieces.append(jnp.pad(weight[:, first:last], ((0, 0), (0, width - (last - first)))))
    return jnp.stack(pieces)


def join_windows(windows, cuts):
    return jnp.concatenate(
        [windows[i, :, : last - first] for i, (first, last) in enumerate(zip(cuts, cuts[1:]))], axis=1
    )


def spread_weights(blocks):
    return lax.all_gather(blocks.reshape(-1, blocks.shape[-1]), "dp", axis=0, tiled=True)


def reduce_grads(full, n_ctx):
    own = lax.psum_scatter(full, "dp", scatter_dimension=0, tiled=True)
    return own.reshape(n_ctx, -1, own.shape[-1])


def gather_rows(piece):
    return lax.all_gather(piece, ("ctx", "tensor"), axis=0, tiled=True)


def scatter_rows(partial_sum):
    return lax.psum_scatter(
        partial_sum.astype(jnp.bfloat16), ("ctx", "tensor"), scatter_dimension=0, tiled=True
    ).astype(jnp.float32)


SLOT = 16
SKEW = 3


def place():
    return lax.axis_index("dp"), lax.axis_index("ctx"), lax.axis_index("tensor")


def slot_rows(base, index):
    return pl.ds(pl.multiple_of(base + index * SLOT, SLOT), SLOT)


def send(src, dst, send_sem, recv_sem, target):
    return pltpu.make_async_remote_copy(
        src_ref=src, dst_ref=dst, send_sem=send_sem, recv_sem=recv_sem, device_id=target, device_id_type=MESH
    )


def greet(d, c, t):
    barrier = pltpu.get_barrier_semaphore()
    for other in ((d, c, 1 - t), (d, c ^ 1, t), (d, c ^ 2, t), (d, c ^ 3, t)):
        pl.semaphore_signal(barrier, inc=1, device_id=other, device_id_type=MESH)
    pl.semaphore_wait(barrier, 4)


class Exchange:
    semaphores = 7

    @staticmethod
    def result(source):
        return jax.ShapeDtypeStruct(source.shape, source.dtype)

    def __init__(self, source, result, sems):
        d, c, t = place()
        self.own = pltpu.make_async_copy(source.at[c], result.at[c], sems.at[6])
        self.copies = [
            send(source.at[c ^ k], result.at[c], sems.at[k - 1], sems.at[k + 2], (d, c ^ k, t)) for k in (3, 2, 1)
        ]

    def start(self):
        for copy in self.copies:
            copy.start()
        self.own.start()

    def finish(self):
        for copy in self.copies:
            copy.wait()
        self.own.wait()


class Collect:
    semaphores = 13

    @staticmethod
    def result(source):
        return jax.ShapeDtypeStruct((4 * source.shape[0], source.shape[1]), source.dtype)

    def __init__(self, source, result, sems):
        d, c, t = place()
        block = source.shape[0]
        half = block // 2

        def piece(chip, core):
            return pl.ds(pl.multiple_of(chip * block + core * half, half), half)

        self.own = pltpu.make_async_copy(source, result.at[pl.ds(pl.multiple_of(c * block, block), block)], sems.at[12])
        mine = source.at[pl.ds(pl.multiple_of(t * half, half), half)]
        self.copies, self.onward = [], []
        for k in (3, 2, 1):
            self.copies.append(
                send(mine, result.at[piece(c, t)], sems.at[k - 1], sems.at[k + 2], (d, c ^ k, t))
            )
            there = result.at[piece(c ^ k, t)]
            self.onward.append(send(there, there, sems.at[k + 5], sems.at[k + 8], (d, c, 1 - t)))

    def start(self):
        for copy in self.copies:
            copy.start()
        self.own.start()

    def finish(self):
        for copy, onward in zip(self.copies, self.onward):
            copy.wait_recv()
            onward.start()
        for copy, onward in zip(self.copies, self.onward):
            copy.wait_send()
            onward.wait()
        self.own.wait()


def make_jobs(kinds, sources, results, sem_refs):
    return [kind(*refs) for kind, *refs in zip(kinds, sources, results, sem_refs)]


def jobs_kernel(kinds, *refs):
    n = len(kinds)
    greet(*place())
    jobs = make_jobs(kinds, refs[:n], refs[n : 2 * n], refs[2 * n :])
    for job in jobs:
        job.start()
    for job in jobs:
        job.finish()


def jobs_call(number, jobs):
    hbm = pl.BlockSpec(memory_space=pl.ANY)
    kinds = [kind for kind, _ in jobs]
    return pl.pallas_call(
        functools.partial(jobs_kernel, kinds),
        name="moves",
        out_shape=tuple(kind.result(source) for kind, source in jobs),
        in_specs=[hbm] * len(jobs),
        out_specs=tuple([hbm] * len(jobs)),
        scratch_shapes=[pltpu.SemaphoreType.DMA((kind.semaphores,)) for kind in kinds],
        compiler_params=pltpu.CompilerParams(collective_id=number, has_side_effects=True),
        cost_estimate=pl.CostEstimate(flops=10**9, bytes_accessed=100 * 10**6, transcendentals=0),
    )(*[source for _, source in jobs])


def line_kernel(settle, with_gather, n_settle_in, n_settle_out, kinds, *refs):
    n_jobs = len(kinds)
    partial_ref, refs = refs[0], refs[1:]
    settle_in, refs = refs[:n_settle_in], refs[n_settle_in:]
    job_sources, refs = refs[:n_jobs], refs[n_jobs:]
    settle_out, refs = refs[:n_settle_out], refs[n_settle_out:]
    if with_gather:
        whole_ref, refs = refs[0], refs[1:]
    job_results, refs = refs[:n_jobs], refs[n_jobs:]
    acc_up, acc_down, in_up, in_down, sib, stage, send_sems, sib_sems, up_sems, down_sems, back_up, back_down = refs[:12]
    whole_sems = refs[12]
    d, c, t = place()
    block = acc_up.shape[0]
    slots = block // SLOT
    sibling, above, below = (d, c, 1 - t), (d, c + 1, t), (d, c - 1, t)
    down_base, up_base = t * block, (2 + t) * block
    low, high = c > 0, c < 3

    greet(d, c, t)
    half = block // 2
    for part in range(2):
        for which, base in ((0, (1 - t) * block), (1, (3 - t) * block)):
            rows = pl.ds(pl.multiple_of(base + part * half, half), half)
            copy = send(
                partial_ref.at[rows],
                sib.at[which, pl.ds(part * half, half)],
                send_sems.at[0],
                sib_sems.at[which, part],
                sibling,
            )
            copy.start()
    middle = low & high
    jobs = make_jobs(kinds, job_sources, job_results, refs[13:])
    for job in jobs:
        job.start()

    @pl.when(middle)
    def _():
        for ref in settle_out:
            ref[...] = jnp.zeros(ref.shape, ref.dtype)

    def own_term(which, base, index):
        @pl.when(index % (slots // 2) == 0)
        def _():
            pltpu.make_async_copy(
                sib.at[which, pl.ds(0, half)], sib.at[which, pl.ds(0, half)], sib_sems.at[which, index // (slots // 2)]
            ).wait()

    def chain(index, which, base, first, last, into, acc, recv_sems, send_sem, target, back_target, back_sems):
        rows = slot_rows(0, index)
        own = slot_rows(base, index)

        @pl.when((index >= 0) & (index < slots))
        def _():
            own_term(which, base, index)

            def term():
                return partial_ref[own].astype(jnp.float32) + sib[which, rows].astype(jnp.float32)

            def pass_on(total):
                acc[rows] = total.astype(jnp.bfloat16)
                send(acc.at[rows], into.at[rows], send_sem, recv_sems.at[index], target).start()

            @pl.when(first)
            def _():
                pass_on(term())

            @pl.when(jnp.logical_not(first))
            def _():
                pltpu.make_async_copy(into.at[rows], into.at[rows], recv_sems.at[index]).wait()

            @pl.when(middle)
            def _():
                pass_on(term() + into[rows].astype(jnp.float32))

            @pl.when(last)
            def _():
                total = term() + into[rows].astype(jnp.float32)
                value = settle(total, rows, settle_in, settle_out)
                if with_gather:
                    stage[rows] = value
                    whole_ref[own] = value
                    send(stage.at[rows], whole_ref.at[own], send_sems.at[3], back_sems.at[index], back_target).start()
                    send(stage.at[rows], whole_ref.at[own], send_sems.at[5], whole_sems.at[which], sibling).start()

    def back(index, which, base, reached, more, back_sems, target):
        own = slot_rows(base, index)

        @pl.when((index >= 0) & (index < slots) & reached)
        def _():
            pltpu.make_async_copy(whole_ref.at[own], whole_ref.at[own], back_sems.at[index]).wait()

            @pl.when(more)
            def _():
                send(whole_ref.at[own], whole_ref.at[own], send_sems.at[4], back_sems.at[index], target).start()

            send(whole_ref.at[own], whole_ref.at[own], send_sems.at[5], whole_sems.at[which], sibling).start()

    def step(j, carry):
        chain(j - SKEW * c, 1, up_base, c == 0, c == 3, in_up, acc_up, up_sems, send_sems.at[1], above, below, back_down)
        chain(j - SKEW * (3 - c), 0, down_base, c == 3, c == 0, in_down, acc_down, down_sems, send_sems.at[2], below, above, back_up)
        if with_gather:
            back(j - SKEW * (6 - c), 1, up_base, high, low, back_down, below)
            back(j - SKEW * (3 + c), 0, down_base, low, high, back_up, above)
        return carry

    lax.fori_loop(0, slots + SKEW * (6 if with_gather else 3), step, 0)

    def drain(ref, sem):
        pltpu.make_async_copy(ref, ref, sem).wait()

    drain(sib, send_sems.at[0])

    @pl.when(high)
    def _():
        drain(acc_up, send_sems.at[1])

    @pl.when(low)
    def _():
        drain(acc_down, send_sems.at[2])

    if with_gather:
        up_rows = pl.ds(pl.multiple_of(up_base, block), block)
        down_rows = pl.ds(pl.multiple_of(down_base, block), block)
        other_up = pl.ds(pl.multiple_of((3 - t) * block, block), block)
        other_down = pl.ds(pl.multiple_of((1 - t) * block, block), block)

        @pl.when(jnp.logical_not(middle))
        def _():
            drain(stage, send_sems.at[3])

        @pl.when(middle)
        def _():
            drain(whole_ref.at[up_rows], send_sems.at[4])
            drain(whole_ref.at[down_rows], send_sems.at[4])

        drain(whole_ref.at[up_rows], send_sems.at[5])
        drain(whole_ref.at[down_rows], send_sems.at[5])
        drain(whole_ref.at[other_up], whole_sems.at[1])
        drain(whole_ref.at[other_down], whole_sems.at[0])

    for job in jobs:
        job.finish()


def line_call(name, number, settle, partial_sum, settle_in, settle_out, with_gather, jobs):
    rows, width = partial_sum.shape
    block = rows // 4
    outs = list(settle_out)
    if with_gather:
        outs.append(jax.ShapeDtypeStruct((rows, width), jnp.bfloat16))
    vmem = pl.BlockSpec(memory_space=pltpu.VMEM)
    hbm = pl.BlockSpec(memory_space=pl.ANY)
    kinds = [kind for kind, _ in jobs]
    piece = pltpu.VMEM((block, width), jnp.bfloat16)
    dma = pltpu.SemaphoreType.DMA
    slots = block // SLOT
    return pl.pallas_call(
        functools.partial(line_kernel, settle, with_gather, len(settle_in), len(settle_out), kinds),
        name=name,
        out_shape=tuple(outs) + tuple(kind.result(source) for kind, source in jobs),
        in_specs=[vmem] * (1 + len(settle_in)) + [hbm] * len(jobs),
        out_specs=tuple([vmem] * len(outs) + [hbm] * len(jobs)),
        scratch_shapes=[
            piece,
            piece,
            piece,
            piece,
            pltpu.VMEM((2, block, width), jnp.bfloat16),
            piece,
            dma((6,)),
            dma((2, 2)),
            dma((slots,)),
            dma((slots,)),
            dma((slots,)),
            dma((slots,)),
            dma((2,)),
        ]
        + [dma((kind.semaphores,)) for kind in kinds],
        compiler_params=pltpu.CompilerParams(
            collective_id=number, has_side_effects=True, vmem_limit_bytes=40 * 2**20
        ),
        cost_estimate=pl.CostEstimate(flops=10**9, bytes_accessed=100 * 10**6, transcendentals=0),
    )(partial_sum, *settle_in, *[source for _, source in jobs])


def settle_forward(total, rows, ins, outs):
    residual_ref, gain_ref = ins
    value = residual_ref[rows] + depth_scale * total
    outs[0][rows] = value
    inverse = lax.rsqrt(jnp.mean(value * value, axis=-1, keepdims=True) + eps_norm)
    return (value * inverse * gain_ref[...]).astype(jnp.bfloat16)


def settle_last(total, rows, ins, outs):
    outs[0][rows] = ins[0][rows] + depth_scale * total
    return None


def settle_backward(total, rows, ins, outs):
    values_ref, grad_ref, gain_ref = ins
    grad_out, gain_grad = outs
    value = values_ref[rows]
    inverse = lax.rsqrt(jnp.mean(value * value, axis=-1, keepdims=True) + eps_norm)
    scaled = value * inverse
    contribution = jnp.sum(total * scaled, axis=0, keepdims=True)

    first = rows.start == 0

    @pl.when(first)
    def _():
        gain_grad[...] = contribution

    @pl.when(jnp.logical_not(first))
    def _():
        gain_grad[...] += contribution

    grad_scaled = total * gain_ref[...]
    grad = grad_ref[rows] + inverse * (
        grad_scaled - scaled * jnp.mean(grad_scaled * scaled, axis=-1, keepdims=True)
    )
    grad_out[rows] = grad
    return (depth_scale * grad).astype(jnp.bfloat16)


class LineComm:
    def __init__(self):
        self.number = 0

    def next_number(self):
        self.number += 1
        return self.number

    def moves(self, *jobs):
        return jobs_call(self.next_number(), jobs)

    def own_rows(self, whole):
        block = whole.shape[0] // 4
        _, c, t = place()
        return lax.dynamic_slice_in_dim(whole, (jnp.where(c >= 2, 2, 0) + t) * block, block, 0)

    def forward(self, partial_sum, residual, gain, jobs):
        value, normed, *moved = line_call(
            "forward_line",
            self.next_number(),
            settle_forward,
            partial_sum,
            [residual, gain],
            [jax.ShapeDtypeStruct(residual.shape, jnp.float32)],
            True,
            jobs,
        )
        return value, normed, moved

    def last(self, partial_sum, residual, jobs):
        value, *moved = line_call(
            "last_line",
            self.next_number(),
            settle_last,
            partial_sum,
            [residual],
            [jax.ShapeDtypeStruct(residual.shape, jnp.float32)],
            False,
            jobs,
        )
        return value, moved

    def backward(self, partial_sum, values, grad_rows, gain, with_gather, jobs):
        outs = line_call(
            "backward_line",
            self.next_number(),
            settle_backward,
            partial_sum,
            [values, grad_rows, gain],
            [jax.ShapeDtypeStruct(values.shape, jnp.float32), jax.ShapeDtypeStruct(gain.shape, jnp.float32)],
            with_gather,
            jobs,
        )
        grad, gain_grad = outs[:2]
        return grad, gain_grad, outs[2] if with_gather else None, outs[3 if with_gather else 2 :]

    def deliver(self, rows):
        block = rows.shape[0]
        _, c, t = place()
        moved = lax.ppermute(rows, "ctx", [(0, 1), (3, 2)])
        mine = jnp.where((c == 0) | (c == 3), rows, moved)
        pair = lax.all_gather(mine, "tensor", axis=0, tiled=False)
        pick = jnp.where((c == 0) | (c == 2), 0, 1)
        return lax.dynamic_index_in_dim(pair, pick, 0, keepdims=False)


class PlainComm:
    def moves(self, *jobs):
        return tuple(
            lax.all_to_all(source, "ctx", 0, 0, tiled=False)
            if kind is Exchange
            else lax.all_gather(source, "ctx", axis=0, tiled=True)
            for kind, source in jobs
        )

    def own_rows(self, whole):
        _, c, t = place()
        share = whole.shape[0] // (lax.axis_size("ctx") * lax.axis_size("tensor"))
        return lax.dynamic_slice_in_dim(whole, (c * lax.axis_size("tensor") + t) * share, share, 0)

    def forward(self, partial_sum, residual, gain, jobs):
        value = residual + depth_scale * scatter_rows(partial_sum)
        return value, gather_rows((rms_parts(value)[0] * gain).astype(jnp.bfloat16)), self.moves(*jobs)

    def last(self, partial_sum, residual, jobs):
        return residual + depth_scale * scatter_rows(partial_sum), self.moves(*jobs)

    def backward(self, partial_sum, values, grad_rows, gain, with_gather, jobs):
        gain_grad, from_norm = norm_backward(values, gain, scatter_rows(partial_sum))
        grad = grad_rows + from_norm
        gathered = gather_rows((depth_scale * grad).astype(jnp.bfloat16)) if with_gather else None
        return grad, gain_grad, gathered, self.moves(*jobs)

    def deliver(self, rows):
        return lax.all_gather(rows, "tensor", axis=0, tiled=True)


def outer_kernel(*refs):
    out_ref, first = refs[-1], 0
    for left, right in zip(refs[:-1:2], refs[1:-1:2]):
        last = first + right.shape[1]
        out_ref[:, first:last] = outer_rows(left[...], right[...]).astype(out_ref.dtype)
        first = last


def outer_sums(*pairs):
    rows, width = pairs[0][0].shape
    columns = sum(right.shape[1] for _, right in pairs)
    tile = 256
    specs, operands = [], []
    for left, right in pairs:
        specs += [
            pl.BlockSpec((rows, tile), lambda i: (0, i)),
            pl.BlockSpec(right.shape, lambda i: (0, 0)),
        ]
        operands += [left, right]
    return pl.pallas_call(
        outer_kernel,
        name="outer_sums",
        grid=(width // tile,),
        out_shape=jax.ShapeDtypeStruct((width, columns), jnp.bfloat16),
        in_specs=specs,
        out_specs=pl.BlockSpec((tile, columns), lambda i: (i, 0)),
        compiler_params=pltpu.CompilerParams(vmem_limit_bytes=40 * 2**20),
        cost_estimate=pl.CostEstimate(
            flops=2 * rows * width * columns, bytes_accessed=2 * (rows + width) * columns, transcendentals=0
        ),
    )(*operands)


def attention_forward(query, key, value, bias):
    scores = jnp.einsum("qhd,khd->hqk", query, key, preferred_element_type=jnp.float32) * score_scale
    scores = scores + bias[None]
    top = jnp.max(scores, axis=-1, keepdims=True)
    terms = jnp.exp(scores - top)
    probs = terms / jnp.sum(terms, axis=-1, keepdims=True)
    attended = jnp.einsum(
        "hqk,khd->qhd", probs.astype(jnp.bfloat16), value, preferred_element_type=jnp.float32
    )
    return attended, probs


def attention_backward(query, key, value, probs, grad_out):
    grad_probs = jnp.einsum("qhd,khd->hqk", grad_out, value, preferred_element_type=jnp.float32)
    delta = jnp.sum(probs * grad_probs, axis=-1, keepdims=True)
    grad_scores = (probs * (grad_probs - delta) * score_scale).astype(jnp.bfloat16)
    grad_query = jnp.einsum("hqk,khd->qhd", grad_scores, key, preferred_element_type=jnp.float32)
    grad_key = jnp.einsum("hqk,qhd->khd", grad_scores, query, preferred_element_type=jnp.float32)
    grad_value = jnp.einsum(
        "hqk,qhd->khd", probs.astype(jnp.bfloat16), grad_out, preferred_element_type=jnp.float32
    )
    return grad_query, grad_key, grad_value


def forward_attention(normed, weight, plan, bias, tables):
    width = plan.head_width
    rows = normed.shape[0]
    head_shape = (rows, plan.head_count, HEAD_DIM)
    mixed = times(normed, weight[:, : 3 * width])
    query = rotate(mixed[:, :width].reshape(head_shape), tables, 1.0).astype(jnp.bfloat16)
    key = rotate(mixed[:, width : 2 * width].reshape(head_shape), tables, 1.0).astype(jnp.bfloat16)
    value = mixed[:, 2 * width :].reshape(head_shape).astype(jnp.bfloat16)
    attended, probs = attention_forward(query, key, value, bias)
    attended = attended.reshape(rows, width).astype(jnp.bfloat16)
    partial_sum = times_transposed(attended, weight[:, 3 * width :]).astype(jnp.bfloat16)
    return partial_sum, (normed, query, key, value, probs, attended)


def forward_feed(normed, weight, plan):
    units = plan.unit_width
    both = times(normed, weight[:, : 2 * units])
    gating, upward = both[:, :units], both[:, units:]
    activated = (jax.nn.silu(gating) * upward).astype(jnp.bfloat16)
    partial_sum = times_transposed(activated, weight[:, 2 * units :]).astype(jnp.bfloat16)
    return partial_sum, (normed, gating, upward, activated)


def backward_feed(down_grad, weight, record, plan):
    normed, gating, upward, activated = record
    units = plan.unit_width
    grad_act = times(down_grad, weight[:, 2 * units :])
    sigmoid_gate = jax.nn.sigmoid(gating)
    grad_gating = grad_act * upward * sigmoid_gate * (1.0 + gating * (1.0 - sigmoid_gate))
    grad_upward = grad_act * gating * sigmoid_gate
    grad_both = jnp.concatenate([grad_gating, grad_upward], axis=1).astype(jnp.bfloat16)
    partial_sum = times_transposed(grad_both, weight[:, : 2 * units]).astype(jnp.bfloat16)
    return partial_sum, ((normed, grad_both), (down_grad, activated))


def backward_attention(branch_grad, weight, record, plan, tables):
    normed, query, key, value, probs, attended = record
    width = plan.head_width
    rows = normed.shape[0]
    grad_mixed = times(branch_grad, weight[:, 3 * width :]).astype(jnp.bfloat16)
    grad_query, grad_key, grad_value = attention_backward(
        query, key, value, probs, grad_mixed.reshape(query.shape)
    )
    grad_all = jnp.concatenate(
        [
            rotate(grad_query, tables, -1.0).reshape(rows, width),
            rotate(grad_key, tables, -1.0).reshape(rows, width),
            grad_value.reshape(rows, width),
        ],
        axis=1,
    ).astype(jnp.bfloat16)
    partial_sum = times_transposed(grad_all, weight[:, : 3 * width]).astype(jnp.bfloat16)
    return partial_sum, ((normed, grad_all), (branch_grad, attended))


def body(
    inputs,
    cotangent,
    lengths,
    dealing,
    span_table,
    prenorm_gain,
    query_weight,
    keys_weight,
    values_weight,
    project_weight,
    postnorm_gain,
    gating_weight,
    upward_weight,
    downward_weight,
):
    n_dp, n_ctx, n_ten = lax.axis_size("dp"), lax.axis_size("ctx"), lax.axis_size("tensor")
    plan = Plan(n_dp, n_ctx, query_weight.shape[2], gating_weight.shape[2])
    own_rows = inputs.shape[0]
    half_span = own_rows // 2
    share = own_rows // n_ten
    group_index = lax.axis_index("dp")
    core = lax.axis_index("tensor")
    seq_count = lengths.shape[0] // n_dp
    starts, seq_lens = group_layout(lengths, dealing, group_index, seq_count)
    span_row = lax.dynamic_index_in_dim(span_table, group_index, 0, keepdims=False)
    facts = slot_facts(slots_for(own_rows * n_ctx, span_row, half_span), starts, seq_lens)
    tables = rope_tables(facts[2], HEAD_DIM // 2)
    bias = jnp.where(allowed(facts, facts), 0.0, masked_score)

    gains = lax.all_gather(
        jnp.concatenate([prenorm_gain, postnorm_gain], axis=0), ("dp", "ctx"), axis=1, tiled=True
    ).astype(jnp.float32)
    comm = LineComm() if (n_dp, n_ctx, n_ten) == (4, 4, 2) else PlainComm()
    head_cuts = [cut * HEAD_DIM for cut in plan.head_cuts]

    def attention_windows(layer):
        weights = (query_weight[layer], keys_weight[layer], values_weight[layer], project_weight[layer].T)
        return jnp.concatenate([cut_windows(weight, head_cuts, plan.head_width) for weight in weights], axis=2)

    def feed_windows(layer):
        weights = (gating_weight[layer], upward_weight[layer], downward_weight[layer].T)
        return jnp.concatenate([cut_windows(weight, plan.unit_cuts, plan.unit_width) for weight in weights], axis=2)

    front = [gains[layer : layer + 1] for layer in range(LAYERS)]
    behind = [gains[LAYERS + layer : LAYERS + layer + 1] for layer in range(LAYERS)]
    attention_weights, feed_weights = [None] * LAYERS, [None] * LAYERS
    attention_records, feed_records, middles = [None] * LAYERS, [None] * LAYERS, [None] * LAYERS
    starts_of = [None] * LAYERS

    blocks, inputs_whole = comm.moves((Exchange, attention_windows(0)), (Collect, inputs))
    attention_weights[0] = spread_weights(blocks)
    residual = comm.own_rows(inputs_whole).astype(jnp.float32)
    normed = (rms_parts(inputs_whole.astype(jnp.float32))[0] * front[0]).astype(jnp.bfloat16)
    windows, normed = lax.optimization_barrier((feed_windows(0), normed))
    (blocks,) = comm.moves((Exchange, windows))
    feed_weights[0] = spread_weights(blocks)
    for layer in range(LAYERS):
        starts_of[layer] = residual
        more = layer + 1 < LAYERS
        partial_sum, attention_records[layer] = forward_attention(
            normed, attention_weights[layer], plan, bias, tables
        )
        jobs = [(Exchange, attention_windows(layer + 1))] if more else [(Collect, cotangent)]
        hidden, normed, moved = comm.forward(partial_sum, residual, behind[layer], jobs)
        if more:
            attention_weights[layer + 1] = spread_weights(moved[0])
        else:
            cotangent_whole = moved[0]
        middles[layer] = hidden
        partial_sum, feed_records[layer] = forward_feed(normed, feed_weights[layer], plan)
        if more:
            jobs = [(Exchange, feed_windows(layer + 1))]
            residual, normed, moved = comm.forward(partial_sum, hidden, front[layer + 1], jobs)
            feed_weights[layer + 1] = spread_weights(moved[0])
        else:
            residual, _ = comm.last(partial_sum, hidden, [])
    output = comm.deliver(residual.astype(jnp.bfloat16))

    grad_rows = comm.own_rows(cotangent_whole).astype(jnp.float32)
    down_grad = (depth_scale * cotangent_whole.astype(jnp.float32)).astype(jnp.bfloat16)
    gain_grads, attention_parts, feed_parts = [None] * LAYERS, [None] * LAYERS, [None] * LAYERS
    for layer in reversed(range(LAYERS)):
        more = layer > 0
        partial_sum, pairs = backward_feed(down_grad, feed_weights[layer], feed_records[layer], plan)
        feed_sums = reduce_grads(outer_sums(*pairs), n_ctx)
        jobs = [] if layer + 1 == LAYERS else [(Exchange, feed_parts[layer + 1])]
        grad_rows, gain_back, branch_grad, moved = comm.backward(
            partial_sum, middles[layer], grad_rows, behind[layer], True, jobs
        )
        if moved:
            feed_parts[layer + 1] = moved[0]
        feed_parts[layer] = feed_sums
        partial_sum, pairs = backward_attention(
            branch_grad, attention_weights[layer], attention_records[layer], plan, tables
        )
        attention_sums = reduce_grads(outer_sums(*pairs), n_ctx)
        jobs = [] if layer + 1 == LAYERS else [(Exchange, attention_parts[layer + 1])]
        grad_rows, gain_front, down_grad, moved = comm.backward(
            partial_sum, starts_of[layer], grad_rows, front[layer], more, jobs
        )
        if moved:
            attention_parts[layer + 1] = moved[0]
        attention_parts[layer] = attention_sums
        gain_grads[layer] = (gain_front, gain_back)
    (feed_parts[0],) = comm.moves((Exchange, feed_parts[0]))
    (attention_parts[0],) = comm.moves((Exchange, attention_parts[0]))
    grad_inputs = comm.deliver(grad_rows.astype(jnp.bfloat16)).astype(jnp.float32)
    gain_sums = jnp.concatenate([pair[which] for which in range(2) for pair in gain_grads], axis=0)
    gain_sums = lax.psum_scatter(
        lax.psum(gain_sums, "tensor"), ("dp", "ctx"), scatter_dimension=1, tiled=True
    )

    def spread(parts, index, width, cuts, flip):
        out = []
        for part in parts:
            whole = join_windows(part[:, :, index * width : (index + 1) * width], cuts)
            out.append((whole.T if flip else whole).astype(jnp.float32))
        return jnp.stack(out)

    attention_out = [
        spread(attention_parts, i, plan.head_width, head_cuts, i == 3) for i in range(4)
    ]
    feed_out = [spread(feed_parts, i, plan.unit_width, plan.unit_cuts, i == 2) for i in range(3)]
    return (
        output,
        grad_inputs,
        gain_sums[:LAYERS],
        *attention_out,
        gain_sums[LAYERS:],
        *feed_out,
    )


def solution(mesh):
    rows = P(("dp", "ctx"), None)
    gain = P(None, ("dp", "ctx"))
    wide = P(None, ("dp", "ctx"), "tensor")
    tall = P(None, "tensor", ("dp", "ctx"))
    weights = (gain, wide, wide, wide, tall, gain, wide, wide, tall)
    return jax.shard_map(
        body,
        mesh=mesh,
        in_specs=(rows, rows, P(), P(), P()) + weights,
        out_specs=(rows, rows) + weights,
        check_vma=False,
    )
```

```python
import math

import functools

import jax
import jax.numpy as jnp
from jax import lax
from jax.experimental import pallas as pl
from jax.experimental.pallas import tpu as pltpu
from jax.sharding import PartitionSpec as P

MESH = pl.DeviceIdType.MESH

HEAD_DIM = 64
LAYERS = 2
BLOCK = 128
LANES = 128

eps_norm = 1e-05
depth_scale = 1.4 / math.sqrt(40.0)
rope_base = 10000.0
masked_score = -1e30
score_scale = 1.0 / math.sqrt(HEAD_DIM)


def times(left, right):
    return jnp.dot(left, right, preferred_element_type=jnp.float32)


def times_transposed(left, right):
    return lax.dot_general(
        left, right, (((1,), (1,)), ((), ())), preferred_element_type=jnp.float32
    )


def outer_rows(left, right):
    return lax.dot_general(
        left, right, (((0,), (0,)), ((), ())), preferred_element_type=jnp.float32
    )


def rms_parts(values):
    inverse = lax.rsqrt(jnp.mean(values * values, axis=-1, keepdims=True) + eps_norm)
    return (values * inverse, inverse)


def norm_backward(values, gain, grad_normed):
    scaled, inverse = rms_parts(values)
    gain_grad = jnp.sum(grad_normed * scaled, axis=0, keepdims=True)
    grad_scaled = grad_normed * gain
    return (
        gain_grad,
        inverse * (grad_scaled - scaled * jnp.mean(grad_scaled * scaled, axis=-1, keepdims=True)),
    )


def rope_tables(position, half_dim):
    inverse = rope_base ** (-jnp.arange(half_dim).astype(jnp.float32) / half_dim)
    angles = position.astype(jnp.float32)[:, None] * inverse[None, :]
    return (jnp.cos(angles)[:, None, :], jnp.sin(angles)[:, None, :])


def rotate(values, tables, direction):
    cosine, sine_table = tables
    half_dim = values.shape[-1] // 2
    front_half = values[..., :half_dim]
    back_half = values[..., half_dim:]
    return jnp.concatenate(
        [
            front_half * cosine - direction * back_half * sine_table,
            back_half * cosine + direction * front_half * sine_table,
        ],
        axis=-1,
    )


def group_layout(lengths, dealing, group_index, seq_count):
    chosen = lax.dynamic_slice_in_dim(dealing, group_index * seq_count, seq_count)
    matches = chosen[:, None] == jnp.arange(lengths.shape[0], dtype=jnp.int32)[None, :]
    seq_lens = jnp.sum(jnp.where(matches, lengths[None, :], 0), axis=1)
    padded = (seq_lens + BLOCK - 1) // BLOCK * BLOCK
    starts = jnp.cumsum(padded) - padded
    return (starts, seq_lens)


def slots_for(number, span_row, half_span):
    rows = jnp.arange(number, dtype=jnp.int32)
    matches = (rows // half_span)[:, None] == jnp.arange(span_row.shape[0], dtype=jnp.int32)[None, :]
    span_of = jnp.sum(jnp.where(matches, span_row[None, :], 0), axis=1)
    return span_of * half_span + rows % half_span


def slot_facts(slots, starts, seq_lens):
    member = jnp.sum((slots[:, None] >= starts[None, :]).astype(jnp.int32), axis=1) - 1
    matches = member[:, None] == jnp.arange(starts.shape[0], dtype=jnp.int32)[None, :]
    anchor = jnp.sum(jnp.where(matches, starts[None, :], 0), axis=1)
    extent = jnp.sum(jnp.where(matches, seq_lens[None, :], 0), axis=1)
    position = slots - anchor
    return (slots, member, position, (position < extent).astype(jnp.int32))


def allowed(query_facts, key_facts):
    query_slot, query_member, query_position, query_valid = query_facts
    key_slot, key_member, key_position, key_valid = key_facts
    same_slot = query_slot[:, None] == key_slot[None, :]
    both_valid = (query_valid[:, None] == 1) & (key_valid[None, :] == 1)
    causal = (query_member[:, None] == key_member[None, :]) & (
        key_position[None, :] <= query_position[:, None]
    )
    return same_slot | both_valid & causal


class Plan:
    def __init__(self, n_dp, n_ctx, columns, hidden):
        self.n_dp, self.n_ctx = n_dp, n_ctx
        heads = columns // HEAD_DIM
        self.head_cuts = [i * heads // n_ctx for i in range(n_ctx + 1)]
        self.head_count = max(b - a for a, b in zip(self.head_cuts, self.head_cuts[1:]))
        self.head_width = self.head_count * HEAD_DIM
        self.unit_cuts = [i * hidden // n_ctx for i in range(n_ctx + 1)]
        units = max(b - a for a, b in zip(self.unit_cuts, self.unit_cuts[1:]))
        self.unit_width = (units + LANES - 1) // LANES * LANES


def cut_windows(weight, cuts, width):
    pieces = []
    for first, last in zip(cuts, cuts[1:]):
        pieces.append(jnp.pad(weight[:, first:last], ((0, 0), (0, width - (last - first)))))
    return jnp.stack(pieces)


def join_windows(windows, cuts):
    return jnp.concatenate(
        [windows[i, :, : last - first] for i, (first, last) in enumerate(zip(cuts, cuts[1:]))], axis=1
    )


def cut_kernel(plan, *refs):
    attention, feed, outs = refs[:4], refs[4:7], refs[7:]
    for i, ref in enumerate(attention):
        for j, (first, last) in enumerate(zip(plan.head_cuts, plan.head_cuts[1:])):
            start, count = i * plan.head_width, (last - first) * HEAD_DIM
            outs[0][j, :, start : start + count] = ref[0, :, first * HEAD_DIM : last * HEAD_DIM]
            if count < plan.head_width:
                outs[0][j, :, start + count : start + plan.head_width] = jnp.zeros(
                    (ref.shape[1], plan.head_width - count), ref.dtype
                )
    for ref, out in zip(feed, outs[1:]):
        for j, (first, last) in enumerate(zip(plan.unit_cuts, plan.unit_cuts[1:])):
            out[j, :, : last - first] = ref[0, :, first:last]
            out[j, :, last - first :] = jnp.zeros((ref.shape[1], plan.unit_width - (last - first)), ref.dtype)


def cut_layer(plan, layer, attention, feed):
    specs = [
        pl.BlockSpec((1,) + weight.shape[1:], lambda i, layer=layer: (layer, 0, 0)) for weight in attention + feed
    ]
    rows = attention[0].shape[1]
    outs = [
        jax.ShapeDtypeStruct((plan.n_ctx, rows, width), jnp.bfloat16)
        for width in [4 * plan.head_width] + [plan.unit_width] * 3
    ]
    return pl.pallas_call(
        functools.partial(cut_kernel, plan),
        name="cut_layer",
        grid=(1,),
        out_shape=tuple(outs),
        in_specs=specs,
        out_specs=tuple(pl.BlockSpec(out.shape, lambda i: (0, 0, 0)) for out in outs),
        compiler_params=pltpu.CompilerParams(vmem_limit_bytes=40 * 2**20),
        cost_estimate=pl.CostEstimate(flops=0, bytes_accessed=8 * 10**6, transcendentals=0),
    )(*attention, *feed)


def join_kernel(plan, places, count, *refs):
    sources, outs = refs[:count], refs[count:]
    for layer in range(LAYERS):
        for i, out in enumerate(outs):
            cuts = [cut * HEAD_DIM for cut in plan.head_cuts] if i < 4 else plan.unit_cuts
            which, start = places[layer][i]
            for j, (first, last) in enumerate(zip(cuts, cuts[1:])):
                out[layer, :, first:last] = sources[which][j, :, start : start + last - first].astype(jnp.float32)


def join_layers(plan, parts):
    widths = [plan.head_width] * 4 + [plan.unit_width] * 3
    sources, places = [], []
    for arrays in parts:
        spots, queue = [], list(widths)
        for array in arrays:
            start = 0
            while start < array.shape[2]:
                spots.append((len(sources), start))
                start += queue.pop(0)
            sources.append(array)
        places.append(spots)
    rows = sources[0].shape[1]
    outs = [
        jax.ShapeDtypeStruct((LAYERS, rows, width), jnp.float32)
        for width in [plan.head_cuts[-1] * HEAD_DIM] * 4 + [plan.unit_cuts[-1]] * 3
    ]
    return local_call(functools.partial(join_kernel, plan, places, len(sources)), "join_layers", sources, outs, [], 0)


def reduce_grads(full, n_ctx):
    own = lax.psum_scatter(full, "dp", scatter_dimension=0, tiled=True)
    return own.reshape(n_ctx, -1, own.shape[-1])


def gather_rows(piece):
    return lax.all_gather(piece, ("ctx", "tensor"), axis=0, tiled=True)


def scatter_rows(partial_sum):
    return lax.psum_scatter(
        partial_sum.astype(jnp.bfloat16), ("ctx", "tensor"), scatter_dimension=0, tiled=True
    ).astype(jnp.float32)


SLOT = 16
PARTS = 1
SKEW = 3


def place():
    return lax.axis_index("dp"), lax.axis_index("ctx"), lax.axis_index("tensor")


def slot_rows(base, index):
    return pl.ds(pl.multiple_of(base + index * SLOT, SLOT), SLOT)


def send(src, dst, send_sem, recv_sem, target):
    return pltpu.make_async_remote_copy(
        src_ref=src, dst_ref=dst, send_sem=send_sem, recv_sem=recv_sem, device_id=target, device_id_type=MESH
    )


def greet(d, c, t, everyone=False):
    barrier = pltpu.get_barrier_semaphore()
    others = [(d, c, 1 - t), (d, c ^ 1, t), (d, c ^ 2, t), (d, c ^ 3, t), (d ^ 1, c, t), (d ^ 2, c, t)]
    if everyone:
        others = others[:1] + [(d ^ (k // 4), c ^ (k % 4), t) for k in range(1, 16)]
    for other in others:
        pl.semaphore_signal(barrier, inc=1, device_id=other, device_id_type=MESH)
    pl.semaphore_wait(barrier, len(others))


class Job:
    everyone = False
    near = False
    late = False

    @staticmethod
    def scratch(source):
        return []

    def steps(self):
        return []


class Exchange(Job):
    semaphores = 7

    @staticmethod
    def result(source):
        return jax.ShapeDtypeStruct(source.shape, source.dtype)

    def __init__(self, source, result, sems):
        d, c, t = place()
        self.own = pltpu.make_async_copy(source.at[c], result.at[c], sems.at[6])
        self.copies = [
            send(source.at[c ^ k], result.at[c], sems.at[k - 1], sems.at[k + 2], (d, c ^ k, t)) for k in (3, 2, 1)
        ]

    def start(self):
        for copy in self.copies:
            copy.start()
        self.own.start()

    def finish(self):
        for copy in self.copies:
            copy.wait()
        self.own.wait()


class Collect(Job):
    semaphores = 25

    @staticmethod
    def result(source):
        return jax.ShapeDtypeStruct((4 * source.shape[0], source.shape[1]), source.dtype)

    def __init__(self, source, result, sems):
        d, c, t = place()
        block = source.shape[0]
        half = block // 2

        def piece(chip):
            return result.at[pl.ds(pl.multiple_of(chip * block + t * half, half), half)]

        self.own = pltpu.make_async_copy(source, result.at[pl.ds(pl.multiple_of(c * block, block), block)], sems.at[24])
        mine = source.at[pl.ds(pl.multiple_of(t * half, half), half)]
        self.hops, self.onward = {}, {}
        for way, more, target in ((0, c < 3, (d, c + 1, t)), (1, c > 0, (d, c - 1, t))):
            for hop in range(4):
                chip = c - hop if way == 0 else c + hop
                held = (chip >= 0) if way == 0 else (chip <= 3)
                if hop < 3:
                    self.hops[way, hop] = (
                        more & held,
                        send(
                            piece(chip) if hop else mine,
                            piece(chip),
                            sems.at[way * 12 + hop],
                            sems.at[way * 12 + 3 + hop],
                            target,
                        ),
                    )
                if hop:
                    self.onward[way, hop] = (
                        held,
                        send(
                            piece(chip),
                            piece(chip),
                            sems.at[way * 12 + 5 + hop],
                            sems.at[way * 12 + 8 + hop],
                            (d, c, 1 - t),
                        ),
                    )

    def start(self):
        for way in range(2):
            go, copy = self.hops[way, 0]
            pl.when(go)(copy.start)
        self.own.start()

    def steps(self):
        return [functools.partial(self.pass_on, hop) for hop in range(1, 4)]

    def pass_on(self, hop):
        for way in range(2):
            held, onward = self.onward[way, hop]
            arrived = self.hops[way, hop - 1][1]

            @pl.when(held)
            def _():
                arrived.wait_recv()
                onward.start()

            if hop < 3:
                go, copy = self.hops[way, hop]
                pl.when(go)(copy.start)

    def finish(self):
        for go, copy in self.hops.values():
            pl.when(go)(copy.wait_send)
        for held, onward in self.onward.values():
            pl.when(held)(onward.wait)
        self.own.wait()


class GainScatter(Job):
    semaphores = 31
    everyone = True
    near = True
    late = True

    @staticmethod
    def blocks(source):
        return (16, 8, (source.shape[1] // 16 + LANES - 1) // LANES * LANES)

    @staticmethod
    def result(source):
        return jax.ShapeDtypeStruct(GainScatter.blocks(source), source.dtype)

    @staticmethod
    def scratch(source):
        return [pltpu.VMEM(GainScatter.blocks(source), source.dtype)]

    def __init__(self, source, result, sems, cut):
        d, c, t = place()
        mine = d * 4 + c
        self.source, self.cut = source, cut
        self.own = pltpu.make_async_copy(cut.at[mine], result.at[mine], sems.at[0])
        self.copies = []
        for k in range(1, 16):
            g, i = d ^ (k // 4), c ^ (k % 4)
            self.copies.append(send(cut.at[g * 4 + i], result.at[mine], sems.at[k], sems.at[k + 15], (g, i, t)))

    def start(self, made):
        self.cut[...] = jnp.zeros(self.cut.shape, self.cut.dtype)
        part = made.shape[1] // 16
        for i in range(16):
            self.cut[i, 0:1, :part] = made[:, i * part : (i + 1) * part]
            rows = self.source.shape[0]
            self.cut[i, 1 : 1 + rows, :part] = self.source[:, i * part : (i + 1) * part]
        for copy in self.copies:
            copy.start()
        self.own.start()

    def finish(self):
        for copy in self.copies:
            copy.wait()
        self.own.wait()


class Return(Job):
    semaphores = 31
    near = True
    order = (0, 2, 1, 3)

    @staticmethod
    def result(source):
        return jax.ShapeDtypeStruct((4,) + source.shape[1:], source.dtype)

    @staticmethod
    def scratch(source):
        four = pltpu.VMEM((4,) + source.shape[1:], source.dtype)
        return [four] * 5

    def __init__(self, source, result, sems, corner_in, x_in, y_in, passed, total):
        d, c, t = place()
        self.corner_in, self.sides_in, self.passed, self.total = corner_in, (x_in, y_in), passed, total
        self.terms, self.corners, self.sides, self.line = [], [], [], [None]
        for k in range(4):
            i = c ^ k
            way = k // 2
            self.terms.append([source.at[(d ^ flip) * 4 + i] for flip in (0, 1, 2)])
            self.corners.append(
                send(source.at[(d ^ 3) * 4 + i], corner_in.at[k], sems.at[k], sems.at[4 + k], (d ^ (1 + way), c, t))
            )
            self.sides.append(
                [
                    send(
                        passed.at[k] if side != way else source.at[(d ^ (1 + side)) * 4 + i],
                        self.sides_in[side].at[k],
                        sems.at[8 + 2 * k + side],
                        sems.at[16 + 2 * k + side],
                        (d ^ (1 + side), c, t),
                    )
                    for side in range(2)
                ]
            )
            if k:
                self.line.append(send(total.at[k], result.at[c], sems.at[23 + k], sems.at[26 + k], (d, i, t)))
        self.own = pltpu.make_async_copy(total.at[0], result.at[c], sems.at[30])

    def start(self):
        for k in self.order:
            self.corners[k].start()
        for k in self.order:
            self.sides[k][k // 2].start()

    def steps(self):
        return [functools.partial(self.pass_term, k) for k in self.order] + [
            functools.partial(self.add_up, k) for k in (3, 2, 1, 0)
        ]

    def pass_term(self, k):
        side = 1 - k // 2
        self.corners[k].wait_recv()
        self.passed[k] = (self.terms[k][1 + side][...].astype(jnp.float32) + self.corner_in[k].astype(jnp.float32)).astype(
            self.passed.dtype
        )
        self.sides[k][side].start()

    def add_up(self, k):
        for side in range(2):
            self.sides[k][side].wait_recv()
        self.total[k] = (
            self.terms[k][0][...].astype(jnp.float32)
            + self.sides_in[0][k].astype(jnp.float32)
            + self.sides_in[1][k].astype(jnp.float32)
        ).astype(self.total.dtype)
        if k:
            self.line[k].start()
        else:
            self.own.start()

    def finish(self):
        for k in range(4):
            self.corners[k].wait_send()
            for copy in self.sides[k]:
                copy.wait_send()
            if k:
                self.line[k].wait()
        self.own.wait()


class Fetch(Job):
    semaphores = 31

    @staticmethod
    def result(source):
        return jax.ShapeDtypeStruct((16,) + source.shape[1:], source.dtype)

    order = (0, 2, 1, 3)

    def __init__(self, source, result, sems):
        d, c, t = place()
        self.own = pltpu.make_async_copy(source.at[c], result.at[d * 4 + c], sems.at[0])
        self.line = [None]
        for k in range(1, 4):
            self.line.append(
                send(source.at[c ^ k], result.at[d * 4 + c], sems.at[k], sems.at[k + 3], (d, c ^ k, t))
            )
        self.link(source, result, sems)

    def link(self, source, result, sems):
        d, c, t = place()
        self.side, self.corners = [], []
        for k in range(4):
            held = result.at[d * 4 + (c ^ k)]
            ready = held if self.line[k] is not None else source.at[c ^ k]
            self.side.append(
                [
                    send(ready, held, sems.at[7 + 2 * k + way], sems.at[15 + 2 * k + way], (d ^ (1 + way), c, t))
                    for way in range(2)
                ]
            )
            way = k // 2
            passed = result.at[(d ^ (1 + way)) * 4 + (c ^ k)]
            self.corners.append(
                send(passed, passed, sems.at[23 + k], sems.at[27 + k], (d ^ (2 - way), c, t))
            )

    def start(self):
        self.own.start()
        for k in (3, 2, 1):
            self.line[k].start()
        for copy in self.side[0]:
            copy.start()

    def steps(self):
        return [functools.partial(self.pass_sides, k) for k in (1, 2, 3)] + self.corner_steps()

    def corner_steps(self):
        return [functools.partial(self.pass_corner, k) for k in self.order]

    def pass_sides(self, k):
        self.line[k].wait_recv()
        for copy in self.side[k]:
            copy.start()

    def pass_corner(self, k):
        self.side[k][k // 2].wait_recv()
        self.corners[k].start()

    def finish(self):
        for k in range(4):
            self.side[k][1 - k // 2].wait_recv()
        for k in range(4):
            self.corners[k].wait()
            for copy in self.side[k]:
                copy.wait_send()
            if self.line[k] is not None:
                self.line[k].wait_send()
        self.own.wait()


class Spread(Fetch):
    @staticmethod
    def result(source):
        return jax.ShapeDtypeStruct((16,) + source.shape[1:], source.dtype)

    def __init__(self, source, result, sems):
        d, c, t = place()
        self.own = pltpu.make_async_copy(source, result.at[pl.ds(d * 4, 4)], sems.at[0])
        self.line = [None] * 4
        self.link(source, result, sems)

    def start(self):
        for k in self.order:
            for copy in self.side[k]:
                copy.start()
        self.own.start()

    def steps(self):
        return self.corner_steps()


def take(refs, count):
    return refs[:count], refs[count:]


def make_jobs(kinds, scratch_counts, sources, results, refs):
    jobs = []
    for kind, count, source, result in zip(kinds, scratch_counts, sources, results):
        (sems, *scratch), refs = take(refs, 1 + count)
        jobs.append(kind(source, result, sems, *scratch))
    return jobs


def job_specs(jobs):
    vmem, hbm = pl.BlockSpec(memory_space=pltpu.VMEM), pl.BlockSpec(memory_space=pl.ANY)
    sources = [job[1] for job in jobs]
    in_specs = [vmem if job[0].near else hbm for job in jobs]
    out_shapes = [job[0].result(job[1]) for job in jobs]
    scratch, counts = [], []
    for kind, source, *_ in jobs:
        extra = kind.scratch(source)
        scratch += [pltpu.SemaphoreType.DMA((kind.semaphores,))] + extra
        counts.append(len(extra))
    return sources, in_specs, out_shapes, [hbm] * len(jobs), scratch, counts


def jobs_kernel(kinds, counts, urgent, *refs):
    n = len(kinds)
    greet(*place(), any(kind.everyone for kind in kinds))
    jobs = make_jobs(kinds, counts, refs[:n], refs[n : 2 * n], refs[2 * n :])
    first, later = jobs[:urgent], jobs[urgent:]
    for job in first:
        job.start()
    rest = []
    for job in first:
        todo = job.steps()
        for act in todo[:3]:
            act()
        rest += todo[3:]
    for job in later:
        job.start()
    for act in rest:
        act()
    for job in later:
        for act in job.steps():
            act()
    for job in jobs:
        job.finish()


def jobs_call(number, jobs, urgent):
    sources, in_specs, out_shapes, out_specs, scratch, counts = job_specs(jobs)
    return pl.pallas_call(
        functools.partial(jobs_kernel, [job[0] for job in jobs], counts, urgent),
        name="moves",
        out_shape=tuple(out_shapes),
        in_specs=in_specs,
        out_specs=tuple(out_specs),
        scratch_shapes=scratch,
        compiler_params=pltpu.CompilerParams(
            collective_id=number, has_side_effects=True, vmem_limit_bytes=48 * 2**20
        ),
        cost_estimate=pl.CostEstimate(flops=10**9, bytes_accessed=100 * 10**6, transcendentals=0),
    )(*sources)


def drain(ref, sem):
    pltpu.make_async_copy(ref, ref, sem).wait()


class Line:
    scratch_count = 14

    @staticmethod
    def scratch(block, width):
        pieces = block // SLOT * PARTS
        piece = pltpu.VMEM((block, width), jnp.bfloat16)
        dma = pltpu.SemaphoreType.DMA
        return (
            [piece] * 4
            + [pltpu.VMEM((2, block, width), jnp.bfloat16), piece, dma((6,)), dma((2, 2))]
            + [dma((pieces,))] * 4
            + [dma((2,)), pltpu.VMEM((SLOT, width), jnp.float32)]
        )

    def __init__(self, settle, gather, partial_ref, settle_in, settle_out, whole_ref, scratch):
        self.settle, self.gather = settle, gather
        self.partial_ref, self.settle_in, self.settle_out, self.whole_ref = partial_ref, settle_in, settle_out, whole_ref
        (
            self.acc_up,
            self.acc_down,
            self.in_up,
            self.in_down,
            self.sib,
            self.stage,
            self.send_sems,
            self.sib_sems,
            self.up_sems,
            self.down_sems,
            self.back_up,
            self.back_down,
            self.whole_sems,
            self.sum_ref,
        ) = scratch
        d, c, t = place()
        self.block = self.acc_up.shape[0]
        self.pieces = self.block // SLOT * PARTS
        self.columns = self.acc_up.shape[1] // PARTS
        self.turns = self.pieces + SKEW * (6 if gather else 3)
        self.sibling, self.above, self.below = (d, c, 1 - t), (d, c + 1, t), (d, c - 1, t)
        self.down_base, self.up_base = t * self.block, (2 + t) * self.block
        self.low, self.high = c > 0, c < 3
        self.middle = self.low & self.high

    def begin(self):
        _, _, t = place()
        half = self.block // 2
        for part in range(2):
            for which, base in ((0, (1 - t) * self.block), (1, (3 - t) * self.block)):
                rows = pl.ds(pl.multiple_of(base + part * half, half), half)
                send(
                    self.partial_ref.at[rows],
                    self.sib.at[which, pl.ds(part * half, half)],
                    self.send_sems.at[0],
                    self.sib_sems.at[which, part],
                    self.sibling,
                ).start()

        @pl.when(self.middle)
        def _():
            for ref in self.settle_out:
                ref[...] = jnp.zeros(ref.shape, ref.dtype)

    def piece(self, base, index, part):
        return (slot_rows(base, index // PARTS), pl.ds(part * self.columns, self.columns))

    def chain(self, index, which, base, first, last, into, acc, recv_sems, send_sem, target, back_target, back_sems):
        half = self.block // 2
        pieces = self.pieces

        @pl.when((index >= 0) & (index < pieces) & (index % (pieces // 2) == 0))
        def _():
            drain(self.sib.at[which, pl.ds(0, half)], self.sib_sems.at[which, index // (pieces // 2)])

        for part in range(PARTS):
            here = self.piece(0, index, part)
            own = self.piece(base, index, part)

            @pl.when((index >= 0) & (index < pieces) & (index % PARTS == part))
            def _():
                def term():
                    return self.partial_ref[own].astype(jnp.float32) + self.sib[(which, *here)].astype(jnp.float32)

                def pass_on(total):
                    acc[here] = total.astype(jnp.bfloat16)
                    send(acc.at[here], into.at[here], send_sem, recv_sems.at[index], target).start()

                @pl.when(first)
                def _():
                    pass_on(term())

                @pl.when(jnp.logical_not(first))
                def _():
                    drain(into.at[here], recv_sems.at[index])

                @pl.when(self.middle)
                def _():
                    pass_on(term() + into[here].astype(jnp.float32))

                @pl.when(last)
                def _():
                    self.sum_ref[:, here[1]] = term() + into[here].astype(jnp.float32)
                    if part == PARTS - 1:
                        self.settled(index, which, here[0], own[0], back_target, back_sems)

    def settled(self, index, which, rows, own_rows, back_target, back_sems):
        value = self.settle(self.sum_ref[...], rows, self.settle_in, self.settle_out)
        self.stage[rows] = value
        if self.gather:
            whole, sems = self.whole_ref, self.send_sems
            whole[own_rows] = value
            for part in range(PARTS):
                columns = pl.ds(part * self.columns, self.columns)
                send(
                    self.stage.at[rows, columns],
                    whole.at[own_rows, columns],
                    sems.at[3],
                    back_sems.at[index - (PARTS - 1) + part],
                    back_target,
                ).start()
            send(self.stage.at[rows], whole.at[own_rows], sems.at[5], self.whole_sems.at[which], self.sibling).start()

    def back(self, index, which, base, reached, more, back_sems, target):
        for part in range(PARTS):
            own = self.piece(base, index, part)
            held = self.whole_ref.at[own]

            @pl.when((index >= 0) & (index < self.pieces) & reached & (index % PARTS == part))
            def _():
                drain(held, back_sems.at[index])

                @pl.when(more)
                def _():
                    send(held, held, self.send_sems.at[4], back_sems.at[index], target).start()

                if part == PARTS - 1:
                    rows = self.whole_ref.at[own[0]]
                    send(rows, rows, self.send_sems.at[5], self.whole_sems.at[which], self.sibling).start()

    def step(self, j):
        _, c, _ = place()
        sems = self.send_sems
        self.chain(
            j - SKEW * c, 1, self.up_base, c == 0, c == 3, self.in_up, self.acc_up, self.up_sems, sems.at[1],
            self.above, self.below, self.back_down,
        )
        self.chain(
            j - SKEW * (3 - c), 0, self.down_base, c == 3, c == 0, self.in_down, self.acc_down, self.down_sems,
            sems.at[2], self.below, self.above, self.back_up,
        )
        if self.gather:
            self.back(j - SKEW * (6 - c), 1, self.up_base, self.high, self.low, self.back_down, self.below)
            self.back(j - SKEW * (3 + c), 0, self.down_base, self.low, self.high, self.back_up, self.above)

    def end(self):
        d, c, t = place()
        sems, whole, stage = self.send_sems, self.whole_ref, self.stage
        drain(self.sib, sems.at[0])

        @pl.when(self.high)
        def _():
            drain(self.acc_up, sems.at[1])

        @pl.when(self.low)
        def _():
            drain(self.acc_down, sems.at[2])

        if self.gather:
            block = self.block
            up_rows, down_rows, other_up, other_down = [
                pl.ds(pl.multiple_of(base, block), block)
                for base in (self.up_base, self.down_base, (3 - t) * block, (1 - t) * block)
            ]

            @pl.when(jnp.logical_not(self.middle))
            def _():
                drain(stage, sems.at[3])

            @pl.when(self.middle)
            def _():
                drain(whole.at[up_rows], sems.at[4])
                drain(whole.at[down_rows], sems.at[4])

            drain(whole.at[up_rows], sems.at[5])
            drain(whole.at[down_rows], sems.at[5])
            drain(whole.at[other_up], self.whole_sems.at[1])
            drain(whole.at[other_down], self.whole_sems.at[0])
            return
        keeps = ((c == 0) & (t == 0)) | ((c == 3) & (t == 1))
        gives = ((c == 0) & (t == 1)) | ((c == 3) & (t == 0))
        takes = ((c == 1) & (t == 1)) | ((c == 2) & (t == 0))
        inner = (d, jnp.where(c == 0, 1, 2), t)
        away = send(stage, whole, sems.at[3], self.whole_sems.at[0], inner)
        across = send(stage, whole, sems.at[5], self.whole_sems.at[1], self.sibling)
        hand_on = send(whole, whole, sems.at[5], self.whole_sems.at[1], self.sibling)

        @pl.when(keeps)
        def _():
            across.start()
            whole[...] = stage[...]
            across.wait_send()

        @pl.when(gives)
        def _():
            away.start()
            away.wait_send()

        @pl.when(takes)
        def _():
            away.wait_recv()
            hand_on.start()
            hand_on.wait_send()

        @pl.when(jnp.logical_not(keeps | takes))
        def _():
            across.wait_recv()


def line_kernel(prelude, lines, kinds, counts, paces, *refs):
    n_jobs = len(kinds)
    line_in = []
    if prelude:
        prelude_in, refs = take(refs, prelude[1])
    for i, (_, _, n_in, _) in enumerate(lines):
        partial_refs, refs = take(refs, 0 if prelude and i == 0 else 1)
        ins, refs = take(refs, n_in)
        line_in.append((partial_refs, ins))
    job_sources, refs = take(refs, n_jobs)
    if prelude:
        prelude_out, refs = take(refs, prelude[2])
    line_out = []
    for _, _, _, n_out in lines:
        outs, refs = take(refs, n_out)
        (whole_ref,), refs = take(refs, 1)
        line_out.append((outs, whole_ref))
    job_results, refs = take(refs, n_jobs)
    if prelude:
        made, refs = take(refs, 1)
        prelude_scratch, refs = take(refs, prelude[3])
    built = []
    for i, (settle, gather, _, _) in enumerate(lines):
        scratch, refs = take(refs, Line.scratch_count)
        partial_refs, ins = line_in[i]
        outs, whole_ref = line_out[i]
        partial_ref = partial_refs[0] if partial_refs else made[0]
        built.append(Line(settle, gather, partial_ref, ins, outs, whole_ref, scratch))
    greet(*place(), any(kind.everyone for kind in kinds))
    jobs = make_jobs(kinds, counts, job_sources, job_results, refs)
    if not prelude:
        built[0].begin()
    for line in built[1:]:
        line.begin()
    for job in jobs:
        if not job.late:
            job.start()
    if prelude:
        prelude[0](*prelude_in, made[0], *prelude_out, *prelude_scratch)
        built[0].begin()

    turns = max(line.turns for line in built)
    timed, rest = {}, []
    for job, (first_turn, gap) in zip(jobs, paces):
        for i, act in enumerate(job.steps()):
            turn = first_turn + i * gap
            if turn < turns:
                timed.setdefault(turn, []).append(act)
            else:
                rest.append(act)

    def step(j, carry):
        for turn, acts in timed.items():

            @pl.when(j == turn)
            def _():
                for act in acts:
                    act()

        for line in built:
            line.step(j)
        return carry

    lax.fori_loop(0, turns, step, 0)
    for job in jobs:
        if job.late:
            job.start(built[0].settle_out[0])
    for act in rest:
        act()
    for line in built:
        line.end()
    for job in jobs:
        job.finish()


def line_call(name, number, lines, jobs, prelude=None):
    vmem = pl.BlockSpec(memory_space=pltpu.VMEM)
    operands, shapes, scratch, facts = [], [], [], []
    if prelude:
        kernel, prelude_in, prelude_out, prelude_scratch, made = prelude
        operands += prelude_in
        shapes += prelude_out
        scratch += [pltpu.VMEM(made, jnp.bfloat16)] + prelude_scratch
    for settle, gather, partial_sum, settle_in, settle_out in lines:
        rows, width = made if partial_sum is None else partial_sum.shape
        block = rows // 4
        operands += ([] if partial_sum is None else [partial_sum]) + settle_in
        shapes += settle_out + [jax.ShapeDtypeStruct((rows if gather else block, width), jnp.bfloat16)]
        scratch += Line.scratch(block, width)
        facts.append((settle, gather, len(settle_in), len(settle_out)))
    sources, in_specs, out_shapes, out_specs, job_scratch, counts = job_specs(jobs)
    paces = [(tuple(job) + (0, 1))[2:4] for job in jobs]
    return pl.pallas_call(
        functools.partial(
            line_kernel,
            (kernel, len(prelude_in), len(prelude_out), len(prelude_scratch)) if prelude else None,
            facts,
            [job[0] for job in jobs],
            counts,
            paces,
        ),
        name=name,
        out_shape=tuple(shapes + out_shapes),
        in_specs=[vmem] * len(operands) + in_specs,
        out_specs=tuple([vmem] * len(shapes) + out_specs),
        scratch_shapes=scratch + job_scratch,
        compiler_params=pltpu.CompilerParams(
            collective_id=number, has_side_effects=True, vmem_limit_bytes=(58 if any(job[0] is Return for job in jobs) else 40) * 2**20
        ),
        cost_estimate=pl.CostEstimate(flops=10**9, bytes_accessed=100 * 10**6, transcendentals=0),
    )(*operands, *sources)


def settle_forward(total, rows, ins, outs):
    residual_ref, gain_ref = ins
    value = residual_ref[rows] + depth_scale * total
    outs[0][rows] = value
    inverse = lax.rsqrt(jnp.mean(value * value, axis=-1, keepdims=True) + eps_norm)
    return (value * inverse * gain_ref[...]).astype(jnp.bfloat16)


def settle_last(total, rows, ins, outs):
    return (ins[0][rows] + depth_scale * total).astype(jnp.bfloat16)


def settle_backward(total, rows, ins, outs, more=True):
    values_ref, grad_ref, gain_ref = ins
    gain_grad = outs[0]
    value = values_ref[rows]
    inverse = lax.rsqrt(jnp.mean(value * value, axis=-1, keepdims=True) + eps_norm)
    scaled = value * inverse
    contribution = jnp.sum(total * scaled, axis=0, keepdims=True)

    first = rows.start == 0

    @pl.when(first)
    def _():
        gain_grad[...] = contribution

    @pl.when(jnp.logical_not(first))
    def _():
        gain_grad[...] += contribution

    grad_scaled = total * gain_ref[...]
    grad = grad_ref[rows] + inverse * (
        grad_scaled - scaled * jnp.mean(grad_scaled * scaled, axis=-1, keepdims=True)
    )
    if not more:
        return grad.astype(jnp.bfloat16)
    outs[1][rows] = grad
    return (depth_scale * grad).astype(jnp.bfloat16)


class LineComm:
    def __init__(self):
        self.number = 0

    def next_number(self):
        self.number += 1
        return self.number

    def moves(self, *jobs, urgent=0):
        return jobs_call(self.next_number(), jobs, urgent)

    def own_rows(self, whole):
        block = whole.shape[0] // 4
        _, c, t = place()
        return lax.dynamic_slice_in_dim(whole, (jnp.where(c >= 2, 2, 0) + t) * block, block, 0)

    def forward(self, partial_sum, residual, gain, jobs, prelude=None):
        outs = line_call(
            "forward_line",
            self.next_number(),
            [(settle_forward, True, partial_sum, [residual, gain], [jax.ShapeDtypeStruct(residual.shape, jnp.float32)])],
            jobs,
            prelude,
        )
        made, (value, normed, *moved) = take(outs, len(prelude[2]) if prelude else 0)
        return value, normed, moved, made

    def last(self, partial_sum, residual, jobs):
        output, *moved = line_call(
            "last_line", self.next_number(), [(settle_last, False, partial_sum, [residual], [])], jobs
        )
        return output, moved

    def backward(self, partial_sum, values, grad_rows, gain, jobs):
        lines = [
            (
                settle_backward,
                True,
                partial_sum,
                [values, grad_rows, gain],
                [jax.ShapeDtypeStruct(gain.shape, jnp.float32), jax.ShapeDtypeStruct(values.shape, jnp.float32)],
            )
        ]
        gain_grad, grad, gathered, *moved = line_call("backward_line", self.next_number(), lines, jobs)
        return grad, gain_grad, gathered, moved

    def backward_last(self, partial_sum, values, grad_rows, gain, jobs, gain_grads):
        gain_grad, own, *moved, gain_blocks = line_call(
            "backward_last_line",
            self.next_number(),
            [
                (
                    functools.partial(settle_backward, more=False),
                    False,
                    partial_sum,
                    [values, grad_rows, gain],
                    [jax.ShapeDtypeStruct(gain.shape, jnp.float32)],
                )
            ],
            jobs + [(GainScatter, gain_grads)],
        )
        return own, jnp.sum(gain_blocks, axis=0)[: 1 + gain_grads.shape[0], : gain.shape[1] // 16], moved

    def return_grads(self, full):
        return full.reshape(16, -1, full.shape[1])


class PlainComm:
    def moves(self, *jobs, urgent=0):
        moved = []
        for kind, source, *_ in jobs:
            if kind is Collect:
                moved.append(lax.all_gather(source, "ctx", axis=0, tiled=True))
                continue
            if kind is Return:
                source = reduce_grads(source, lax.axis_size("ctx"))
                moved.append(lax.all_to_all(source, "ctx", 0, 0, tiled=False))
                continue
            blocks = source if kind is Spread else lax.all_to_all(source, "ctx", 0, 0, tiled=False)
            moved.append(blocks if kind is Exchange else lax.all_gather(blocks, "dp", axis=0, tiled=True))
        return tuple(moved)

    def own_rows(self, whole):
        _, c, t = place()
        share = whole.shape[0] // (lax.axis_size("ctx") * lax.axis_size("tensor"))
        return lax.dynamic_slice_in_dim(whole, (c * lax.axis_size("tensor") + t) * share, share, 0)

    def forward(self, partial_sum, residual, gain, jobs, prelude=None):
        value = residual + depth_scale * scatter_rows(partial_sum)
        return value, gather_rows((rms_parts(value)[0] * gain).astype(jnp.bfloat16)), self.moves(*jobs), ()

    def deliver(self, rows):
        return lax.all_gather(rows.astype(jnp.bfloat16), "tensor", axis=0, tiled=True)

    def last(self, partial_sum, residual, jobs):
        return self.deliver(residual + depth_scale * scatter_rows(partial_sum)), self.moves(*jobs)

    def backward(self, partial_sum, values, grad_rows, gain, jobs):
        gain_grad, from_norm = norm_backward(values, gain, scatter_rows(partial_sum))
        grad = grad_rows + from_norm
        gathered = gather_rows((depth_scale * grad).astype(jnp.bfloat16))
        return grad, gain_grad, gathered, self.moves(*jobs)

    def backward_last(self, partial_sum, values, grad_rows, gain, jobs, gain_grads):
        gain_grad, from_norm = norm_backward(values, gain, scatter_rows(partial_sum))
        sums = jnp.concatenate([gain_grad, gain_grads], axis=0)
        sums = lax.psum_scatter(sums, ("dp", "ctx"), scatter_dimension=1, tiled=True)
        return self.deliver(grad_rows + from_norm), sums, self.moves(*jobs)

    def return_grads(self, full):
        return full


def swap_halves(values):
    lane = lax.broadcasted_iota(jnp.int32, values.shape, 1)
    half = HEAD_DIM // 2
    width = values.shape[1]
    return jnp.where(lane % HEAD_DIM < half, pltpu.roll(values, width - half, 1), pltpu.roll(values, half, 1))


def head_scores(query, key, bias):
    return times_transposed(query, key) * score_scale + bias


def attend_kernel(heads, normed_ref, weight_ref, cosine_ref, sine_ref, bias_ref, partial_ref, mixed_ref, attended_ref, total_ref, wide):
    width = heads * HEAD_DIM
    lead = wide.shape[1] - width
    cosine, sine = cosine_ref[...], sine_ref[...]
    columns = mixed_ref.shape[1]
    normed = normed_ref[...]
    for first in range(0, columns, 2 * LANES):
        block = times(normed, weight_ref[:, first : first + 2 * LANES])
        for part in range(2):
            start = first + part * LANES
            tile = block[:, part * LANES : (part + 1) * LANES]
            if start < 2 * width:
                tile = tile * cosine + swap_halves(tile) * sine
            mixed_ref[:, start : start + LANES] = tile.astype(jnp.bfloat16)
    wide[:, :lead] = jnp.zeros((wide.shape[0], lead), jnp.bfloat16)
    for head in range(heads):
        low = head * HEAD_DIM
        query = mixed_ref[:, low : low + HEAD_DIM]
        key = mixed_ref[:, width + low : width + low + HEAD_DIM]
        value = mixed_ref[:, 2 * width + low : 2 * width + low + HEAD_DIM]
        scores = head_scores(query, key, bias_ref[...])
        top = jnp.max(scores, axis=-1, keepdims=True)
        terms = jnp.exp(scores - top)
        total = jnp.sum(terms, axis=-1, keepdims=True)
        probs = (terms / total).astype(jnp.bfloat16)
        wide[:, lead + low : lead + low + HEAD_DIM] = times(probs, value).astype(jnp.bfloat16)
        total_ref[:, head : head + 1] = top + jnp.log(total)
    attended_ref[...] = wide[:, lead:]
    attended = wide[...]
    for first in range(0, partial_ref.shape[1], 3 * LANES):
        partial_ref[:, first : first + 3 * LANES] = times_transposed(
            attended, weight_ref[first : first + 3 * LANES, 3 * width - lead :]
        ).astype(jnp.bfloat16)


def attend_back_kernel(heads, grad_ref, weight_ref, mixed_ref, total_ref, cosine_ref, sine_ref, bias_ref, partial_ref, all_ref, wide, turned):
    width = heads * HEAD_DIM
    lead = wide.shape[1] - width
    wide[...] = times(grad_ref[...], weight_ref[:, 3 * width - lead :]).astype(jnp.bfloat16)
    all_ref[:, 3 * width :] = jnp.zeros((all_ref.shape[0], all_ref.shape[1] - 3 * width), jnp.bfloat16)
    for head in range(heads):
        low = head * HEAD_DIM
        query = mixed_ref[:, low : low + HEAD_DIM]
        key = mixed_ref[:, width + low : width + low + HEAD_DIM]
        value = mixed_ref[:, 2 * width + low : 2 * width + low + HEAD_DIM]
        grad_out = wide[:, lead + low : lead + low + HEAD_DIM]
        scores = head_scores(query, key, bias_ref[...])
        probs = jnp.exp(scores - total_ref[:, head : head + 1])
        grad_probs = times_transposed(grad_out, value)
        delta = jnp.sum(probs * grad_probs, axis=-1, keepdims=True)
        grad_scores = (probs * (grad_probs - delta) * score_scale).astype(jnp.bfloat16)
        turned[:, low : low + HEAD_DIM] = times(grad_scores, key)
        turned[:, width + low : width + low + HEAD_DIM] = outer_rows(grad_scores, query)
        all_ref[:, 2 * width + low : 2 * width + low + HEAD_DIM] = outer_rows(
            probs.astype(jnp.bfloat16), grad_out
        ).astype(jnp.bfloat16)
    cosine, sine = cosine_ref[...], sine_ref[...]
    for start in range(0, 2 * width, LANES):
        tile = turned[:, start : start + LANES]
        all_ref[:, start : start + LANES] = (tile * cosine - swap_halves(tile) * sine).astype(jnp.bfloat16)
    grad_all = all_ref[...]
    for first in range(0, partial_ref.shape[1], 3 * LANES):
        partial_ref[:, first : first + 3 * LANES] = times_transposed(
            grad_all, weight_ref[first : first + 3 * LANES, : grad_all.shape[1]]
        ).astype(jnp.bfloat16)


def local_call(kernel, name, operands, outs, scratch, flops):
    vmem = pl.BlockSpec(memory_space=pltpu.VMEM)
    return pl.pallas_call(
        kernel,
        name=name,
        out_shape=tuple(outs),
        in_specs=[vmem] * len(operands),
        out_specs=tuple([vmem] * len(outs)),
        scratch_shapes=scratch,
        compiler_params=pltpu.CompilerParams(vmem_limit_bytes=48 * 2**20),
        cost_estimate=pl.CostEstimate(flops=flops, bytes_accessed=20 * 10**6, transcendentals=0),
    )(*operands)


def outer_kernel(*refs):
    out_ref, first = refs[-1], 0
    for left, right in zip(refs[:-1:2], refs[1:-1:2]):
        last = first + right.shape[1]
        out_ref[:, first:last] = outer_rows(left[...], right[...]).astype(out_ref.dtype)
        first = last


def outer_sums(*pairs):
    rows, width = pairs[0][0].shape
    columns = sum(right.shape[1] for _, right in pairs)
    tile = 256
    specs, operands = [], []
    for left, right in pairs:
        specs += [
            pl.BlockSpec((rows, tile), lambda i: (0, i)),
            pl.BlockSpec(right.shape, lambda i: (0, 0)),
        ]
        operands += [left, right]
    return pl.pallas_call(
        outer_kernel,
        name="outer_sums",
        grid=(width // tile,),
        out_shape=jax.ShapeDtypeStruct((width, columns), jnp.bfloat16),
        in_specs=specs,
        out_specs=pl.BlockSpec((tile, columns), lambda i: (i, 0)),
        compiler_params=pltpu.CompilerParams(vmem_limit_bytes=40 * 2**20),
        cost_estimate=pl.CostEstimate(
            flops=2 * rows * width * columns, bytes_accessed=2 * (rows + width) * columns, transcendentals=0
        ),
    )(*operands)


def attention_forward(query, key, value, bias):
    scores = jnp.einsum("qhd,khd->hqk", query, key, preferred_element_type=jnp.float32) * score_scale
    scores = scores + bias[None]
    top = jnp.max(scores, axis=-1, keepdims=True)
    terms = jnp.exp(scores - top)
    probs = terms / jnp.sum(terms, axis=-1, keepdims=True)
    attended = jnp.einsum(
        "hqk,khd->qhd", probs.astype(jnp.bfloat16), value, preferred_element_type=jnp.float32
    )
    return attended, probs


def attention_backward(query, key, value, probs, grad_out):
    grad_probs = jnp.einsum("qhd,khd->hqk", grad_out, value, preferred_element_type=jnp.float32)
    delta = jnp.sum(probs * grad_probs, axis=-1, keepdims=True)
    grad_scores = (probs * (grad_probs - delta) * score_scale).astype(jnp.bfloat16)
    grad_query = jnp.einsum("hqk,khd->qhd", grad_scores, key, preferred_element_type=jnp.float32)
    grad_key = jnp.einsum("hqk,qhd->khd", grad_scores, query, preferred_element_type=jnp.float32)
    grad_value = jnp.einsum(
        "hqk,qhd->khd", probs.astype(jnp.bfloat16), grad_out, preferred_element_type=jnp.float32
    )
    return grad_query, grad_key, grad_value


def lane_tables(tables):
    cosine, sine_table = tables[0][:, 0], tables[1][:, 0]
    return (
        jnp.concatenate([cosine] * (LANES // cosine.shape[1]), axis=1),
        jnp.concatenate([-sine_table, sine_table] * (LANES // HEAD_DIM), axis=1),
    )


def forward_attention(normed, weight, plan, bias, tables, kernels):
    width = plan.head_width
    rows = normed.shape[0]
    if kernels:
        columns = (3 * width + LANES - 1) // LANES * LANES
        wide = (width + LANES - 1) // LANES * LANES
        sized = jax.ShapeDtypeStruct
        return (
            functools.partial(attend_kernel, plan.head_count),
            [normed, weight, *lane_tables(tables), bias],
            [
                sized((rows, columns), jnp.bfloat16),
                sized((rows, width), jnp.bfloat16),
                sized((rows, LANES), jnp.float32),
            ],
            [pltpu.VMEM((rows, wide), jnp.bfloat16)],
            (rows, weight.shape[0]),
        ), None
    head_shape = (rows, plan.head_count, HEAD_DIM)
    mixed = times(normed, weight[:, : 3 * width])
    query = rotate(mixed[:, :width].reshape(head_shape), tables, 1.0).astype(jnp.bfloat16)
    key = rotate(mixed[:, width : 2 * width].reshape(head_shape), tables, 1.0).astype(jnp.bfloat16)
    value = mixed[:, 2 * width :].reshape(head_shape).astype(jnp.bfloat16)
    attended, probs = attention_forward(query, key, value, bias)
    attended = attended.reshape(rows, width).astype(jnp.bfloat16)
    partial_sum = times_transposed(attended, weight[:, 3 * width :]).astype(jnp.bfloat16)
    return partial_sum, (normed, query, key, value, probs, attended)


def feed_kernel(normed_ref, gate_ref, up_ref, down_ref, partial_ref, gating_ref, upward_ref, activated_ref):
    normed = normed_ref[...]
    for first in range(0, gating_ref.shape[1], 2 * LANES):
        tile = slice(first, first + 2 * LANES)
        gating, upward = times(normed, gate_ref[:, tile]), times(normed, up_ref[:, tile])
        gating_ref[:, tile] = gating
        upward_ref[:, tile] = upward
        activated_ref[:, tile] = (jax.nn.silu(gating) * upward).astype(jnp.bfloat16)
    activated = activated_ref[...]
    for first in range(0, partial_ref.shape[1], 2 * LANES):
        tile = slice(first, first + 2 * LANES)
        partial_ref[:, tile] = times_transposed(activated, down_ref[tile, :]).astype(jnp.bfloat16)


def feed_prelude(normed, weights):
    rows, width = normed.shape
    units = weights[0].shape[1]
    sized = jax.ShapeDtypeStruct
    wide = sized((rows, units), jnp.float32)
    return (feed_kernel, [normed, *weights], [wide, wide, sized((rows, units), jnp.bfloat16)], [], (rows, width))


def forward_feed(normed, weights):
    gate_weight, up_weight, down_weight = weights
    gating, upward = times(normed, gate_weight), times(normed, up_weight)
    activated = (jax.nn.silu(gating) * upward).astype(jnp.bfloat16)
    partial_sum = times_transposed(activated, down_weight).astype(jnp.bfloat16)
    return partial_sum, (normed, gating, upward, activated)


def backward_feed(down_grad, weights, record):
    gate_weight, up_weight, down_weight = weights
    normed, gating, upward, activated = record
    grad_act = times(down_grad, down_weight)
    sigmoid_gate = jax.nn.sigmoid(gating)
    grad_gating = (grad_act * upward * sigmoid_gate * (1.0 + gating * (1.0 - sigmoid_gate))).astype(jnp.bfloat16)
    grad_upward = (grad_act * gating * sigmoid_gate).astype(jnp.bfloat16)
    partial_sum = (times_transposed(grad_gating, gate_weight) + times_transposed(grad_upward, up_weight)).astype(
        jnp.bfloat16
    )
    return partial_sum, ((normed, grad_gating), (normed, grad_upward), (down_grad, activated))


def backward_attention(branch_grad, weight, record, plan, bias, tables, kernels):
    width = plan.head_width
    rows = branch_grad.shape[0]
    if kernels:
        normed, mixed, attended, total = record
        wide = (width + LANES - 1) // LANES * LANES
        sized = jax.ShapeDtypeStruct
        partial_sum, grad_all = local_call(
            functools.partial(attend_back_kernel, plan.head_count),
            "attend_back",
            [branch_grad, weight, mixed, total, *lane_tables(tables), bias],
            [sized((rows, weight.shape[0]), jnp.bfloat16), sized(mixed.shape, jnp.bfloat16)],
            [pltpu.VMEM((rows, wide), jnp.bfloat16), pltpu.VMEM((rows, 2 * width), jnp.float32)],
            4 * rows * weight.shape[0] * weight.shape[1],
        )
        return partial_sum, ((normed, grad_all[:, : 3 * width]), (branch_grad, attended))
    normed, query, key, value, probs, attended = record
    grad_mixed = times(branch_grad, weight[:, 3 * width :]).astype(jnp.bfloat16)
    grad_query, grad_key, grad_value = attention_backward(
        query, key, value, probs, grad_mixed.reshape(query.shape)
    )
    grad_all = jnp.concatenate(
        [
            rotate(grad_query, tables, -1.0).reshape(rows, width),
            rotate(grad_key, tables, -1.0).reshape(rows, width),
            grad_value.reshape(rows, width),
        ],
        axis=1,
    ).astype(jnp.bfloat16)
    partial_sum = times_transposed(grad_all, weight[:, : 3 * width]).astype(jnp.bfloat16)
    return partial_sum, ((normed, grad_all), (branch_grad, attended))


def body(
    inputs,
    cotangent,
    lengths,
    dealing,
    span_table,
    prenorm_gain,
    query_weight,
    keys_weight,
    values_weight,
    project_weight,
    postnorm_gain,
    gating_weight,
    upward_weight,
    downward_weight,
):
    n_dp, n_ctx, n_ten = lax.axis_size("dp"), lax.axis_size("ctx"), lax.axis_size("tensor")
    plan = Plan(n_dp, n_ctx, query_weight.shape[2], gating_weight.shape[2])
    own_rows = inputs.shape[0]
    half_span = own_rows // 2
    share = own_rows // n_ten
    group_index = lax.axis_index("dp")
    core = lax.axis_index("tensor")
    seq_count = lengths.shape[0] // n_dp
    starts, seq_lens = group_layout(lengths, dealing, group_index, seq_count)
    span_row = lax.dynamic_index_in_dim(span_table, group_index, 0, keepdims=False)
    facts = slot_facts(slots_for(own_rows * n_ctx, span_row, half_span), starts, seq_lens)
    tables = rope_tables(facts[2], HEAD_DIM // 2)
    bias = jnp.where(allowed(facts, facts), 0.0, masked_score)

    kernels = (n_dp, n_ctx, n_ten) == (4, 4, 2)
    comm = LineComm() if kernels else PlainComm()
    head_cuts = [cut * HEAD_DIM for cut in plan.head_cuts]

    attention_stack = [query_weight, keys_weight, values_weight, project_weight.transpose(0, 2, 1)]
    feed_stack = [gating_weight, upward_weight, downward_weight.transpose(0, 2, 1)]

    def windows(layer):
        if kernels:
            return cut_layer(plan, layer, attention_stack, feed_stack)
        attention = [cut_windows(weight[layer], head_cuts, plan.head_width) for weight in attention_stack]
        feed = [cut_windows(weight[layer], plan.unit_cuts, plan.unit_width) for weight in feed_stack]
        return [jnp.concatenate(attention, axis=2)] + feed

    def joined(blocks):
        return blocks.reshape(-1, blocks.shape[-1])

    own_gains = jnp.pad(
        jnp.concatenate([prenorm_gain, postnorm_gain], axis=0).T, ((0, 0), (0, LANES - 2 * LAYERS))
    )
    own_gains = jnp.broadcast_to(own_gains[None], (n_ctx,) + own_gains.shape)
    attention_windows, gate, up, down = windows(0)
    attention_blocks, gain_blocks, inputs_whole, gate, up, down = comm.moves(
        (Fetch, attention_windows),
        (Fetch, own_gains),
        (Collect, inputs),
        (Fetch, gate),
        (Exchange, up),
        (Exchange, down),
        urgent=3,
    )
    gains = gain_blocks.reshape(-1, LANES)[:, : 2 * LAYERS].T.astype(jnp.float32)
    front = [gains[layer : layer + 1] for layer in range(LAYERS)]
    behind = [gains[LAYERS + layer : LAYERS + layer + 1] for layer in range(LAYERS)]
    attention_weights, feed_weights = [None] * LAYERS, [None] * LAYERS
    attention_records, feed_records, middles = [None] * LAYERS, [None] * LAYERS, [None] * LAYERS
    starts_of = [None] * LAYERS

    attention_weights[0] = joined(attention_blocks)
    residual = comm.own_rows(inputs_whole).astype(jnp.float32)
    normed = (rms_parts(inputs_whole.astype(jnp.float32))[0] * front[0]).astype(jnp.bfloat16)
    for layer in range(LAYERS):
        starts_of[layer] = residual
        more = layer + 1 < LAYERS
        partial_sum, attention_records[layer] = forward_attention(
            normed, attention_weights[layer], plan, bias, tables, kernels
        )
        prelude = partial_sum if kernels else None
        jobs = [(Spread, up, 6, 2), (Spread, down, 14, 2)]
        if more:
            next_windows = windows(layer + 1)
            jobs += [(Exchange, next_windows[0]), (Exchange, next_windows[1])]
        else:
            jobs += [(Collect, cotangent, 5, 4)]
        hidden, normed_two, (up, down, *moved), made = comm.forward(
            None if kernels else partial_sum, residual, behind[layer], jobs, prelude
        )
        if kernels:
            attention_records[layer] = (normed, *made)
        normed = normed_two
        feed_weights[layer] = [joined(blocks) for blocks in (gate, up, down)]
        middles[layer] = hidden
        if more:
            jobs = [
                (Spread, moved[0], 8, 3),
                (Spread, moved[1], 19, 2),
                (Exchange, next_windows[2]),
                (Exchange, next_windows[3]),
            ]
            prelude, partial_sum = None, None
            if kernels:
                prelude = feed_prelude(normed, feed_weights[layer])
            else:
                partial_sum, feed_records[layer] = forward_feed(normed, feed_weights[layer])
            residual, normed_next, moved, made = comm.forward(partial_sum, hidden, front[layer + 1], jobs, prelude)
            if kernels:
                feed_records[layer] = (normed, *made)
            normed = normed_next
            attention_weights[layer + 1] = joined(moved[0])
            gate, up, down = moved[1:]
        else:
            last_sum, feed_records[layer] = forward_feed(normed, feed_weights[layer])
            cotangent_whole = moved[0]

    grad_rows = comm.own_rows(cotangent_whole).astype(jnp.float32)
    down_grad = (depth_scale * cotangent_whole.astype(jnp.float32)).astype(jnp.bfloat16)
    gain_fronts, gain_backs, attention_parts, feed_parts = [[None] * LAYERS for _ in range(4)]
    for layer in reversed(range(LAYERS)):
        more, last_layer = layer > 0, layer + 1 == LAYERS
        partial_sum, pairs = backward_feed(down_grad, feed_weights[layer], feed_records[layer])
        sums = outer_sums(*pairs)
        partial_sum, sums = lax.optimization_barrier((partial_sum, sums))
        feed_parts[layer] = reduce_grads(sums, n_ctx)
        jobs = [] if last_layer else [(Exchange, feed_parts[layer + 1])]
        grad_rows, gain_backs[layer], branch_grad, moved = comm.backward(
            partial_sum, middles[layer], grad_rows, behind[layer], jobs
        )
        if not last_layer:
            feed_parts[layer + 1] = moved[0]
        partial_sum, pairs = backward_attention(
            branch_grad, attention_weights[layer], attention_records[layer], plan, bias, tables, kernels
        )
        sums = outer_sums(*pairs)
        partial_sum, sums = lax.optimization_barrier((partial_sum, sums))
        attention_parts[layer] = reduce_grads(sums, n_ctx)
        if more:
            grad_rows, gain_fronts[layer], down_grad, _ = comm.backward(
                partial_sum, starts_of[layer], grad_rows, front[layer], []
            )
        else:
            others = jnp.concatenate(gain_fronts[1:] + gain_backs, axis=0)
            jobs = [(Exchange, attention_parts[layer + 1])]
            grad_inputs, gain_sums, moved = comm.backward_last(
                partial_sum, starts_of[layer], grad_rows, front[layer], jobs, others
            )
            attention_parts[layer + 1] = moved[0]
    last_sum, grad_inputs = lax.optimization_barrier((last_sum, grad_inputs))
    output, moved = comm.last(last_sum, middles[LAYERS - 1], [(Exchange, feed_parts[0])])
    feed_parts[0] = moved[0]
    attention_parts[0], output = lax.optimization_barrier((attention_parts[0], output))
    (attention_parts[0],) = comm.moves((Exchange, attention_parts[0]))
    grad_inputs = grad_inputs.astype(jnp.float32)
    gain_sums = lax.psum(gain_sums, "tensor")

    if kernels:
        joins = join_layers(plan, list(zip(attention_parts, feed_parts)))
    else:

        def spread(parts, index, width, cuts):
            return jnp.stack(
                [join_windows(part[:, :, index * width : (index + 1) * width], cuts) for part in parts]
            ).astype(jnp.float32)

        joins = [spread(attention_parts, i, plan.head_width, head_cuts) for i in range(4)]
        joins += [spread(feed_parts, i, plan.unit_width, plan.unit_cuts) for i in range(3)]
    query_out, keys_out, values_out, project_out, gating_out, upward_out, downward_out = joins
    return (
        output,
        grad_inputs,
        gain_sums[:LAYERS],
        query_out,
        keys_out,
        values_out,
        project_out.transpose(0, 2, 1),
        gain_sums[LAYERS:],
        gating_out,
        upward_out,
        downward_out.transpose(0, 2, 1),
    )


def solution(mesh):
    rows = P(("dp", "ctx"), None)
    gain = P(None, ("dp", "ctx"))
    wide = P(None, ("dp", "ctx"), "tensor")
    tall = P(None, "tensor", ("dp", "ctx"))
    weights = (gain, wide, wide, wide, tall, gain, wide, wide, tall)
    return jax.shard_map(
        body,
        mesh=mesh,
        in_specs=(rows, rows, P(), P(), P()) + weights,
        out_specs=(rows, rows) + weights,
        check_vma=False,
    )
```

```python
import math

import functools

import jax
import jax.numpy as jnp
from jax import lax
from jax.experimental import pallas as pl
from jax.experimental.pallas import tpu as pltpu
from jax.sharding import PartitionSpec as P

MESH = pl.DeviceIdType.MESH

HEAD_DIM = 64
LAYERS = 2
BLOCK = 128
LANES = 128

eps_norm = 1e-05
depth_scale = 1.4 / math.sqrt(40.0)
rope_base = 10000.0
masked_score = -1e30
score_scale = 1.0 / math.sqrt(HEAD_DIM)


def times(left, right):
    return jnp.dot(left, right, preferred_element_type=jnp.float32)


def times_transposed(left, right):
    return lax.dot_general(
        left, right, (((1,), (1,)), ((), ())), preferred_element_type=jnp.float32
    )


def outer_rows(left, right):
    return lax.dot_general(
        left, right, (((0,), (0,)), ((), ())), preferred_element_type=jnp.float32
    )


def rms_parts(values):
    inverse = lax.rsqrt(jnp.mean(values * values, axis=-1, keepdims=True) + eps_norm)
    return (values * inverse, inverse)


def norm_backward(values, gain, grad_normed):
    scaled, inverse = rms_parts(values)
    gain_grad = jnp.sum(grad_normed * scaled, axis=0, keepdims=True)
    grad_scaled = grad_normed * gain
    return (
        gain_grad,
        inverse * (grad_scaled - scaled * jnp.mean(grad_scaled * scaled, axis=-1, keepdims=True)),
    )


def rope_tables(position, half_dim):
    inverse = rope_base ** (-jnp.arange(half_dim).astype(jnp.float32) / half_dim)
    angles = position.astype(jnp.float32)[:, None] * inverse[None, :]
    return (jnp.cos(angles)[:, None, :], jnp.sin(angles)[:, None, :])


def rotate(values, tables, direction):
    cosine, sine_table = tables
    half_dim = values.shape[-1] // 2
    front_half = values[..., :half_dim]
    back_half = values[..., half_dim:]
    return jnp.concatenate(
        [
            front_half * cosine - direction * back_half * sine_table,
            back_half * cosine + direction * front_half * sine_table,
        ],
        axis=-1,
    )


def group_layout(lengths, dealing, group_index, seq_count):
    chosen = lax.dynamic_slice_in_dim(dealing, group_index * seq_count, seq_count)
    matches = chosen[:, None] == jnp.arange(lengths.shape[0], dtype=jnp.int32)[None, :]
    seq_lens = jnp.sum(jnp.where(matches, lengths[None, :], 0), axis=1)
    padded = (seq_lens + BLOCK - 1) // BLOCK * BLOCK
    starts = jnp.cumsum(padded) - padded
    return (starts, seq_lens)


def slots_for(number, span_row, half_span):
    rows = jnp.arange(number, dtype=jnp.int32)
    matches = (rows // half_span)[:, None] == jnp.arange(span_row.shape[0], dtype=jnp.int32)[None, :]
    span_of = jnp.sum(jnp.where(matches, span_row[None, :], 0), axis=1)
    return span_of * half_span + rows % half_span


def slot_facts(slots, starts, seq_lens):
    member = jnp.sum((slots[:, None] >= starts[None, :]).astype(jnp.int32), axis=1) - 1
    matches = member[:, None] == jnp.arange(starts.shape[0], dtype=jnp.int32)[None, :]
    anchor = jnp.sum(jnp.where(matches, starts[None, :], 0), axis=1)
    extent = jnp.sum(jnp.where(matches, seq_lens[None, :], 0), axis=1)
    position = slots - anchor
    return (slots, member, position, (position < extent).astype(jnp.int32))


def allowed(query_facts, key_facts):
    query_slot, query_member, query_position, query_valid = query_facts
    key_slot, key_member, key_position, key_valid = key_facts
    same_slot = query_slot[:, None] == key_slot[None, :]
    both_valid = (query_valid[:, None] == 1) & (key_valid[None, :] == 1)
    causal = (query_member[:, None] == key_member[None, :]) & (
        key_position[None, :] <= query_position[:, None]
    )
    return same_slot | both_valid & causal


class Plan:
    def __init__(self, n_dp, n_ctx, columns, hidden):
        self.n_dp, self.n_ctx = n_dp, n_ctx
        heads = columns // HEAD_DIM
        self.head_cuts = [i * heads // n_ctx for i in range(n_ctx + 1)]
        self.head_count = max(b - a for a, b in zip(self.head_cuts, self.head_cuts[1:]))
        self.head_width = self.head_count * HEAD_DIM
        self.unit_cuts = [i * hidden // n_ctx for i in range(n_ctx + 1)]
        units = max(b - a for a, b in zip(self.unit_cuts, self.unit_cuts[1:]))
        self.unit_width = (units + LANES - 1) // LANES * LANES


def cut_windows(weight, cuts, width):
    pieces = []
    for first, last in zip(cuts, cuts[1:]):
        pieces.append(jnp.pad(weight[:, first:last], ((0, 0), (0, width - (last - first)))))
    return jnp.stack(pieces)


def join_windows(windows, cuts):
    return jnp.concatenate(
        [windows[i, :, : last - first] for i, (first, last) in enumerate(zip(cuts, cuts[1:]))], axis=1
    )


def cut_attention(plan, sources, out):
    for i, ref in enumerate(sources):
        for j, (first, last) in enumerate(zip(plan.head_cuts, plan.head_cuts[1:])):
            start, count = i * plan.head_width, (last - first) * HEAD_DIM
            out[j, :, start : start + count] = ref[:, first * HEAD_DIM : last * HEAD_DIM]
            if count < plan.head_width:
                out[j, :, start + count : start + plan.head_width] = jnp.zeros(
                    (ref.shape[0], plan.head_width - count), ref.dtype
                )


def cut_feed(plan, ref, out):
    for j, (first, last) in enumerate(zip(plan.unit_cuts, plan.unit_cuts[1:])):
        out[j, :, : last - first] = ref[:, first:last]
        out[j, :, last - first :] = jnp.zeros((ref.shape[0], plan.unit_width - (last - first)), ref.dtype)


def start_kernel(plan, *refs):
    weights, refs = take(refs, 7)
    (front_ref, behind_ref, inputs_ref), refs = take(refs, 3)
    cuts, refs = take(refs, 4 * (LAYERS - 1))
    results, refs = take(refs, 6)
    raw, refs = take(refs, 7 * LAYERS)
    (load_sems,), refs = take(refs, 1)
    own_cuts, refs = take(refs, 4)
    (gain_blocks,), refs = take(refs, 1)
    loads = start_loads([ref.at[layer] for layer in range(LAYERS) for ref in weights], raw, load_sems)
    greet(*place())
    kinds = (Collect, Fetch, Fetch, Fetch, Exchange, Exchange)
    sources = [inputs_ref, own_cuts[0], gain_blocks, *own_cuts[1:]]
    jobs = make_jobs(kinds, [0] * 6, sources, results, refs)
    jobs[0].start()
    for copy in loads[:4]:
        copy.wait()
    cut_attention(plan, raw[:4], own_cuts[0])
    jobs[1].start()
    gain_blocks[...] = jnp.zeros(gain_blocks.shape, gain_blocks.dtype)
    for j in range(gain_blocks.shape[0]):
        gain_blocks[j, 0:LAYERS, : front_ref.shape[1]] = front_ref[...]
        gain_blocks[j, LAYERS : 2 * LAYERS, : front_ref.shape[1]] = behind_ref[...]
    jobs[2].start()
    for i in range(3):
        loads[4 + i].wait()
        cut_feed(plan, raw[4 + i], own_cuts[1 + i])
    steps = [job.steps() for job in jobs]
    for i in range(3):
        steps[0][i]()
        steps[1][i]()
    for i in range(3):
        steps[2][i]()
    jobs[3].start()
    for act in steps[3][:3]:
        act()
    jobs[4].start()
    jobs[5].start()
    for act in steps[1][3:] + steps[2][3:]:
        act()
    for layer in range(1, LAYERS):
        for copy in loads[7 * layer : 7 * layer + 7]:
            copy.wait()
        layer_raw, layer_cuts = raw[7 * layer : 7 * layer + 7], cuts[4 * (layer - 1) : 4 * layer]
        cut_attention(plan, layer_raw[:4], layer_cuts[0])
        for i in range(3):
            cut_feed(plan, layer_raw[4 + i], layer_cuts[1 + i])
    for act in steps[3][3:]:
        act()
    for job in jobs:
        job.finish()


def start_call(plan, number, weights, front, behind, inputs):
    vmem, hbm = pl.BlockSpec(memory_space=pltpu.VMEM), pl.BlockSpec(memory_space=pltpu.HBM)
    rows = weights[0].shape[1]
    sized = jax.ShapeDtypeStruct
    windows = [(plan.n_ctx, rows, width) for width in [4 * plan.head_width] + [plan.unit_width] * 3]
    gain_shape = (plan.n_ctx, 16, (rows + LANES - 1) // LANES * LANES)
    own = [sized(shape, jnp.bfloat16) for shape in windows]
    gain_source = sized(gain_shape, jnp.bfloat16)
    kinds = (Collect, Fetch, Fetch, Fetch, Exchange, Exchange)
    sources = (inputs, own[0], gain_source, *own[1:])
    results = [kind.result(source) for kind, source in zip(kinds, sources)]
    dma = pltpu.SemaphoreType.DMA
    outs = pl.pallas_call(
        functools.partial(start_kernel, plan),
        name="start",
        out_shape=tuple(own * (LAYERS - 1) + results),
        in_specs=[hbm] * 7 + [vmem] * 2 + [hbm],
        out_specs=tuple([vmem] * 4 * (LAYERS - 1) + [hbm] * 6),
        scratch_shapes=[pltpu.VMEM(weight.shape[1:], weight.dtype) for _ in range(LAYERS) for weight in weights]
        + [dma((7 * LAYERS,))]
        + [pltpu.VMEM(shape, jnp.bfloat16) for shape in windows + [gain_shape]]
        + [dma((kind.semaphores,)) for kind in kinds],
        compiler_params=pltpu.CompilerParams(
            collective_id=number, has_side_effects=True, vmem_limit_bytes=START_MIB * 2**20
        ),
        cost_estimate=pl.CostEstimate(flops=10**9, bytes_accessed=100 * 10**6, transcendentals=0),
    )(*weights, front, behind, inputs)
    cuts, results = take(outs, 4 * (LAYERS - 1))
    return [cuts[4 * i : 4 * i + 4] for i in range(LAYERS - 1)], results


def join_kernel(plan, places, count, *refs):
    sources, outs = refs[:count], refs[count:]
    for source, (layer, top, weights) in zip(sources, places):
        rows, start = source.shape[1], 0
        for i in weights:
            cuts = [cut * HEAD_DIM for cut in plan.head_cuts] if i < 4 else plan.unit_cuts
            for j, (first, last) in enumerate(zip(cuts, cuts[1:])):
                outs[i][layer, top : top + rows, first:last] = source[j, :, start : start + last - first].astype(
                    jnp.float32
                )
            start += plan.head_width if i < 4 else plan.unit_width


def join_layers(plan, attention_parts, feed_parts):
    sources, places = [], []
    for parts_of, weights in ((attention_parts, (0, 1, 2, 3)), (feed_parts, (4, 5, 6))):
        for layer, parts in enumerate(parts_of):
            top = 0
            for part in parts:
                sources.append(part)
                places.append((layer, top, weights))
                top += part.shape[1]
    outs = [
        jax.ShapeDtypeStruct((LAYERS, top, width), jnp.float32)
        for width in [plan.head_cuts[-1] * HEAD_DIM] * 4 + [plan.unit_cuts[-1]] * 3
    ]
    return local_call(functools.partial(join_kernel, plan, places, len(sources)), "join_layers", sources, outs, [], 0)


def reduce_grads(full, n_ctx):
    own = lax.psum_scatter(full, "dp", scatter_dimension=0, tiled=True)
    return own.reshape(n_ctx, -1, own.shape[-1])


def gather_rows(piece):
    return lax.all_gather(piece, ("ctx", "tensor"), axis=0, tiled=True)


def scatter_rows(partial_sum):
    return lax.psum_scatter(
        partial_sum.astype(jnp.bfloat16), ("ctx", "tensor"), scatter_dimension=0, tiled=True
    ).astype(jnp.float32)


SLOT = 16
START_MIB = 58
PARTS = 1
SKEW = 3


def place():
    return lax.axis_index("dp"), lax.axis_index("ctx"), lax.axis_index("tensor")


def slot_rows(base, index):
    return pl.ds(pl.multiple_of(base + index * SLOT, SLOT), SLOT)


def send(src, dst, send_sem, recv_sem, target):
    return pltpu.make_async_remote_copy(
        src_ref=src, dst_ref=dst, send_sem=send_sem, recv_sem=recv_sem, device_id=target, device_id_type=MESH
    )


def greet(d, c, t, everyone=False):
    barrier = pltpu.get_barrier_semaphore()
    others = [(d, c, 1 - t), (d, c ^ 1, t), (d, c ^ 2, t), (d, c ^ 3, t), (d ^ 1, c, t), (d ^ 2, c, t)]
    if everyone:
        others = others[:1] + [(d ^ (k // 4), c ^ (k % 4), t) for k in range(1, 16)]
    for other in others:
        pl.semaphore_signal(barrier, inc=1, device_id=other, device_id_type=MESH)
    pl.semaphore_wait(barrier, len(others))


class Job:
    everyone = False
    near = False
    late = False

    @staticmethod
    def scratch(source):
        return []

    def steps(self):
        return []


class Exchange(Job):
    semaphores = 7
    span = None

    @classmethod
    def rows(cls, source):
        return cls.span or (0, source.shape[1])

    @classmethod
    def result(cls, source):
        first, last = cls.rows(source)
        return jax.ShapeDtypeStruct((source.shape[0], last - first, source.shape[2]), source.dtype)

    def __init__(self, source, result, sems):
        d, c, t = place()
        first, last = self.rows(source)
        rows = pl.ds(first, last - first)
        self.own = pltpu.make_async_copy(source.at[c, rows], result.at[c], sems.at[6])
        self.copies = [
            send(source.at[c ^ k, rows], result.at[c], sems.at[k - 1], sems.at[k + 2], (d, c ^ k, t))
            for k in (3, 2, 1)
        ]

    def start(self):
        for copy in self.copies:
            copy.start()
        self.own.start()

    def finish(self):
        for copy in self.copies:
            copy.wait()
        self.own.wait()


def exchange_rows(first, last):
    class Some(Exchange):
        span = (first, last)

    return Some


class Collect(Job):
    semaphores = 25

    @staticmethod
    def result(source):
        return jax.ShapeDtypeStruct((4 * source.shape[0], source.shape[1]), source.dtype)

    def __init__(self, source, result, sems):
        d, c, t = place()
        block = source.shape[0]
        half = block // 2

        def piece(chip):
            return result.at[pl.ds(pl.multiple_of(chip * block + t * half, half), half)]

        self.own = pltpu.make_async_copy(source, result.at[pl.ds(pl.multiple_of(c * block, block), block)], sems.at[24])
        mine = source.at[pl.ds(pl.multiple_of(t * half, half), half)]
        self.hops, self.onward = {}, {}
        for way, more, target in ((0, c < 3, (d, c + 1, t)), (1, c > 0, (d, c - 1, t))):
            for hop in range(4):
                chip = c - hop if way == 0 else c + hop
                held = (chip >= 0) if way == 0 else (chip <= 3)
                if hop < 3:
                    self.hops[way, hop] = (
                        more & held,
                        send(
                            piece(chip) if hop else mine,
                            piece(chip),
                            sems.at[way * 12 + hop],
                            sems.at[way * 12 + 3 + hop],
                            target,
                        ),
                    )
                if hop:
                    self.onward[way, hop] = (
                        held,
                        send(
                            piece(chip),
                            piece(chip),
                            sems.at[way * 12 + 5 + hop],
                            sems.at[way * 12 + 8 + hop],
                            (d, c, 1 - t),
                        ),
                    )

    def start(self):
        for way in range(2):
            go, copy = self.hops[way, 0]
            pl.when(go)(copy.start)
        self.own.start()

    def steps(self):
        return [functools.partial(self.pass_on, hop) for hop in range(1, 4)]

    def pass_on(self, hop):
        for way in range(2):
            held, onward = self.onward[way, hop]
            arrived = self.hops[way, hop - 1][1]

            @pl.when(held)
            def _():
                arrived.wait_recv()
                onward.start()

            if hop < 3:
                go, copy = self.hops[way, hop]
                pl.when(go)(copy.start)

    def finish(self):
        for go, copy in self.hops.values():
            pl.when(go)(copy.wait_send)
        for held, onward in self.onward.values():
            pl.when(held)(onward.wait)
        self.own.wait()


class GainScatter(Job):
    semaphores = 33
    everyone = True
    near = True
    late = True

    @staticmethod
    def blocks(source):
        return (16, 8, (source.shape[1] // 16 + LANES - 1) // LANES * LANES)

    @staticmethod
    def result(source):
        return jax.ShapeDtypeStruct(GainScatter.blocks(source), source.dtype)

    @staticmethod
    def scratch(source):
        return [pltpu.VMEM(GainScatter.blocks(source), source.dtype)] * 3

    def __init__(self, source, result, sems, own, other, cut):
        d, c, t = place()
        mine = d * 4 + c
        self.source, self.terms, self.cut = source, (own, other), cut
        self.across = send(own, other, sems.at[31], sems.at[32], (d, c, 1 - t))
        self.own = pltpu.make_async_copy(cut.at[mine], result.at[mine], sems.at[0])
        self.copies = []
        for k in range(1, 16):
            g, i = d ^ (k // 4), c ^ (k % 4)
            self.copies.append(send(cut.at[g * 4 + i], result.at[mine], sems.at[k], sems.at[k + 15], (g, i, t)))

    def start(self, made):
        own, other = self.terms
        own[...] = jnp.zeros(own.shape, own.dtype)
        part = made.shape[1] // 16
        for i in range(16):
            own[i, 0:1, :part] = made[:, i * part : (i + 1) * part]
            rows = self.source.shape[0]
            own[i, 1 : 1 + rows, :part] = self.source[:, i * part : (i + 1) * part]
        self.across.start()
        self.across.wait()
        self.cut[...] = own[...] + other[...]
        for copy in self.copies:
            copy.start()
        self.own.start()

    def finish(self):
        for copy in self.copies:
            copy.wait()
        self.own.wait()


class Return(Job):
    semaphores = 31
    near = True
    order = (0, 2, 1, 3)

    @staticmethod
    def result(source):
        return jax.ShapeDtypeStruct((4,) + source.shape[1:], source.dtype)

    @staticmethod
    def scratch(source):
        four = pltpu.VMEM((4,) + source.shape[1:], source.dtype)
        return [four] * 5

    def __init__(self, source, result, sems, corner_in, x_in, y_in, passed, total):
        d, c, t = place()
        self.corner_in, self.sides_in, self.passed, self.total = corner_in, (x_in, y_in), passed, total
        self.terms, self.corners, self.sides, self.line = [], [], [], [None]
        for k in range(4):
            i = c ^ k
            way = k // 2
            self.terms.append([source.at[(d ^ flip) * 4 + i] for flip in (0, 1, 2)])
            self.corners.append(
                send(source.at[(d ^ 3) * 4 + i], corner_in.at[k], sems.at[k], sems.at[4 + k], (d ^ (1 + way), c, t))
            )
            self.sides.append(
                [
                    send(
                        passed.at[k] if side != way else source.at[(d ^ (1 + side)) * 4 + i],
                        self.sides_in[side].at[k],
                        sems.at[8 + 2 * k + side],
                        sems.at[16 + 2 * k + side],
                        (d ^ (1 + side), c, t),
                    )
                    for side in range(2)
                ]
            )
            if k:
                self.line.append(send(total.at[k], result.at[c], sems.at[23 + k], sems.at[26 + k], (d, i, t)))
        self.own = pltpu.make_async_copy(total.at[0], result.at[c], sems.at[30])

    def start(self):
        for k in self.order:
            self.corners[k].start()
        for k in self.order:
            self.sides[k][k // 2].start()

    def steps(self):
        return [functools.partial(self.pass_term, k) for k in self.order] + [
            functools.partial(self.add_up, k) for k in (3, 2, 1, 0)
        ]

    def pass_term(self, k):
        side = 1 - k // 2
        self.corners[k].wait_recv()
        self.passed[k] = (self.terms[k][1 + side][...].astype(jnp.float32) + self.corner_in[k].astype(jnp.float32)).astype(
            self.passed.dtype
        )
        self.sides[k][side].start()

    def add_up(self, k):
        for side in range(2):
            self.sides[k][side].wait_recv()
        self.total[k] = (
            self.terms[k][0][...].astype(jnp.float32)
            + self.sides_in[0][k].astype(jnp.float32)
            + self.sides_in[1][k].astype(jnp.float32)
        ).astype(self.total.dtype)
        if k:
            self.line[k].start()
        else:
            self.own.start()

    def finish(self):
        for k in range(4):
            self.corners[k].wait_send()
            for copy in self.sides[k]:
                copy.wait_send()
            if k:
                self.line[k].wait()
        self.own.wait()


class Fetch(Job):
    semaphores = 31

    @staticmethod
    def result(source):
        return jax.ShapeDtypeStruct((16,) + source.shape[1:], source.dtype)

    order = (0, 2, 1, 3)

    def __init__(self, source, result, sems):
        d, c, t = place()
        self.own = pltpu.make_async_copy(source.at[c], result.at[d * 4 + c], sems.at[0])
        self.line = [None]
        for k in range(1, 4):
            self.line.append(
                send(source.at[c ^ k], result.at[d * 4 + c], sems.at[k], sems.at[k + 3], (d, c ^ k, t))
            )
        self.link(source, result, sems)

    def link(self, source, result, sems):
        d, c, t = place()
        self.side, self.corners = [], []
        for k in range(4):
            held = result.at[d * 4 + (c ^ k)]
            ready = held if self.line[k] is not None else source.at[c ^ k]
            self.side.append(
                [
                    send(ready, held, sems.at[7 + 2 * k + way], sems.at[15 + 2 * k + way], (d ^ (1 + way), c, t))
                    for way in range(2)
                ]
            )
            way = k // 2
            passed = result.at[(d ^ (1 + way)) * 4 + (c ^ k)]
            self.corners.append(
                send(passed, passed, sems.at[23 + k], sems.at[27 + k], (d ^ (2 - way), c, t))
            )

    def start(self):
        self.own.start()
        for k in (3, 2, 1):
            self.line[k].start()
        for copy in self.side[0]:
            copy.start()

    def steps(self):
        return [functools.partial(self.pass_sides, k) for k in (1, 2, 3)] + self.corner_steps()

    def corner_steps(self):
        return [functools.partial(self.pass_corner, k) for k in self.order]

    def pass_sides(self, k):
        self.line[k].wait_recv()
        for copy in self.side[k]:
            copy.start()

    def pass_corner(self, k):
        self.side[k][k // 2].wait_recv()
        self.corners[k].start()

    def finish(self):
        for k in range(4):
            self.side[k][1 - k // 2].wait_recv()
        for k in range(4):
            self.corners[k].wait()
            for copy in self.side[k]:
                copy.wait_send()
            if self.line[k] is not None:
                self.line[k].wait_send()
        self.own.wait()


class Spread(Fetch):
    @staticmethod
    def result(source):
        return jax.ShapeDtypeStruct((16,) + source.shape[1:], source.dtype)

    def __init__(self, source, result, sems):
        d, c, t = place()
        self.own = pltpu.make_async_copy(source, result.at[pl.ds(d * 4, 4)], sems.at[0])
        self.line = [None] * 4
        self.link(source, result, sems)

    def start(self):
        for k in self.order:
            for copy in self.side[k]:
                copy.start()
        self.own.start()

    def steps(self):
        return self.corner_steps()


def take(refs, count):
    return refs[:count], refs[count:]


def make_jobs(kinds, scratch_counts, sources, results, refs):
    jobs = []
    for kind, count, source, result in zip(kinds, scratch_counts, sources, results):
        (sems, *scratch), refs = take(refs, 1 + count)
        jobs.append(kind(source, result, sems, *scratch))
    return jobs


def job_specs(jobs):
    vmem, hbm = pl.BlockSpec(memory_space=pltpu.VMEM), pl.BlockSpec(memory_space=pltpu.HBM)
    sources = [job[1] for job in jobs]
    in_specs = [vmem if job[0].near else hbm for job in jobs]
    out_shapes = [job[0].result(job[1]) for job in jobs]
    scratch, counts = [], []
    for kind, source, *_ in jobs:
        extra = kind.scratch(source)
        scratch += [pltpu.SemaphoreType.DMA((kind.semaphores,))] + extra
        counts.append(len(extra))
    return sources, in_specs, out_shapes, [hbm] * len(jobs), scratch, counts


def jobs_kernel(kinds, counts, urgent, *refs):
    n = len(kinds)
    greet(*place(), any(kind.everyone for kind in kinds))
    jobs = make_jobs(kinds, counts, refs[:n], refs[n : 2 * n], refs[2 * n :])
    first, later = jobs[:urgent], jobs[urgent:]
    for job in first:
        job.start()
    rest = []
    for job in first:
        todo = job.steps()
        for act in todo[:3]:
            act()
        rest += todo[3:]
    for job in later:
        job.start()
    for act in rest:
        act()
    for job in later:
        for act in job.steps():
            act()
    for job in jobs:
        job.finish()


def jobs_call(number, jobs, urgent):
    sources, in_specs, out_shapes, out_specs, scratch, counts = job_specs(jobs)
    return pl.pallas_call(
        functools.partial(jobs_kernel, [job[0] for job in jobs], counts, urgent),
        name="moves",
        out_shape=tuple(out_shapes),
        in_specs=in_specs,
        out_specs=tuple(out_specs),
        scratch_shapes=scratch,
        compiler_params=pltpu.CompilerParams(
            collective_id=number, has_side_effects=True, vmem_limit_bytes=48 * 2**20
        ),
        cost_estimate=pl.CostEstimate(flops=10**9, bytes_accessed=100 * 10**6, transcendentals=0),
    )(*sources)


def drain(ref, sem):
    pltpu.make_async_copy(ref, ref, sem).wait()


class Line:
    scratch_count = 14

    @staticmethod
    def scratch(block, width):
        pieces = block // SLOT * PARTS
        piece = pltpu.VMEM((block, width), jnp.bfloat16)
        dma = pltpu.SemaphoreType.DMA
        return (
            [piece] * 4
            + [pltpu.VMEM((2, block, width), jnp.bfloat16), piece, dma((6,)), dma((2, 2))]
            + [dma((pieces,))] * 4
            + [dma((2,)), pltpu.VMEM((SLOT, width), jnp.float32)]
        )

    def __init__(self, settle, gather, partial_ref, settle_in, settle_out, whole_ref, scratch):
        self.settle, self.gather = settle, gather
        self.partial_ref, self.settle_in, self.settle_out, self.whole_ref = partial_ref, settle_in, settle_out, whole_ref
        (
            self.acc_up,
            self.acc_down,
            self.in_up,
            self.in_down,
            self.sib,
            self.stage,
            self.send_sems,
            self.sib_sems,
            self.up_sems,
            self.down_sems,
            self.back_up,
            self.back_down,
            self.whole_sems,
            self.sum_ref,
        ) = scratch
        d, c, t = place()
        self.block = self.acc_up.shape[0]
        self.pieces = self.block // SLOT * PARTS
        self.columns = self.acc_up.shape[1] // PARTS
        self.turns = self.pieces + SKEW * (6 if gather else 3)
        self.sibling, self.above, self.below = (d, c, 1 - t), (d, c + 1, t), (d, c - 1, t)
        self.down_base, self.up_base = t * self.block, (2 + t) * self.block
        self.low, self.high = c > 0, c < 3
        self.middle = self.low & self.high

    def begin(self):
        _, _, t = place()
        half = self.block // 2
        for part in range(2):
            for which, base in ((0, (1 - t) * self.block), (1, (3 - t) * self.block)):
                rows = pl.ds(pl.multiple_of(base + part * half, half), half)
                send(
                    self.partial_ref.at[rows],
                    self.sib.at[which, pl.ds(part * half, half)],
                    self.send_sems.at[0],
                    self.sib_sems.at[which, part],
                    self.sibling,
                ).start()

        @pl.when(self.middle)
        def _():
            for ref in self.settle_out:
                ref[...] = jnp.zeros(ref.shape, ref.dtype)

    def piece(self, base, index, part):
        return (slot_rows(base, index // PARTS), pl.ds(part * self.columns, self.columns))

    def chain(self, index, which, base, first, last, into, acc, recv_sems, send_sem, target, back_target, back_sems):
        half = self.block // 2
        pieces = self.pieces

        @pl.when((index >= 0) & (index < pieces) & (index % (pieces // 2) == 0))
        def _():
            drain(self.sib.at[which, pl.ds(0, half)], self.sib_sems.at[which, index // (pieces // 2)])

        for part in range(PARTS):
            here = self.piece(0, index, part)
            own = self.piece(base, index, part)

            @pl.when((index >= 0) & (index < pieces) & (index % PARTS == part))
            def _():
                def term():
                    return self.partial_ref[own].astype(jnp.float32) + self.sib[(which, *here)].astype(jnp.float32)

                def pass_on(total):
                    acc[here] = total.astype(jnp.bfloat16)
                    send(acc.at[here], into.at[here], send_sem, recv_sems.at[index], target).start()

                @pl.when(first)
                def _():
                    pass_on(term())

                @pl.when(jnp.logical_not(first))
                def _():
                    drain(into.at[here], recv_sems.at[index])

                @pl.when(self.middle)
                def _():
                    pass_on(term() + into[here].astype(jnp.float32))

                @pl.when(last)
                def _():
                    self.sum_ref[:, here[1]] = term() + into[here].astype(jnp.float32)
                    if part == PARTS - 1:
                        self.settled(index, which, here[0], own[0], back_target, back_sems)

    def settled(self, index, which, rows, own_rows, back_target, back_sems):
        value = self.settle(self.sum_ref[...], rows, self.settle_in, self.settle_out)
        self.stage[rows] = value
        if self.gather:
            whole, sems = self.whole_ref, self.send_sems
            whole[own_rows] = value
            for part in range(PARTS):
                columns = pl.ds(part * self.columns, self.columns)
                send(
                    self.stage.at[rows, columns],
                    whole.at[own_rows, columns],
                    sems.at[3],
                    back_sems.at[index - (PARTS - 1) + part],
                    back_target,
                ).start()
            send(self.stage.at[rows], whole.at[own_rows], sems.at[5], self.whole_sems.at[which], self.sibling).start()

    def back(self, index, which, base, reached, more, back_sems, target):
        for part in range(PARTS):
            own = self.piece(base, index, part)
            held = self.whole_ref.at[own]

            @pl.when((index >= 0) & (index < self.pieces) & reached & (index % PARTS == part))
            def _():
                drain(held, back_sems.at[index])

                @pl.when(more)
                def _():
                    send(held, held, self.send_sems.at[4], back_sems.at[index], target).start()

                if part == PARTS - 1:
                    rows = self.whole_ref.at[own[0]]
                    send(rows, rows, self.send_sems.at[5], self.whole_sems.at[which], self.sibling).start()

    def step(self, j):
        _, c, _ = place()
        sems = self.send_sems
        self.chain(
            j - SKEW * c, 1, self.up_base, c == 0, c == 3, self.in_up, self.acc_up, self.up_sems, sems.at[1],
            self.above, self.below, self.back_down,
        )
        self.chain(
            j - SKEW * (3 - c), 0, self.down_base, c == 3, c == 0, self.in_down, self.acc_down, self.down_sems,
            sems.at[2], self.below, self.above, self.back_up,
        )
        if self.gather:
            self.back(j - SKEW * (6 - c), 1, self.up_base, self.high, self.low, self.back_down, self.below)
            self.back(j - SKEW * (3 + c), 0, self.down_base, self.low, self.high, self.back_up, self.above)

    def end(self):
        d, c, t = place()
        sems, whole, stage = self.send_sems, self.whole_ref, self.stage
        drain(self.sib, sems.at[0])

        @pl.when(self.high)
        def _():
            drain(self.acc_up, sems.at[1])

        @pl.when(self.low)
        def _():
            drain(self.acc_down, sems.at[2])

        if self.gather:
            block = self.block
            up_rows, down_rows, other_up, other_down = [
                pl.ds(pl.multiple_of(base, block), block)
                for base in (self.up_base, self.down_base, (3 - t) * block, (1 - t) * block)
            ]

            @pl.when(jnp.logical_not(self.middle))
            def _():
                drain(stage, sems.at[3])

            @pl.when(self.middle)
            def _():
                drain(whole.at[up_rows], sems.at[4])
                drain(whole.at[down_rows], sems.at[4])

            drain(whole.at[up_rows], sems.at[5])
            drain(whole.at[down_rows], sems.at[5])
            drain(whole.at[other_up], self.whole_sems.at[1])
            drain(whole.at[other_down], self.whole_sems.at[0])
            return
        keeps = ((c == 0) & (t == 0)) | ((c == 3) & (t == 1))
        gives = ((c == 0) & (t == 1)) | ((c == 3) & (t == 0))
        takes = ((c == 1) & (t == 1)) | ((c == 2) & (t == 0))
        inner = (d, jnp.where(c == 0, 1, 2), t)
        away = send(stage, whole, sems.at[3], self.whole_sems.at[0], inner)
        across = send(stage, whole, sems.at[5], self.whole_sems.at[1], self.sibling)
        hand_on = send(whole, whole, sems.at[5], self.whole_sems.at[1], self.sibling)

        @pl.when(keeps)
        def _():
            across.start()
            whole[...] = stage[...]
            across.wait_send()

        @pl.when(gives)
        def _():
            away.start()
            away.wait_send()

        @pl.when(takes)
        def _():
            away.wait_recv()
            hand_on.start()
            hand_on.wait_send()

        @pl.when(jnp.logical_not(keeps | takes))
        def _():
            across.wait_recv()


def line_kernel(prelude, lines, kinds, counts, paces, *refs):
    n_jobs = len(kinds)
    line_in = []
    if prelude:
        prelude_in, refs = take(refs, prelude[1])
    for i, (_, _, n_in, _) in enumerate(lines):
        partial_refs, refs = take(refs, 0 if prelude and i == 0 else 1)
        ins, refs = take(refs, n_in)
        line_in.append((partial_refs, ins))
    job_sources, refs = take(refs, n_jobs)
    if prelude:
        prelude_out, refs = take(refs, prelude[2])
    line_out = []
    for _, _, _, n_out in lines:
        outs, refs = take(refs, n_out)
        (whole_ref,), refs = take(refs, 1)
        line_out.append((outs, whole_ref))
    job_results, refs = take(refs, n_jobs)
    if prelude:
        made, refs = take(refs, 1)
        prelude_scratch, refs = take(refs, prelude[3])
        held, refs = take(refs, prelude[1])
        (load_sems,), refs = take(refs, 1)
        loads = start_loads(prelude_in, held, load_sems)
    built = []
    for i, (settle, gather, _, _) in enumerate(lines):
        scratch, refs = take(refs, Line.scratch_count)
        partial_refs, ins = line_in[i]
        outs, whole_ref = line_out[i]
        partial_ref = partial_refs[0] if partial_refs else made[0]
        built.append(Line(settle, gather, partial_ref, ins, outs, whole_ref, scratch))
    greet(*place(), any(kind.everyone for kind in kinds))
    jobs = make_jobs(kinds, counts, job_sources, job_results, refs)
    if not prelude:
        built[0].begin()
    for line in built[1:]:
        line.begin()
    for job in jobs:
        if not job.late:
            job.start()
    if prelude:
        for copy in loads:
            copy.wait()
        prelude[0](*held, made[0], *prelude_out, *prelude_scratch)
        built[0].begin()

    turns = max(line.turns for line in built)
    timed, rest = {}, []
    for job, (first_turn, gap) in zip(jobs, paces):
        for i, act in enumerate(job.steps()):
            turn = first_turn + i * gap
            if turn < turns:
                timed.setdefault(turn, []).append(act)
            else:
                rest.append(act)

    def step(j, carry):
        for turn, acts in timed.items():

            @pl.when(j == turn)
            def _():
                for act in acts:
                    act()

        for line in built:
            line.step(j)
        return carry

    lax.fori_loop(0, turns, step, 0)
    for job in jobs:
        if job.late:
            job.start(built[0].settle_out[0])
    for act in rest:
        act()
    for line in built:
        line.end()
    for job in jobs:
        job.finish()


def line_call(name, number, lines, jobs, prelude=None):
    vmem, hbm = pl.BlockSpec(memory_space=pltpu.VMEM), pl.BlockSpec(memory_space=pltpu.HBM)
    operands, shapes, scratch, facts, far = [], [], [], [], 0
    if prelude:
        kernel, prelude_in, prelude_out, prelude_scratch, made = prelude
        far = len(prelude_in)
        operands += prelude_in
        shapes += prelude_out
        scratch += [pltpu.VMEM(made, jnp.bfloat16)] + prelude_scratch + load_scratch(prelude_in)
    for settle, gather, partial_sum, settle_in, settle_out in lines:
        rows, width = made if partial_sum is None else partial_sum.shape
        block = rows // 4
        operands += ([] if partial_sum is None else [partial_sum]) + settle_in
        shapes += settle_out + [jax.ShapeDtypeStruct((rows if gather else block, width), jnp.bfloat16)]
        scratch += Line.scratch(block, width)
        facts.append((settle, gather, len(settle_in), len(settle_out)))
    sources, in_specs, out_shapes, out_specs, job_scratch, counts = job_specs(jobs)
    paces = [(tuple(job) + (0, 1))[2:4] for job in jobs]
    return pl.pallas_call(
        functools.partial(
            line_kernel,
            (kernel, len(prelude_in), len(prelude_out), len(prelude_scratch)) if prelude else None,
            facts,
            [job[0] for job in jobs],
            counts,
            paces,
        ),
        name=name,
        out_shape=tuple(shapes + out_shapes),
        in_specs=[hbm] * far + [vmem] * (len(operands) - far) + in_specs,
        out_specs=tuple([vmem] * len(shapes) + out_specs),
        scratch_shapes=scratch + job_scratch,
        compiler_params=pltpu.CompilerParams(
            collective_id=number, has_side_effects=True, vmem_limit_bytes=(58 if any(job[0] is Return for job in jobs) else 40) * 2**20
        ),
        cost_estimate=pl.CostEstimate(flops=10**9, bytes_accessed=100 * 10**6, transcendentals=0),
    )(*operands, *sources)


def load_scratch(operands):
    return [pltpu.VMEM(operand.shape, operand.dtype) for operand in operands] + [
        pltpu.SemaphoreType.DMA((len(operands),))
    ]


def start_loads(sources, held, sems):
    copies = [pltpu.make_async_copy(source, ref, sems.at[i]) for i, (source, ref) in enumerate(zip(sources, held))]
    for copy in copies:
        copy.start()
    return copies


def work_kernel(kernel, n_in, n_out, n_scratch, kinds, counts, *refs):
    far, refs = take(refs, n_in)
    sources, refs = take(refs, len(kinds))
    outs, refs = take(refs, n_out)
    results, refs = take(refs, len(kinds))
    scratch, refs = take(refs, n_scratch)
    ins, refs = take(refs, n_in)
    (load_sems,), refs = take(refs, 1)
    loads = start_loads(far, ins, load_sems)
    if kinds:
        greet(*place())
    jobs = make_jobs(kinds, counts, sources, results, refs)
    for job in jobs:
        job.start()
    for copy in loads:
        copy.wait()
    kernel(*ins, *outs, *scratch)
    for job in jobs:
        for act in job.steps():
            act()
    for job in jobs:
        job.finish()


def work_call(kernel, name, number, operands, outs, scratch, jobs):
    vmem, hbm = pl.BlockSpec(memory_space=pltpu.VMEM), pl.BlockSpec(memory_space=pltpu.HBM)
    sources, in_specs, out_shapes, out_specs, job_scratch, counts = job_specs(jobs)
    results = pl.pallas_call(
        functools.partial(
            work_kernel, kernel, len(operands), len(outs), len(scratch), [job[0] for job in jobs], counts
        ),
        name=name,
        out_shape=tuple(list(outs) + out_shapes),
        in_specs=[hbm] * len(operands) + in_specs,
        out_specs=tuple([vmem] * len(outs) + out_specs),
        scratch_shapes=list(scratch) + load_scratch(operands) + job_scratch,
        compiler_params=pltpu.CompilerParams(
            collective_id=number if jobs else None, has_side_effects=bool(jobs), vmem_limit_bytes=48 * 2**20
        ),
        cost_estimate=pl.CostEstimate(flops=10**10, bytes_accessed=50 * 10**6, transcendentals=0),
    )(*operands, *sources)
    return take(results, len(outs))


def settle_forward(total, rows, ins, outs):
    residual_ref, gain_ref = ins
    value = residual_ref[rows] + depth_scale * total
    outs[0][rows] = value
    inverse = lax.rsqrt(jnp.mean(value * value, axis=-1, keepdims=True) + eps_norm)
    return (value * inverse * gain_ref[...]).astype(jnp.bfloat16)


def settle_last(total, rows, ins, outs):
    return (ins[0][rows] + depth_scale * total).astype(jnp.bfloat16)


def settle_backward(total, rows, ins, outs, more=True):
    values_ref, grad_ref, gain_ref = ins
    gain_grad = outs[0]
    value = values_ref[rows]
    inverse = lax.rsqrt(jnp.mean(value * value, axis=-1, keepdims=True) + eps_norm)
    scaled = value * inverse
    contribution = jnp.sum(total * scaled, axis=0, keepdims=True)

    first = rows.start == 0

    @pl.when(first)
    def _():
        gain_grad[...] = contribution

    @pl.when(jnp.logical_not(first))
    def _():
        gain_grad[...] += contribution

    grad_scaled = total * gain_ref[...]
    grad = grad_ref[rows] + inverse * (
        grad_scaled - scaled * jnp.mean(grad_scaled * scaled, axis=-1, keepdims=True)
    )
    if not more:
        return grad.astype(jnp.bfloat16)
    outs[1][rows] = grad
    return (depth_scale * grad).astype(jnp.bfloat16)


class LineComm:
    def __init__(self):
        self.number = 0

    def next_number(self):
        self.number += 1
        return self.number

    def moves(self, *jobs, urgent=0):
        return jobs_call(self.next_number(), jobs, urgent)

    def own_rows(self, whole):
        block = whole.shape[0] // 4
        _, c, t = place()
        return lax.dynamic_slice_in_dim(whole, (jnp.where(c >= 2, 2, 0) + t) * block, block, 0)

    def forward(self, partial_sum, residual, gain, jobs, prelude=None):
        outs = line_call(
            "forward_line",
            self.next_number(),
            [(settle_forward, True, partial_sum, [residual, gain], [jax.ShapeDtypeStruct(residual.shape, jnp.float32)])],
            jobs,
            prelude,
        )
        made, (value, normed, *moved) = take(outs, len(prelude[2]) if prelude else 0)
        return value, normed, moved, made

    def last(self, partial_sum, residual, jobs):
        output, *moved = line_call(
            "last_line", self.next_number(), [(settle_last, False, partial_sum, [residual], [])], jobs
        )
        return output, moved

    def backward(self, partial_sum, values, grad_rows, gain, jobs, last=None):
        lines = [
            (
                settle_backward,
                True,
                partial_sum,
                [values, grad_rows, gain],
                [jax.ShapeDtypeStruct(gain.shape, jnp.float32), jax.ShapeDtypeStruct(values.shape, jnp.float32)],
            )
        ]
        if last:
            lines.append((settle_last, False, last[0], [last[1]], []))
        gain_grad, grad, gathered, *moved = line_call("backward_line", self.next_number(), lines, jobs)
        if last:
            return grad, gain_grad, gathered, moved[1:], moved[0]
        return grad, gain_grad, gathered, moved, None

    def backward_last(self, partial_sum, values, grad_rows, gain, jobs, gain_grads):
        gain_grad, own, *moved, gain_blocks = line_call(
            "backward_last_line",
            self.next_number(),
            [
                (
                    functools.partial(settle_backward, more=False),
                    False,
                    partial_sum,
                    [values, grad_rows, gain],
                    [jax.ShapeDtypeStruct(gain.shape, jnp.float32)],
                )
            ],
            jobs + [(GainScatter, gain_grads)],
        )
        return own, jnp.sum(gain_blocks, axis=0)[: 1 + gain_grads.shape[0], : gain.shape[1] // 16], moved

    def return_grads(self, full):
        return full.reshape(16, -1, full.shape[1])


class PlainComm:
    def moves(self, *jobs, urgent=0):
        moved = []
        for kind, source, *_ in jobs:
            if kind is Collect:
                moved.append(lax.all_gather(source, "ctx", axis=0, tiled=True))
                continue
            if kind is Return:
                source = reduce_grads(source, lax.axis_size("ctx"))
                moved.append(lax.all_to_all(source, "ctx", 0, 0, tiled=False))
                continue
            some = issubclass(kind, Exchange)
            if some:
                first, last = kind.rows(source)
                source = source[:, first:last]
            blocks = source if kind is Spread else lax.all_to_all(source, "ctx", 0, 0, tiled=False)
            moved.append(blocks if some else lax.all_gather(blocks, "dp", axis=0, tiled=True))
        return tuple(moved)

    def own_rows(self, whole):
        _, c, t = place()
        share = whole.shape[0] // (lax.axis_size("ctx") * lax.axis_size("tensor"))
        return lax.dynamic_slice_in_dim(whole, (c * lax.axis_size("tensor") + t) * share, share, 0)

    def forward(self, partial_sum, residual, gain, jobs, prelude=None):
        value = residual + depth_scale * scatter_rows(partial_sum)
        return value, gather_rows((rms_parts(value)[0] * gain).astype(jnp.bfloat16)), self.moves(*jobs), ()

    def deliver(self, rows):
        return lax.all_gather(rows.astype(jnp.bfloat16), "tensor", axis=0, tiled=True)

    def last(self, partial_sum, residual, jobs):
        return self.deliver(residual + depth_scale * scatter_rows(partial_sum)), self.moves(*jobs)

    def backward(self, partial_sum, values, grad_rows, gain, jobs, last=None):
        gain_grad, from_norm = norm_backward(values, gain, scatter_rows(partial_sum))
        grad = grad_rows + from_norm
        gathered = gather_rows((depth_scale * grad).astype(jnp.bfloat16))
        output = self.last(*last, [])[0] if last else None
        return grad, gain_grad, gathered, self.moves(*jobs), output

    def backward_last(self, partial_sum, values, grad_rows, gain, jobs, gain_grads):
        gain_grad, from_norm = norm_backward(values, gain, scatter_rows(partial_sum))
        sums = jnp.concatenate([gain_grad, gain_grads], axis=0)
        sums = lax.psum(lax.psum_scatter(sums, ("dp", "ctx"), scatter_dimension=1, tiled=True), "tensor")
        return self.deliver(grad_rows + from_norm), sums, self.moves(*jobs)

    def return_grads(self, full):
        return full


def swap_halves(values):
    lane = lax.broadcasted_iota(jnp.int32, values.shape, 1)
    half = HEAD_DIM // 2
    width = values.shape[1]
    return jnp.where(lane % HEAD_DIM < half, pltpu.roll(values, width - half, 1), pltpu.roll(values, half, 1))


def head_scores(query, key, bias):
    return times_transposed(query, key) * score_scale + bias


def attend_kernel(heads, normed_ref, weight_ref, cosine_ref, sine_ref, bias_ref, partial_ref, mixed_ref, attended_ref, total_ref, wide):
    width = heads * HEAD_DIM
    lead = wide.shape[1] - width
    cosine, sine = cosine_ref[...], sine_ref[...]
    columns = mixed_ref.shape[1]
    normed = normed_ref[...]
    for first in range(0, columns, 2 * LANES):
        block = times(normed, weight_ref[:, first : first + 2 * LANES])
        for part in range(2):
            start = first + part * LANES
            tile = block[:, part * LANES : (part + 1) * LANES]
            if start < 2 * width:
                tile = tile * cosine + swap_halves(tile) * sine
            mixed_ref[:, start : start + LANES] = tile.astype(jnp.bfloat16)
    wide[:, :lead] = jnp.zeros((wide.shape[0], lead), jnp.bfloat16)
    for head in range(heads):
        low = head * HEAD_DIM
        query = mixed_ref[:, low : low + HEAD_DIM]
        key = mixed_ref[:, width + low : width + low + HEAD_DIM]
        value = mixed_ref[:, 2 * width + low : 2 * width + low + HEAD_DIM]
        scores = head_scores(query, key, bias_ref[...])
        top = jnp.max(scores, axis=-1, keepdims=True)
        terms = jnp.exp(scores - top)
        total = jnp.sum(terms, axis=-1, keepdims=True)
        probs = (terms / total).astype(jnp.bfloat16)
        wide[:, lead + low : lead + low + HEAD_DIM] = times(probs, value).astype(jnp.bfloat16)
        total_ref[:, head : head + 1] = top + jnp.log(total)
    attended_ref[...] = wide[:, lead:]
    attended = wide[...]
    for first in range(0, partial_ref.shape[1], 3 * LANES):
        partial_ref[:, first : first + 3 * LANES] = times_transposed(
            attended, weight_ref[first : first + 3 * LANES, 3 * width - lead :]
        ).astype(jnp.bfloat16)


def norm_attend_kernel(
    heads, inputs_ref, gain_ref, weight_ref, cosine_ref, sine_ref, bias_ref, partial_ref, mixed_ref, attended_ref, total_ref, normed_ref, wide
):
    rows = 128
    for first in range(0, inputs_ref.shape[0], rows):
        values = inputs_ref[first : first + rows].astype(jnp.float32)
        normed_ref[first : first + rows] = (rms_parts(values)[0] * gain_ref[...]).astype(jnp.bfloat16)
    attend_kernel(
        heads, normed_ref, weight_ref, cosine_ref, sine_ref, bias_ref, partial_ref, mixed_ref, attended_ref, total_ref, wide
    )


def attend_back_kernel(
    heads, grad_ref, weight_ref, mixed_ref, total_ref, cosine_ref, sine_ref, bias_ref, normed_ref, attended_ref, partial_ref, sums_ref, wide, turned, all_ref
):
    width = heads * HEAD_DIM
    lead = wide.shape[1] - width
    wide[...] = times(grad_ref[...], weight_ref[:, 3 * width - lead :]).astype(jnp.bfloat16)
    all_ref[:, 3 * width :] = jnp.zeros((all_ref.shape[0], all_ref.shape[1] - 3 * width), jnp.bfloat16)
    for head in range(heads):
        low = head * HEAD_DIM
        query = mixed_ref[:, low : low + HEAD_DIM]
        key = mixed_ref[:, width + low : width + low + HEAD_DIM]
        value = mixed_ref[:, 2 * width + low : 2 * width + low + HEAD_DIM]
        grad_out = wide[:, lead + low : lead + low + HEAD_DIM]
        scores = head_scores(query, key, bias_ref[...])
        probs = jnp.exp(scores - total_ref[:, head : head + 1])
        grad_probs = times_transposed(grad_out, value)
        delta = jnp.sum(probs * grad_probs, axis=-1, keepdims=True)
        grad_scores = (probs * (grad_probs - delta) * score_scale).astype(jnp.bfloat16)
        turned[:, low : low + HEAD_DIM] = times(grad_scores, key)
        turned[:, width + low : width + low + HEAD_DIM] = outer_rows(grad_scores, query)
        all_ref[:, 2 * width + low : 2 * width + low + HEAD_DIM] = outer_rows(
            probs.astype(jnp.bfloat16), grad_out
        ).astype(jnp.bfloat16)
    cosine, sine = cosine_ref[...], sine_ref[...]
    for start in range(0, 2 * width, LANES):
        tile = turned[:, start : start + LANES]
        all_ref[:, start : start + LANES] = (tile * cosine - swap_halves(tile) * sine).astype(jnp.bfloat16)
    grad_all = all_ref[...]
    for first in range(0, partial_ref.shape[1], 3 * LANES):
        partial_ref[:, first : first + 3 * LANES] = times_transposed(
            grad_all, weight_ref[first : first + 3 * LANES, : grad_all.shape[1]]
        ).astype(jnp.bfloat16)
    for first in range(0, sums_ref.shape[0], 2 * LANES):
        tile = slice(first, first + 2 * LANES)
        sums_ref[tile, : 3 * width] = outer_rows(normed_ref[:, tile], all_ref[:, : 3 * width]).astype(jnp.bfloat16)
        sums_ref[tile, 3 * width :] = outer_rows(grad_ref[:, tile], attended_ref[...]).astype(jnp.bfloat16)


def local_call(kernel, name, operands, outs, scratch, flops):
    vmem = pl.BlockSpec(memory_space=pltpu.VMEM)
    return pl.pallas_call(
        kernel,
        name=name,
        out_shape=tuple(outs),
        in_specs=[vmem] * len(operands),
        out_specs=tuple([vmem] * len(outs)),
        scratch_shapes=scratch,
        compiler_params=pltpu.CompilerParams(vmem_limit_bytes=48 * 2**20),
        cost_estimate=pl.CostEstimate(flops=flops, bytes_accessed=20 * 10**6, transcendentals=0),
    )(*operands)


def outer_kernel(*refs):
    out_ref, first = refs[-1], 0
    for left, right in zip(refs[:-1:2], refs[1:-1:2]):
        last = first + right.shape[1]
        out_ref[:, first:last] = outer_rows(left[...], right[...]).astype(out_ref.dtype)
        first = last


def outer_sums(*pairs):
    rows, width = pairs[0][0].shape
    columns = sum(right.shape[1] for _, right in pairs)
    tile = 256
    specs, operands = [], []
    for left, right in pairs:
        specs += [
            pl.BlockSpec((rows, tile), lambda i: (0, i)),
            pl.BlockSpec(right.shape, lambda i: (0, 0)),
        ]
        operands += [left, right]
    return pl.pallas_call(
        outer_kernel,
        name="outer_sums",
        grid=(width // tile,),
        out_shape=jax.ShapeDtypeStruct((width, columns), jnp.bfloat16),
        in_specs=specs,
        out_specs=pl.BlockSpec((tile, columns), lambda i: (i, 0)),
        compiler_params=pltpu.CompilerParams(vmem_limit_bytes=40 * 2**20),
        cost_estimate=pl.CostEstimate(
            flops=2 * rows * width * columns, bytes_accessed=2 * (rows + width) * columns, transcendentals=0
        ),
    )(*operands)


def attention_forward(query, key, value, bias):
    scores = jnp.einsum("qhd,khd->hqk", query, key, preferred_element_type=jnp.float32) * score_scale
    scores = scores + bias[None]
    top = jnp.max(scores, axis=-1, keepdims=True)
    terms = jnp.exp(scores - top)
    probs = terms / jnp.sum(terms, axis=-1, keepdims=True)
    attended = jnp.einsum(
        "hqk,khd->qhd", probs.astype(jnp.bfloat16), value, preferred_element_type=jnp.float32
    )
    return attended, probs


def attention_backward(query, key, value, probs, grad_out):
    grad_probs = jnp.einsum("qhd,khd->hqk", grad_out, value, preferred_element_type=jnp.float32)
    delta = jnp.sum(probs * grad_probs, axis=-1, keepdims=True)
    grad_scores = (probs * (grad_probs - delta) * score_scale).astype(jnp.bfloat16)
    grad_query = jnp.einsum("hqk,khd->qhd", grad_scores, key, preferred_element_type=jnp.float32)
    grad_key = jnp.einsum("hqk,qhd->khd", grad_scores, query, preferred_element_type=jnp.float32)
    grad_value = jnp.einsum(
        "hqk,qhd->khd", probs.astype(jnp.bfloat16), grad_out, preferred_element_type=jnp.float32
    )
    return grad_query, grad_key, grad_value


def lane_tables(tables):
    cosine, sine_table = tables[0][:, 0], tables[1][:, 0]
    return (
        jnp.concatenate([cosine] * (LANES // cosine.shape[1]), axis=1),
        jnp.concatenate([-sine_table, sine_table] * (LANES // HEAD_DIM), axis=1),
    )


def forward_attention(normed, weight, plan, bias, tables, kernels, gain):
    width = plan.head_width
    rows = normed.shape[0]
    if kernels:
        columns = (3 * width + LANES - 1) // LANES * LANES
        wide = (width + LANES - 1) // LANES * LANES
        sized = jax.ShapeDtypeStruct
        first = gain is not None
        return (
            functools.partial(norm_attend_kernel if first else attend_kernel, plan.head_count),
            [normed] + ([gain] if first else []) + [weight, *lane_tables(tables), bias],
            [
                sized((rows, columns), jnp.bfloat16),
                sized((rows, width), jnp.bfloat16),
                sized((rows, LANES), jnp.float32),
            ]
            + ([sized(normed.shape, jnp.bfloat16)] if first else []),
            [pltpu.VMEM((rows, wide), jnp.bfloat16)],
            (rows, weight.shape[0]),
        ), None
    head_shape = (rows, plan.head_count, HEAD_DIM)
    mixed = times(normed, weight[:, : 3 * width])
    query = rotate(mixed[:, :width].reshape(head_shape), tables, 1.0).astype(jnp.bfloat16)
    key = rotate(mixed[:, width : 2 * width].reshape(head_shape), tables, 1.0).astype(jnp.bfloat16)
    value = mixed[:, 2 * width :].reshape(head_shape).astype(jnp.bfloat16)
    attended, probs = attention_forward(query, key, value, bias)
    attended = attended.reshape(rows, width).astype(jnp.bfloat16)
    partial_sum = times_transposed(attended, weight[:, 3 * width :]).astype(jnp.bfloat16)
    return partial_sum, (normed, query, key, value, probs, attended)


def feed_kernel(normed_ref, gate_ref, up_ref, down_ref, partial_ref, gating_ref, upward_ref, activated_ref):
    normed = normed_ref[...]
    for first in range(0, gating_ref.shape[1], 2 * LANES):
        tile = slice(first, first + 2 * LANES)
        gating, upward = times(normed, gate_ref[:, tile]), times(normed, up_ref[:, tile])
        gating_ref[:, tile] = gating
        upward_ref[:, tile] = upward
        activated_ref[:, tile] = (jax.nn.silu(gating) * upward).astype(jnp.bfloat16)
    activated = activated_ref[...]
    for first in range(0, partial_ref.shape[1], 2 * LANES):
        tile = slice(first, first + 2 * LANES)
        partial_ref[:, tile] = times_transposed(activated, down_ref[tile, :]).astype(jnp.bfloat16)


def feed_prelude(normed, weights):
    rows, width = normed.shape
    units = weights[0].shape[1]
    sized = jax.ShapeDtypeStruct
    wide = sized((rows, units), jnp.float32)
    return (feed_kernel, [normed, *weights], [wide, wide, sized((rows, units), jnp.bfloat16)], [], (rows, width))


def forward_feed(normed, weights):
    gate_weight, up_weight, down_weight = weights
    gating, upward = times(normed, gate_weight), times(normed, up_weight)
    activated = (jax.nn.silu(gating) * upward).astype(jnp.bfloat16)
    partial_sum = times_transposed(activated, down_weight).astype(jnp.bfloat16)
    return partial_sum, (normed, gating, upward, activated)


def feed_back_kernel(
    grad_ref, normed_ref, gate_ref, up_ref, down_ref, gating_ref, upward_ref, activated_ref, partial_ref, sums_ref, gate_grad, up_grad
):
    units = gating_ref.shape[1]
    grad = grad_ref[...]
    for first in range(0, units, 2 * LANES):
        tile = slice(first, first + 2 * LANES)
        grad_act = times(grad, down_ref[:, tile])
        gating, upward = gating_ref[:, tile], upward_ref[:, tile]
        sigmoid_gate = jax.nn.sigmoid(gating)
        gate_grad[:, tile] = (grad_act * upward * sigmoid_gate * (1.0 + gating * (1.0 - sigmoid_gate))).astype(
            jnp.bfloat16
        )
        up_grad[:, tile] = (grad_act * gating * sigmoid_gate).astype(jnp.bfloat16)
    for first in range(0, partial_ref.shape[1], 2 * LANES):
        tile = slice(first, first + 2 * LANES)
        partial_ref[:, tile] = (
            times_transposed(gate_grad[...], gate_ref[tile, :]) + times_transposed(up_grad[...], up_ref[tile, :])
        ).astype(jnp.bfloat16)
        normed = normed_ref[:, tile]
        sums_ref[tile, :units] = outer_rows(normed, gate_grad[...]).astype(jnp.bfloat16)
        sums_ref[tile, units : 2 * units] = outer_rows(normed, up_grad[...]).astype(jnp.bfloat16)
        sums_ref[tile, 2 * units :] = outer_rows(grad_ref[:, tile], activated_ref[...]).astype(jnp.bfloat16)


def backward_feed_beside(down_grad, weights, record, number, jobs):
    normed, gating, upward, activated = record
    rows, width = down_grad.shape
    units = gating.shape[1]
    sized = jax.ShapeDtypeStruct
    return work_call(
        feed_back_kernel,
        "feed_back",
        number,
        [down_grad, normed, *weights, gating, upward, activated],
        [sized((rows, width), jnp.bfloat16), sized((width, 3 * units), jnp.bfloat16)],
        [pltpu.VMEM((rows, units), jnp.bfloat16)] * 2,
        jobs,
    )


def backward_feed(down_grad, weights, record):
    gate_weight, up_weight, down_weight = weights
    normed, gating, upward, activated = record
    grad_act = times(down_grad, down_weight)
    sigmoid_gate = jax.nn.sigmoid(gating)
    grad_gating = (grad_act * upward * sigmoid_gate * (1.0 + gating * (1.0 - sigmoid_gate))).astype(jnp.bfloat16)
    grad_upward = (grad_act * gating * sigmoid_gate).astype(jnp.bfloat16)
    partial_sum = (times_transposed(grad_gating, gate_weight) + times_transposed(grad_upward, up_weight)).astype(
        jnp.bfloat16
    )
    return partial_sum, ((normed, grad_gating), (normed, grad_upward), (down_grad, activated))


def backward_attention(branch_grad, weight, record, plan, bias, tables, kernels, jobs):
    width = plan.head_width
    rows = branch_grad.shape[0]
    if kernels:
        normed, mixed, attended, total = record
        wide = (width + LANES - 1) // LANES * LANES
        sized = jax.ShapeDtypeStruct
        (partial_sum, sums), moved = work_call(
            functools.partial(attend_back_kernel, plan.head_count),
            "attend_back",
            kernels.next_number() if jobs else None,
            [branch_grad, weight, mixed, total, *lane_tables(tables), bias, normed, attended],
            [sized((rows, weight.shape[0]), jnp.bfloat16), sized((weight.shape[0], 4 * width), jnp.bfloat16)],
            [
                pltpu.VMEM((rows, wide), jnp.bfloat16),
                pltpu.VMEM((rows, 2 * width), jnp.float32),
                pltpu.VMEM(mixed.shape, jnp.bfloat16),
            ],
            jobs,
        )
        return partial_sum, sums, moved
    normed, query, key, value, probs, attended = record
    grad_mixed = times(branch_grad, weight[:, 3 * width :]).astype(jnp.bfloat16)
    grad_query, grad_key, grad_value = attention_backward(
        query, key, value, probs, grad_mixed.reshape(query.shape)
    )
    grad_all = jnp.concatenate(
        [
            rotate(grad_query, tables, -1.0).reshape(rows, width),
            rotate(grad_key, tables, -1.0).reshape(rows, width),
            grad_value.reshape(rows, width),
        ],
        axis=1,
    ).astype(jnp.bfloat16)
    partial_sum = times_transposed(grad_all, weight[:, : 3 * width]).astype(jnp.bfloat16)
    return partial_sum, outer_sums((normed, grad_all), (branch_grad, attended)), None


def body(
    inputs,
    cotangent,
    lengths,
    dealing,
    span_table,
    prenorm_gain,
    query_weight,
    keys_weight,
    values_weight,
    project_weight,
    postnorm_gain,
    gating_weight,
    upward_weight,
    downward_weight,
):
    n_dp, n_ctx, n_ten = lax.axis_size("dp"), lax.axis_size("ctx"), lax.axis_size("tensor")
    plan = Plan(n_dp, n_ctx, query_weight.shape[2], gating_weight.shape[2])
    own_rows = inputs.shape[0]
    half_span = own_rows // 2
    share = own_rows // n_ten
    group_index = lax.axis_index("dp")
    core = lax.axis_index("tensor")
    seq_count = lengths.shape[0] // n_dp
    starts, seq_lens = group_layout(lengths, dealing, group_index, seq_count)
    span_row = lax.dynamic_index_in_dim(span_table, group_index, 0, keepdims=False)
    facts = slot_facts(slots_for(own_rows * n_ctx, span_row, half_span), starts, seq_lens)
    tables = rope_tables(facts[2], HEAD_DIM // 2)
    bias = jnp.where(allowed(facts, facts), 0.0, masked_score)

    kernels = (n_dp, n_ctx, n_ten) == (4, 4, 2)
    comm = LineComm() if kernels else PlainComm()
    head_cuts = [cut * HEAD_DIM for cut in plan.head_cuts]

    attention_stack = [query_weight, keys_weight, values_weight, project_weight.transpose(0, 2, 1)]
    feed_stack = [gating_weight, upward_weight, downward_weight.transpose(0, 2, 1)]

    def windows(layer):
        attention = [cut_windows(weight[layer], head_cuts, plan.head_width) for weight in attention_stack]
        feed = [cut_windows(weight[layer], plan.unit_cuts, plan.unit_width) for weight in feed_stack]
        return [jnp.concatenate(attention, axis=2)] + feed

    def joined(blocks):
        return blocks.reshape(-1, blocks.shape[-1])

    if kernels:
        later_windows, moved = start_call(
            plan, comm.next_number(), attention_stack + feed_stack, prenorm_gain, postnorm_gain, inputs
        )
        inputs_whole, attention_blocks, gain_blocks, gate, up, down = moved
        gains = gain_blocks[:, : 2 * LAYERS, : prenorm_gain.shape[1]].transpose(1, 0, 2).reshape(2 * LAYERS, -1)
    else:
        attention_windows, gate, up, down = windows(0)
        later_windows = [windows(layer) for layer in range(1, LAYERS)]
        attention_blocks, inputs_whole, gate, up, down = comm.moves(
            (Fetch, attention_windows), (Collect, inputs), (Fetch, gate), (Exchange, up), (Exchange, down)
        )
        gains = lax.all_gather(
            jnp.concatenate([prenorm_gain, postnorm_gain], axis=0), ("dp", "ctx"), axis=1, tiled=True
        )
    gains = gains.astype(jnp.float32)
    front = [gains[layer : layer + 1] for layer in range(LAYERS)]
    behind = [gains[LAYERS + layer : LAYERS + layer + 1] for layer in range(LAYERS)]
    attention_weights, feed_weights = [None] * LAYERS, [None] * LAYERS
    attention_records, feed_records, middles = [None] * LAYERS, [None] * LAYERS, [None] * LAYERS
    starts_of = [None] * LAYERS

    attention_weights[0] = joined(attention_blocks)
    residual = comm.own_rows(inputs_whole).astype(jnp.float32)
    normed = inputs_whole
    if not kernels:
        normed = (rms_parts(inputs_whole.astype(jnp.float32))[0] * front[0]).astype(jnp.bfloat16)
    for layer in range(LAYERS):
        starts_of[layer] = residual
        more = layer + 1 < LAYERS
        partial_sum, attention_records[layer] = forward_attention(
            normed, attention_weights[layer], plan, bias, tables, kernels, None if layer else front[0]
        )
        prelude = partial_sum if kernels else None
        jobs = [(Spread, up, 6, 2), (Spread, down, 14, 2)]
        if more:
            next_windows = later_windows[layer]
            jobs += [(Exchange, next_windows[0]), (Exchange, next_windows[1])]
        else:
            jobs += [(Collect, cotangent, 5, 4)]
        hidden, normed_two, (up, down, *moved), made = comm.forward(
            None if kernels else partial_sum, residual, behind[layer], jobs, prelude
        )
        if kernels:
            attention_records[layer] = (made[3] if layer == 0 else normed, *made[:3])
        normed = normed_two
        feed_weights[layer] = [joined(blocks) for blocks in (gate, up, down)]
        middles[layer] = hidden
        if more:
            jobs = [
                (Spread, moved[0], 8, 3),
                (Spread, moved[1], 19, 2),
                (Exchange, next_windows[2]),
                (Exchange, next_windows[3]),
            ]
            prelude, partial_sum = None, None
            if kernels:
                prelude = feed_prelude(normed, feed_weights[layer])
            else:
                partial_sum, feed_records[layer] = forward_feed(normed, feed_weights[layer])
            residual, normed_next, moved, made = comm.forward(partial_sum, hidden, front[layer + 1], jobs, prelude)
            if kernels:
                feed_records[layer] = (normed, *made)
            normed = normed_next
            attention_weights[layer + 1] = joined(moved[0])
            gate, up, down = moved[1:]
        else:
            last_sum, feed_records[layer] = forward_feed(normed, feed_weights[layer])
            cotangent_whole = moved[0]

    grad_rows = comm.own_rows(cotangent_whole).astype(jnp.float32)
    down_grad = (depth_scale * cotangent_whole.astype(jnp.float32)).astype(jnp.bfloat16)
    gain_fronts, gain_backs, attention_parts, feed_parts = [[None] * LAYERS for _ in range(4)]
    for layer in reversed(range(LAYERS)):
        more, last_layer = layer > 0, layer + 1 == LAYERS
        own_width = query_weight.shape[1]
        cut_feed, cut_attention = own_width * 5 // 9 // 16 * 16, own_width // 2 // 16 * 16
        cut_last = own_width // 3 // 16 * 16

        def two(whole, cut):
            if last_layer:
                return [], []
            return [(exchange_rows(0, cut), whole)], [(exchange_rows(cut, own_width), whole)]

        beside, in_line = two(feed_parts[layer + 1] if not last_layer else None, cut_feed)
        if kernels and beside:
            (partial_sum, sums), upper = backward_feed_beside(
                down_grad, feed_weights[layer], feed_records[layer], comm.next_number(), beside
            )
        else:
            partial_sum, pairs = backward_feed(down_grad, feed_weights[layer], feed_records[layer])
            sums = outer_sums(*pairs)
            upper = comm.moves(*beside) if beside else ()
        partial_sum, sums = lax.optimization_barrier((partial_sum, sums))
        feed_sums = reduce_grads(sums, n_ctx)
        grad_rows, gain_backs[layer], branch_grad, lower, last_output = comm.backward(
            partial_sum,
            middles[layer],
            grad_rows,
            behind[layer],
            in_line,
            None if more else (last_sum, middles[LAYERS - 1]),
        )
        if beside:
            feed_parts[layer + 1] = [upper[0], lower[0]]
        if not more:
            output = last_output
        beside, in_line = two(attention_parts[layer + 1] if not last_layer else None, cut_attention)
        partial_sum, sums, upper = backward_attention(
            branch_grad,
            attention_weights[layer],
            attention_records[layer],
            plan,
            bias,
            tables,
            comm if kernels else None,
            beside,
        )
        if beside and upper is None:
            upper = comm.moves(*beside)
        partial_sum, sums = lax.optimization_barrier((partial_sum, sums))
        attention_sums = reduce_grads(sums, n_ctx)
        if more:
            grad_rows, gain_fronts[layer], down_grad, lower, _ = comm.backward(
                partial_sum, starts_of[layer], grad_rows, front[layer], in_line
            )
        else:
            others = jnp.concatenate(gain_fronts[1:] + gain_backs, axis=0)
            grad_inputs, gain_sums, (feed_moved, *lower) = comm.backward_last(
                partial_sum,
                starts_of[layer],
                grad_rows,
                front[layer],
                [(exchange_rows(0, cut_last), feed_sums)] + in_line,
                others,
            )
        if beside:
            attention_parts[layer + 1] = [upper[0], lower[0]]
        feed_parts[layer], attention_parts[layer] = feed_sums, attention_sums
    attention_parts[0], grad_inputs = lax.optimization_barrier((attention_parts[0], grad_inputs))
    feed_rest, attention_moved = comm.moves(
        (exchange_rows(cut_last, own_width), feed_parts[0]), (Exchange, attention_parts[0])
    )
    feed_parts[0], attention_parts[0] = [feed_moved, feed_rest], [attention_moved]
    grad_inputs = grad_inputs.astype(jnp.float32)

    if kernels:
        joins = join_layers(plan, attention_parts, feed_parts)
    else:

        def spread(parts, index, width, cuts):
            return jnp.stack(
                [
                    join_windows(jnp.concatenate(part, axis=1)[:, :, index * width : (index + 1) * width], cuts)
                    for part in parts
                ]
            ).astype(jnp.float32)

        joins = [spread(attention_parts, i, plan.head_width, head_cuts) for i in range(4)]
        joins += [spread(feed_parts, i, plan.unit_width, plan.unit_cuts) for i in range(3)]
    query_out, keys_out, values_out, project_out, gating_out, upward_out, downward_out = joins
    return (
        output,
        grad_inputs,
        gain_sums[:LAYERS],
        query_out,
        keys_out,
        values_out,
        project_out.transpose(0, 2, 1),
        gain_sums[LAYERS:],
        gating_out,
        upward_out,
        downward_out.transpose(0, 2, 1),
    )


def solution(mesh):
    rows = P(("dp", "ctx"), None)
    gain = P(None, ("dp", "ctx"))
    wide = P(None, ("dp", "ctx"), "tensor")
    tall = P(None, "tensor", ("dp", "ctx"))
    weights = (gain, wide, wide, wide, tall, gain, wide, wide, tall)
    return jax.shard_map(
        body,
        mesh=mesh,
        in_specs=(rows, rows, P(), P(), P()) + weights,
        out_specs=(rows, rows) + weights,
        check_vma=False,
    )
```

```python
import math

import functools

import jax
import jax.numpy as jnp
from jax import lax
from jax.experimental import pallas as pl
from jax.experimental.pallas import tpu as pltpu
from jax.sharding import PartitionSpec as P

MESH = pl.DeviceIdType.MESH

HEAD_DIM = 64
LAYERS = 2
BLOCK = 128
LANES = 128

eps_norm = 1e-05
depth_scale = 1.4 / math.sqrt(40.0)
rope_base = 10000.0
masked_score = -1e30
score_scale = 1.0 / math.sqrt(HEAD_DIM)


def times(left, right):
    return jnp.dot(left, right, preferred_element_type=jnp.float32)


def times_transposed(left, right):
    return lax.dot_general(
        left, right, (((1,), (1,)), ((), ())), preferred_element_type=jnp.float32
    )


def outer_rows(left, right):
    return lax.dot_general(
        left, right, (((0,), (0,)), ((), ())), preferred_element_type=jnp.float32
    )


def rms_parts(values):
    inverse = lax.rsqrt(jnp.mean(values * values, axis=-1, keepdims=True) + eps_norm)
    return (values * inverse, inverse)


def norm_backward(values, gain, grad_normed):
    scaled, inverse = rms_parts(values)
    gain_grad = jnp.sum(grad_normed * scaled, axis=0, keepdims=True)
    grad_scaled = grad_normed * gain
    return (
        gain_grad,
        inverse * (grad_scaled - scaled * jnp.mean(grad_scaled * scaled, axis=-1, keepdims=True)),
    )


def rope_tables(position, half_dim):
    inverse = rope_base ** (-jnp.arange(half_dim).astype(jnp.float32) / half_dim)
    angles = position.astype(jnp.float32)[:, None] * inverse[None, :]
    return (jnp.cos(angles)[:, None, :], jnp.sin(angles)[:, None, :])


def rotate(values, tables, direction):
    cosine, sine_table = tables
    half_dim = values.shape[-1] // 2
    front_half = values[..., :half_dim]
    back_half = values[..., half_dim:]
    return jnp.concatenate(
        [
            front_half * cosine - direction * back_half * sine_table,
            back_half * cosine + direction * front_half * sine_table,
        ],
        axis=-1,
    )


def group_layout(lengths, dealing, group_index, seq_count):
    chosen = lax.dynamic_slice_in_dim(dealing, group_index * seq_count, seq_count)
    matches = chosen[:, None] == jnp.arange(lengths.shape[0], dtype=jnp.int32)[None, :]
    seq_lens = jnp.sum(jnp.where(matches, lengths[None, :], 0), axis=1)
    padded = (seq_lens + BLOCK - 1) // BLOCK * BLOCK
    starts = jnp.cumsum(padded) - padded
    return (starts, seq_lens)


def slots_for(number, span_row, half_span):
    rows = jnp.arange(number, dtype=jnp.int32)
    matches = (rows // half_span)[:, None] == jnp.arange(span_row.shape[0], dtype=jnp.int32)[None, :]
    span_of = jnp.sum(jnp.where(matches, span_row[None, :], 0), axis=1)
    return span_of * half_span + rows % half_span


def slot_facts(slots, starts, seq_lens):
    member = jnp.sum((slots[:, None] >= starts[None, :]).astype(jnp.int32), axis=1) - 1
    matches = member[:, None] == jnp.arange(starts.shape[0], dtype=jnp.int32)[None, :]
    anchor = jnp.sum(jnp.where(matches, starts[None, :], 0), axis=1)
    extent = jnp.sum(jnp.where(matches, seq_lens[None, :], 0), axis=1)
    position = slots - anchor
    return (slots, member, position, (position < extent).astype(jnp.int32))


def allowed(query_facts, key_facts):
    query_slot, query_member, query_position, query_valid = query_facts
    key_slot, key_member, key_position, key_valid = key_facts
    same_slot = query_slot[:, None] == key_slot[None, :]
    both_valid = (query_valid[:, None] == 1) & (key_valid[None, :] == 1)
    causal = (query_member[:, None] == key_member[None, :]) & (
        key_position[None, :] <= query_position[:, None]
    )
    return same_slot | both_valid & causal


class Plan:
    def __init__(self, n_dp, n_ctx, columns, hidden):
        self.n_dp, self.n_ctx = n_dp, n_ctx
        heads = columns // HEAD_DIM
        self.head_cuts = [i * heads // n_ctx for i in range(n_ctx + 1)]
        self.head_count = max(b - a for a, b in zip(self.head_cuts, self.head_cuts[1:]))
        self.head_width = self.head_count * HEAD_DIM
        self.unit_cuts = [i * hidden // n_ctx for i in range(n_ctx + 1)]
        units = max(b - a for a, b in zip(self.unit_cuts, self.unit_cuts[1:]))
        self.unit_width = (units + LANES - 1) // LANES * LANES


def cut_windows(weight, cuts, width):
    pieces = []
    for first, last in zip(cuts, cuts[1:]):
        pieces.append(jnp.pad(weight[:, first:last], ((0, 0), (0, width - (last - first)))))
    return jnp.stack(pieces)


def join_windows(windows, cuts):
    return jnp.concatenate(
        [windows[i, :, : last - first] for i, (first, last) in enumerate(zip(cuts, cuts[1:]))], axis=1
    )


def cut_attention(plan, sources, out):
    for i, ref in enumerate(sources):
        for j, (first, last) in enumerate(zip(plan.head_cuts, plan.head_cuts[1:])):
            start, count = i * plan.head_width, (last - first) * HEAD_DIM
            out[j, :, start : start + count] = ref[:, first * HEAD_DIM : last * HEAD_DIM]
            if count < plan.head_width:
                out[j, :, start + count : start + plan.head_width] = jnp.zeros(
                    (ref.shape[0], plan.head_width - count), ref.dtype
                )


def cut_feed(plan, ref, out):
    for j, (first, last) in enumerate(zip(plan.unit_cuts, plan.unit_cuts[1:])):
        out[j, :, : last - first] = ref[:, first:last]
        out[j, :, last - first :] = jnp.zeros((ref.shape[0], plan.unit_width - (last - first)), ref.dtype)


def start_kernel(plan, *refs):
    weights, refs = take(refs, 7)
    (front_ref, behind_ref, inputs_ref), refs = take(refs, 3)
    cuts, refs = take(refs, 4 * (LAYERS - 1))
    results, refs = take(refs, 6)
    raw, refs = take(refs, 7 * LAYERS)
    (load_sems,), refs = take(refs, 1)
    own_cuts, refs = take(refs, 4)
    (gain_blocks,), refs = take(refs, 1)
    loads = start_loads([ref.at[layer] for layer in range(LAYERS) for ref in weights], raw, load_sems)
    greet(*place())
    kinds = (Collect, Fetch, Fetch, Fetch, Exchange, Exchange)
    sources = [inputs_ref, own_cuts[0], gain_blocks, *own_cuts[1:]]
    jobs = make_jobs(kinds, [0] * 6, sources, results, refs)
    jobs[0].start()
    for copy in loads[:4]:
        copy.wait()
    cut_attention(plan, raw[:4], own_cuts[0])
    jobs[1].start()
    gain_blocks[...] = jnp.zeros(gain_blocks.shape, gain_blocks.dtype)
    for j in range(gain_blocks.shape[0]):
        gain_blocks[j, 0:LAYERS, : front_ref.shape[1]] = front_ref[...]
        gain_blocks[j, LAYERS : 2 * LAYERS, : front_ref.shape[1]] = behind_ref[...]
    jobs[2].start()
    for i in range(3):
        loads[4 + i].wait()
        cut_feed(plan, raw[4 + i], own_cuts[1 + i])
    steps = [job.steps() for job in jobs]
    for i in range(3):
        steps[0][i]()
        steps[1][i]()
    for i in range(3):
        steps[2][i]()
    jobs[3].start()
    for act in steps[3][:3]:
        act()
    jobs[4].start()
    jobs[5].start()
    for act in steps[1][3:] + steps[2][3:]:
        act()
    for layer in range(1, LAYERS):
        for copy in loads[7 * layer : 7 * layer + 7]:
            copy.wait()
        layer_raw, layer_cuts = raw[7 * layer : 7 * layer + 7], cuts[4 * (layer - 1) : 4 * layer]
        cut_attention(plan, layer_raw[:4], layer_cuts[0])
        for i in range(3):
            cut_feed(plan, layer_raw[4 + i], layer_cuts[1 + i])
    for act in steps[3][3:]:
        act()
    for job in jobs:
        job.finish()


def start_call(plan, number, weights, front, behind, inputs):
    vmem, hbm = pl.BlockSpec(memory_space=pltpu.VMEM), pl.BlockSpec(memory_space=pltpu.HBM)
    rows = weights[0].shape[1]
    sized = jax.ShapeDtypeStruct
    windows = [(plan.n_ctx, rows, width) for width in [4 * plan.head_width] + [plan.unit_width] * 3]
    gain_shape = (plan.n_ctx, 16, (rows + LANES - 1) // LANES * LANES)
    own = [sized(shape, jnp.bfloat16) for shape in windows]
    gain_source = sized(gain_shape, jnp.bfloat16)
    kinds = (Collect, Fetch, Fetch, Fetch, Exchange, Exchange)
    sources = (inputs, own[0], gain_source, *own[1:])
    results = [kind.result(source) for kind, source in zip(kinds, sources)]
    dma = pltpu.SemaphoreType.DMA
    outs = pl.pallas_call(
        functools.partial(start_kernel, plan),
        name="start",
        out_shape=tuple(own * (LAYERS - 1) + results),
        in_specs=[hbm] * 7 + [vmem] * 2 + [hbm],
        out_specs=tuple([vmem] * 4 * (LAYERS - 1) + [hbm] * 6),
        scratch_shapes=[pltpu.VMEM(weight.shape[1:], weight.dtype) for _ in range(LAYERS) for weight in weights]
        + [dma((7 * LAYERS,))]
        + [pltpu.VMEM(shape, jnp.bfloat16) for shape in windows + [gain_shape]]
        + [dma((kind.semaphores,)) for kind in kinds],
        compiler_params=pltpu.CompilerParams(
            collective_id=number, has_side_effects=True, vmem_limit_bytes=START_MIB * 2**20
        ),
        cost_estimate=pl.CostEstimate(flops=10**9, bytes_accessed=100 * 10**6, transcendentals=0),
    )(*weights, front, behind, inputs)
    cuts, results = take(outs, 4 * (LAYERS - 1))
    return [cuts[4 * i : 4 * i + 4] for i in range(LAYERS - 1)], results


def join_kernel(plan, places, count, *refs):
    sources, outs = refs[:count], refs[count:]
    for source, (layer, top, weights) in zip(sources, places):
        rows, start = source.shape[1], 0
        for i in weights:
            cuts = [cut * HEAD_DIM for cut in plan.head_cuts] if i < 4 else plan.unit_cuts
            for j, (first, last) in enumerate(zip(cuts, cuts[1:])):
                outs[i][layer, top : top + rows, first:last] = source[j, :, start : start + last - first].astype(
                    jnp.float32
                )
            start += plan.head_width if i < 4 else plan.unit_width


def join_layers(plan, attention_parts, feed_parts):
    sources, places = [], []
    for parts_of, weights in ((attention_parts, (0, 1, 2, 3)), (feed_parts, (4, 5, 6))):
        for layer, parts in enumerate(parts_of):
            top = 0
            for part in parts:
                sources.append(part)
                places.append((layer, top, weights))
                top += part.shape[1]
    outs = [
        jax.ShapeDtypeStruct((LAYERS, top, width), jnp.float32)
        for width in [plan.head_cuts[-1] * HEAD_DIM] * 4 + [plan.unit_cuts[-1]] * 3
    ]
    return local_call(functools.partial(join_kernel, plan, places, len(sources)), "join_layers", sources, outs, [], 0)


def reduce_grads(full, n_ctx):
    own = lax.psum_scatter(full, "dp", scatter_dimension=0, tiled=True)
    return own.reshape(n_ctx, -1, own.shape[-1])


def gather_rows(piece):
    return lax.all_gather(piece, ("ctx", "tensor"), axis=0, tiled=True)


def scatter_rows(partial_sum):
    return lax.psum_scatter(
        partial_sum.astype(jnp.bfloat16), ("ctx", "tensor"), scatter_dimension=0, tiled=True
    ).astype(jnp.float32)


SLOT = 16
START_MIB = 60
PARTS = 1
SKEW = 3


def place():
    return lax.axis_index("dp"), lax.axis_index("ctx"), lax.axis_index("tensor")


def slot_rows(base, index):
    return pl.ds(pl.multiple_of(base + index * SLOT, SLOT), SLOT)


def send(src, dst, send_sem, recv_sem, target):
    return pltpu.make_async_remote_copy(
        src_ref=src, dst_ref=dst, send_sem=send_sem, recv_sem=recv_sem, device_id=target, device_id_type=MESH
    )


def greet(d, c, t, everyone=False):
    barrier = pltpu.get_barrier_semaphore()
    others = [(d, c, 1 - t), (d, c ^ 1, t), (d, c ^ 2, t), (d, c ^ 3, t), (d ^ 1, c, t), (d ^ 2, c, t)]
    if everyone:
        others = others[:1] + [(d ^ (k // 4), c ^ (k % 4), t) for k in range(1, 16)]
    for other in others:
        pl.semaphore_signal(barrier, inc=1, device_id=other, device_id_type=MESH)
    pl.semaphore_wait(barrier, len(others))


class Job:
    everyone = False
    near = False

    @staticmethod
    def scratch(source):
        return []

    def steps(self):
        return []


class Exchange(Job):
    semaphores = 7
    span = None

    @classmethod
    def rows(cls, source):
        return cls.span or (0, source.shape[1])

    @classmethod
    def result(cls, source):
        first, last = cls.rows(source)
        return jax.ShapeDtypeStruct((source.shape[0], last - first, source.shape[2]), source.dtype)

    def __init__(self, source, result, sems):
        d, c, t = place()
        first, last = self.rows(source)
        rows = pl.ds(first, last - first)
        self.own = pltpu.make_async_copy(source.at[c, rows], result.at[c], sems.at[6])
        self.copies = [
            send(source.at[c ^ k, rows], result.at[c], sems.at[k - 1], sems.at[k + 2], (d, c ^ k, t))
            for k in (3, 2, 1)
        ]

    def start(self):
        for copy in self.copies:
            copy.start()
        self.own.start()

    def finish(self):
        for copy in self.copies:
            copy.wait()
        self.own.wait()


def exchange_rows(first, last):
    class Some(Exchange):
        span = (first, last)

    return Some


class Collect(Job):
    semaphores = 25

    @staticmethod
    def result(source):
        return jax.ShapeDtypeStruct((4 * source.shape[0], source.shape[1]), source.dtype)

    def __init__(self, source, result, sems):
        d, c, t = place()
        block = source.shape[0]
        half = block // 2

        def piece(chip):
            return result.at[pl.ds(pl.multiple_of(chip * block + t * half, half), half)]

        self.own = pltpu.make_async_copy(source, result.at[pl.ds(pl.multiple_of(c * block, block), block)], sems.at[24])
        mine = source.at[pl.ds(pl.multiple_of(t * half, half), half)]
        self.hops, self.onward = {}, {}
        for way, more, target in ((0, c < 3, (d, c + 1, t)), (1, c > 0, (d, c - 1, t))):
            for hop in range(4):
                chip = c - hop if way == 0 else c + hop
                held = (chip >= 0) if way == 0 else (chip <= 3)
                if hop < 3:
                    self.hops[way, hop] = (
                        more & held,
                        send(
                            piece(chip) if hop else mine,
                            piece(chip),
                            sems.at[way * 12 + hop],
                            sems.at[way * 12 + 3 + hop],
                            target,
                        ),
                    )
                if hop:
                    self.onward[way, hop] = (
                        held,
                        send(
                            piece(chip),
                            piece(chip),
                            sems.at[way * 12 + 5 + hop],
                            sems.at[way * 12 + 8 + hop],
                            (d, c, 1 - t),
                        ),
                    )

    def start(self):
        for way in range(2):
            go, copy = self.hops[way, 0]
            pl.when(go)(copy.start)
        self.own.start()

    def steps(self):
        return [functools.partial(self.pass_on, hop) for hop in range(1, 4)]

    def pass_on(self, hop):
        for way in range(2):
            held, onward = self.onward[way, hop]
            arrived = self.hops[way, hop - 1][1]

            @pl.when(held)
            def _():
                arrived.wait_recv()
                onward.start()

            if hop < 3:
                go, copy = self.hops[way, hop]
                pl.when(go)(copy.start)

    def finish(self):
        for go, copy in self.hops.values():
            pl.when(go)(copy.wait_send)
        for held, onward in self.onward.values():
            pl.when(held)(onward.wait)
        self.own.wait()


class GainScatter(Job):
    semaphores = 33
    everyone = True
    near = True

    @staticmethod
    def blocks(source):
        return (16, 8, (source.shape[1] // 16 + LANES - 1) // LANES * LANES)

    @staticmethod
    def result(source):
        return jax.ShapeDtypeStruct(GainScatter.blocks(source), source.dtype)

    @staticmethod
    def scratch(source):
        return [pltpu.VMEM(GainScatter.blocks(source), source.dtype)] * 3

    def __init__(self, source, result, sems, own, other, cut):
        d, c, t = place()
        mine = d * 4 + c
        self.source, self.terms, self.cut = source, (own, other), cut
        self.across = send(own, other, sems.at[31], sems.at[32], (d, c, 1 - t))
        self.own = pltpu.make_async_copy(cut.at[mine], result.at[mine], sems.at[0])
        self.copies = []
        for k in range(1, 16):
            g, i = d ^ (k // 4), c ^ (k % 4)
            self.copies.append(send(cut.at[g * 4 + i], result.at[mine], sems.at[k], sems.at[k + 15], (g, i, t)))

    def start(self):
        own, other = self.terms
        own[...] = jnp.zeros(own.shape, own.dtype)
        part = self.source.shape[1] // 16
        for i in range(16):
            own[i, : self.source.shape[0], :part] = self.source[:, i * part : (i + 1) * part]
        self.across.start()
        self.across.wait()
        self.cut[...] = own[...] + other[...]
        for copy in self.copies:
            copy.start()
        self.own.start()

    def finish(self):
        for copy in self.copies:
            copy.wait()
        self.own.wait()


class Return(Job):
    semaphores = 31
    near = True
    order = (0, 2, 1, 3)

    @staticmethod
    def result(source):
        return jax.ShapeDtypeStruct((4,) + source.shape[1:], source.dtype)

    @staticmethod
    def scratch(source):
        four = pltpu.VMEM((4,) + source.shape[1:], source.dtype)
        return [four] * 5

    def __init__(self, source, result, sems, corner_in, x_in, y_in, passed, total):
        d, c, t = place()
        self.corner_in, self.sides_in, self.passed, self.total = corner_in, (x_in, y_in), passed, total
        self.terms, self.corners, self.sides, self.line = [], [], [], [None]
        for k in range(4):
            i = c ^ k
            way = k // 2
            self.terms.append([source.at[(d ^ flip) * 4 + i] for flip in (0, 1, 2)])
            self.corners.append(
                send(source.at[(d ^ 3) * 4 + i], corner_in.at[k], sems.at[k], sems.at[4 + k], (d ^ (1 + way), c, t))
            )
            self.sides.append(
                [
                    send(
                        passed.at[k] if side != way else source.at[(d ^ (1 + side)) * 4 + i],
                        self.sides_in[side].at[k],
                        sems.at[8 + 2 * k + side],
                        sems.at[16 + 2 * k + side],
                        (d ^ (1 + side), c, t),
                    )
                    for side in range(2)
                ]
            )
            if k:
                self.line.append(send(total.at[k], result.at[c], sems.at[23 + k], sems.at[26 + k], (d, i, t)))
        self.own = pltpu.make_async_copy(total.at[0], result.at[c], sems.at[30])

    def start(self):
        for k in self.order:
            self.corners[k].start()
        for k in self.order:
            self.sides[k][k // 2].start()

    def steps(self):
        return [functools.partial(self.pass_term, k) for k in self.order] + [
            functools.partial(self.add_up, k) for k in (3, 2, 1, 0)
        ]

    def pass_term(self, k):
        side = 1 - k // 2
        self.corners[k].wait_recv()
        self.passed[k] = (self.terms[k][1 + side][...].astype(jnp.float32) + self.corner_in[k].astype(jnp.float32)).astype(
            self.passed.dtype
        )
        self.sides[k][side].start()

    def add_up(self, k):
        for side in range(2):
            self.sides[k][side].wait_recv()
        self.total[k] = (
            self.terms[k][0][...].astype(jnp.float32)
            + self.sides_in[0][k].astype(jnp.float32)
            + self.sides_in[1][k].astype(jnp.float32)
        ).astype(self.total.dtype)
        if k:
            self.line[k].start()
        else:
            self.own.start()

    def finish(self):
        for k in range(4):
            self.corners[k].wait_send()
            for copy in self.sides[k]:
                copy.wait_send()
            if k:
                self.line[k].wait()
        self.own.wait()


class Fetch(Job):
    semaphores = 31

    @staticmethod
    def result(source):
        return jax.ShapeDtypeStruct((16,) + source.shape[1:], source.dtype)

    order = (0, 2, 1, 3)

    def __init__(self, source, result, sems):
        d, c, t = place()
        self.own = pltpu.make_async_copy(source.at[c], result.at[d * 4 + c], sems.at[0])
        self.line = [None]
        for k in range(1, 4):
            self.line.append(
                send(source.at[c ^ k], result.at[d * 4 + c], sems.at[k], sems.at[k + 3], (d, c ^ k, t))
            )
        self.link(source, result, sems)

    def link(self, source, result, sems):
        d, c, t = place()
        self.side, self.corners = [], []
        for k in range(4):
            held = result.at[d * 4 + (c ^ k)]
            ready = held if self.line[k] is not None else source.at[c ^ k]
            self.side.append(
                [
                    send(ready, held, sems.at[7 + 2 * k + way], sems.at[15 + 2 * k + way], (d ^ (1 + way), c, t))
                    for way in range(2)
                ]
            )
            way = k // 2
            passed = result.at[(d ^ (1 + way)) * 4 + (c ^ k)]
            self.corners.append(
                send(passed, passed, sems.at[23 + k], sems.at[27 + k], (d ^ (2 - way), c, t))
            )

    def start(self):
        self.own.start()
        for k in (3, 2, 1):
            self.line[k].start()
        for copy in self.side[0]:
            copy.start()

    def steps(self):
        return [functools.partial(self.pass_sides, k) for k in (1, 2, 3)] + self.corner_steps()

    def corner_steps(self):
        return [functools.partial(self.pass_corner, k) for k in self.order]

    def pass_sides(self, k):
        self.line[k].wait_recv()
        for copy in self.side[k]:
            copy.start()

    def pass_corner(self, k):
        self.side[k][k // 2].wait_recv()
        self.corners[k].start()

    def finish(self):
        for k in range(4):
            self.side[k][1 - k // 2].wait_recv()
        for k in range(4):
            self.corners[k].wait()
            for copy in self.side[k]:
                copy.wait_send()
            if self.line[k] is not None:
                self.line[k].wait_send()
        self.own.wait()


class Spread(Fetch):
    @staticmethod
    def result(source):
        return jax.ShapeDtypeStruct((16,) + source.shape[1:], source.dtype)

    def __init__(self, source, result, sems):
        d, c, t = place()
        self.own = pltpu.make_async_copy(source, result.at[pl.ds(d * 4, 4)], sems.at[0])
        self.line = [None] * 4
        self.link(source, result, sems)

    def start(self):
        for k in self.order:
            for copy in self.side[k]:
                copy.start()
        self.own.start()

    def steps(self):
        return self.corner_steps()


def take(refs, count):
    return refs[:count], refs[count:]


def make_jobs(kinds, scratch_counts, sources, results, refs):
    jobs = []
    for kind, count, source, result in zip(kinds, scratch_counts, sources, results):
        (sems, *scratch), refs = take(refs, 1 + count)
        jobs.append(kind(source, result, sems, *scratch))
    return jobs


def job_specs(jobs):
    vmem, hbm = pl.BlockSpec(memory_space=pltpu.VMEM), pl.BlockSpec(memory_space=pltpu.HBM)
    sources = [job[1] for job in jobs]
    in_specs = [vmem if job[0].near else hbm for job in jobs]
    out_shapes = [job[0].result(job[1]) for job in jobs]
    scratch, counts = [], []
    for kind, source, *_ in jobs:
        extra = kind.scratch(source)
        scratch += [pltpu.SemaphoreType.DMA((kind.semaphores,))] + extra
        counts.append(len(extra))
    return sources, in_specs, out_shapes, [hbm] * len(jobs), scratch, counts


def jobs_kernel(kinds, counts, urgent, *refs):
    n = len(kinds)
    greet(*place(), any(kind.everyone for kind in kinds))
    jobs = make_jobs(kinds, counts, refs[:n], refs[n : 2 * n], refs[2 * n :])
    first, later = jobs[:urgent], jobs[urgent:]
    for job in first:
        job.start()
    rest = []
    for job in first:
        todo = job.steps()
        for act in todo[:3]:
            act()
        rest += todo[3:]
    for job in later:
        job.start()
    for act in rest:
        act()
    for job in later:
        for act in job.steps():
            act()
    for job in jobs:
        job.finish()


def jobs_call(number, jobs, urgent):
    sources, in_specs, out_shapes, out_specs, scratch, counts = job_specs(jobs)
    return pl.pallas_call(
        functools.partial(jobs_kernel, [job[0] for job in jobs], counts, urgent),
        name="moves",
        out_shape=tuple(out_shapes),
        in_specs=in_specs,
        out_specs=tuple(out_specs),
        scratch_shapes=scratch,
        compiler_params=pltpu.CompilerParams(
            collective_id=number, has_side_effects=True, vmem_limit_bytes=60 * 2**20
        ),
        cost_estimate=pl.CostEstimate(flops=10**9, bytes_accessed=100 * 10**6, transcendentals=0),
    )(*sources)


def drain(ref, sem):
    pltpu.make_async_copy(ref, ref, sem).wait()


class Line:
    scratch_count = 14

    @staticmethod
    def scratch(block, width):
        pieces = block // SLOT * PARTS
        piece = pltpu.VMEM((block, width), jnp.bfloat16)
        dma = pltpu.SemaphoreType.DMA
        return (
            [piece] * 4
            + [pltpu.VMEM((2, block, width), jnp.bfloat16), piece, dma((6,)), dma((2, 2))]
            + [dma((pieces,))] * 4
            + [dma((2,)), pltpu.VMEM((SLOT, width), jnp.float32)]
        )

    def __init__(self, settle, gather, partial_ref, settle_in, settle_out, whole_ref, scratch):
        self.settle, self.gather = settle, gather
        self.partial_ref, self.settle_in, self.settle_out, self.whole_ref = partial_ref, settle_in, settle_out, whole_ref
        (
            self.acc_up,
            self.acc_down,
            self.in_up,
            self.in_down,
            self.sib,
            self.stage,
            self.send_sems,
            self.sib_sems,
            self.up_sems,
            self.down_sems,
            self.back_up,
            self.back_down,
            self.whole_sems,
            self.sum_ref,
        ) = scratch
        d, c, t = place()
        self.block = self.acc_up.shape[0]
        self.pieces = self.block // SLOT * PARTS
        self.columns = self.acc_up.shape[1] // PARTS
        self.turns = self.pieces + SKEW * (6 if gather else 3)
        self.sibling, self.above, self.below = (d, c, 1 - t), (d, c + 1, t), (d, c - 1, t)
        self.down_base, self.up_base = t * self.block, (2 + t) * self.block
        self.low, self.high = c > 0, c < 3
        self.middle = self.low & self.high

    def begin(self):
        _, _, t = place()
        half = self.block // 2
        for part in range(2):
            for which, base in ((0, (1 - t) * self.block), (1, (3 - t) * self.block)):
                rows = pl.ds(pl.multiple_of(base + part * half, half), half)
                send(
                    self.partial_ref.at[rows],
                    self.sib.at[which, pl.ds(part * half, half)],
                    self.send_sems.at[0],
                    self.sib_sems.at[which, part],
                    self.sibling,
                ).start()

        @pl.when(self.middle)
        def _():
            for ref in self.settle_out:
                ref[...] = jnp.zeros(ref.shape, ref.dtype)

    def piece(self, base, index, part):
        return (slot_rows(base, index // PARTS), pl.ds(part * self.columns, self.columns))

    def chain(self, index, which, base, first, last, into, acc, recv_sems, send_sem, target, back_target, back_sems):
        half = self.block // 2
        pieces = self.pieces

        @pl.when((index >= 0) & (index < pieces) & (index % (pieces // 2) == 0))
        def _():
            drain(self.sib.at[which, pl.ds(0, half)], self.sib_sems.at[which, index // (pieces // 2)])

        for part in range(PARTS):
            here = self.piece(0, index, part)
            own = self.piece(base, index, part)

            @pl.when((index >= 0) & (index < pieces) & (index % PARTS == part))
            def _():
                def term():
                    return self.partial_ref[own].astype(jnp.float32) + self.sib[(which, *here)].astype(jnp.float32)

                def pass_on(total):
                    acc[here] = total.astype(jnp.bfloat16)
                    send(acc.at[here], into.at[here], send_sem, recv_sems.at[index], target).start()

                @pl.when(first)
                def _():
                    pass_on(term())

                @pl.when(jnp.logical_not(first))
                def _():
                    drain(into.at[here], recv_sems.at[index])

                @pl.when(self.middle)
                def _():
                    pass_on(term() + into[here].astype(jnp.float32))

                @pl.when(last)
                def _():
                    self.sum_ref[:, here[1]] = term() + into[here].astype(jnp.float32)
                    if part == PARTS - 1:
                        self.settled(index, which, here[0], own[0], back_target, back_sems)

    def settled(self, index, which, rows, own_rows, back_target, back_sems):
        value = self.settle(self.sum_ref[...], rows, self.settle_in, self.settle_out)
        self.stage[rows] = value
        if self.gather:
            whole, sems = self.whole_ref, self.send_sems
            whole[own_rows] = value
            for part in range(PARTS):
                columns = pl.ds(part * self.columns, self.columns)
                send(
                    self.stage.at[rows, columns],
                    whole.at[own_rows, columns],
                    sems.at[3],
                    back_sems.at[index - (PARTS - 1) + part],
                    back_target,
                ).start()
            send(self.stage.at[rows], whole.at[own_rows], sems.at[5], self.whole_sems.at[which], self.sibling).start()

    def back(self, index, which, base, reached, more, back_sems, target):
        for part in range(PARTS):
            own = self.piece(base, index, part)
            held = self.whole_ref.at[own]

            @pl.when((index >= 0) & (index < self.pieces) & reached & (index % PARTS == part))
            def _():
                drain(held, back_sems.at[index])

                @pl.when(more)
                def _():
                    send(held, held, self.send_sems.at[4], back_sems.at[index], target).start()

                if part == PARTS - 1:
                    rows = self.whole_ref.at[own[0]]
                    send(rows, rows, self.send_sems.at[5], self.whole_sems.at[which], self.sibling).start()

    def step(self, j):
        _, c, _ = place()
        sems = self.send_sems
        self.chain(
            j - SKEW * c, 1, self.up_base, c == 0, c == 3, self.in_up, self.acc_up, self.up_sems, sems.at[1],
            self.above, self.below, self.back_down,
        )
        self.chain(
            j - SKEW * (3 - c), 0, self.down_base, c == 3, c == 0, self.in_down, self.acc_down, self.down_sems,
            sems.at[2], self.below, self.above, self.back_up,
        )
        if self.gather:
            self.back(j - SKEW * (6 - c), 1, self.up_base, self.high, self.low, self.back_down, self.below)
            self.back(j - SKEW * (3 + c), 0, self.down_base, self.low, self.high, self.back_up, self.above)

    def end(self):
        d, c, t = place()
        sems, whole, stage = self.send_sems, self.whole_ref, self.stage
        drain(self.sib, sems.at[0])

        @pl.when(self.high)
        def _():
            drain(self.acc_up, sems.at[1])

        @pl.when(self.low)
        def _():
            drain(self.acc_down, sems.at[2])

        if self.gather:
            block = self.block
            up_rows, down_rows, other_up, other_down = [
                pl.ds(pl.multiple_of(base, block), block)
                for base in (self.up_base, self.down_base, (3 - t) * block, (1 - t) * block)
            ]

            @pl.when(jnp.logical_not(self.middle))
            def _():
                drain(stage, sems.at[3])

            @pl.when(self.middle)
            def _():
                drain(whole.at[up_rows], sems.at[4])
                drain(whole.at[down_rows], sems.at[4])

            drain(whole.at[up_rows], sems.at[5])
            drain(whole.at[down_rows], sems.at[5])
            drain(whole.at[other_up], self.whole_sems.at[1])
            drain(whole.at[other_down], self.whole_sems.at[0])
            return
        keeps = ((c == 0) & (t == 0)) | ((c == 3) & (t == 1))
        gives = ((c == 0) & (t == 1)) | ((c == 3) & (t == 0))
        takes = ((c == 1) & (t == 1)) | ((c == 2) & (t == 0))
        inner = (d, jnp.where(c == 0, 1, 2), t)
        away = send(stage, whole, sems.at[3], self.whole_sems.at[0], inner)
        across = send(stage, whole, sems.at[5], self.whole_sems.at[1], self.sibling)
        hand_on = send(whole, whole, sems.at[5], self.whole_sems.at[1], self.sibling)

        @pl.when(keeps)
        def _():
            across.start()
            whole[...] = stage[...]
            across.wait_send()

        @pl.when(gives)
        def _():
            away.start()
            away.wait_send()

        @pl.when(takes)
        def _():
            away.wait_recv()
            hand_on.start()
            hand_on.wait_send()

        @pl.when(jnp.logical_not(keeps | takes))
        def _():
            across.wait_recv()


def line_kernel(prelude, lines, kinds, counts, paces, *refs):
    n_jobs = len(kinds)
    line_in = []
    if prelude:
        prelude_in, refs = take(refs, prelude[1])
    for i, (_, _, n_in, _) in enumerate(lines):
        partial_refs, refs = take(refs, 0 if prelude and i == 0 else 1)
        ins, refs = take(refs, n_in)
        line_in.append((partial_refs, ins))
    job_sources, refs = take(refs, n_jobs)
    if prelude:
        prelude_out, refs = take(refs, prelude[2])
    line_out = []
    for _, _, _, n_out in lines:
        outs, refs = take(refs, n_out)
        (whole_ref,), refs = take(refs, 1)
        line_out.append((outs, whole_ref))
    job_results, refs = take(refs, n_jobs)
    if prelude:
        made, refs = take(refs, 1)
        prelude_scratch, refs = take(refs, prelude[3])
        held, refs = take(refs, prelude[1])
        (load_sems,), refs = take(refs, 1)
        loads = start_loads(prelude_in, held, load_sems)
    built = []
    for i, (settle, gather, _, _) in enumerate(lines):
        scratch, refs = take(refs, Line.scratch_count)
        partial_refs, ins = line_in[i]
        outs, whole_ref = line_out[i]
        partial_ref = partial_refs[0] if partial_refs else made[0]
        built.append(Line(settle, gather, partial_ref, ins, outs, whole_ref, scratch))
    greet(*place(), any(kind.everyone for kind in kinds))
    jobs = make_jobs(kinds, counts, job_sources, job_results, refs)
    if not prelude:
        built[0].begin()
    for line in built[1:]:
        line.begin()
    for job in jobs:
        job.start()
    if prelude:
        for copy in loads:
            copy.wait()
        prelude[0](*held, made[0], *prelude_out, *prelude_scratch)
        built[0].begin()

    turns = max(line.turns for line in built)
    timed, rest = {}, []
    for job, (first_turn, gap) in zip(jobs, paces):
        for i, act in enumerate(job.steps()):
            turn = first_turn + i * gap
            if turn < turns:
                timed.setdefault(turn, []).append(act)
            else:
                rest.append(act)

    def step(j, carry):
        for turn, acts in timed.items():

            @pl.when(j == turn)
            def _():
                for act in acts:
                    act()

        for line in built:
            line.step(j)
        return carry

    lax.fori_loop(0, turns, step, 0)
    for act in rest:
        act()
    for line in built:
        line.end()
    for job in jobs:
        job.finish()


def line_call(name, number, lines, jobs, prelude=None):
    vmem, hbm = pl.BlockSpec(memory_space=pltpu.VMEM), pl.BlockSpec(memory_space=pltpu.HBM)
    operands, shapes, scratch, facts, far = [], [], [], [], 0
    if prelude:
        kernel, prelude_in, prelude_out, prelude_scratch, made = prelude
        far = len(prelude_in)
        operands += prelude_in
        shapes += prelude_out
        scratch += [pltpu.VMEM(made, jnp.bfloat16)] + prelude_scratch + load_scratch(prelude_in)
    for settle, gather, partial_sum, settle_in, settle_out in lines:
        rows, width = made if partial_sum is None else partial_sum.shape
        block = rows // 4
        operands += ([] if partial_sum is None else [partial_sum]) + settle_in
        shapes += settle_out + [jax.ShapeDtypeStruct((rows if gather else block, width), jnp.bfloat16)]
        scratch += Line.scratch(block, width)
        facts.append((settle, gather, len(settle_in), len(settle_out)))
    sources, in_specs, out_shapes, out_specs, job_scratch, counts = job_specs(jobs)
    paces = [(tuple(job) + (0, 1))[2:4] for job in jobs]
    return pl.pallas_call(
        functools.partial(
            line_kernel,
            (kernel, len(prelude_in), len(prelude_out), len(prelude_scratch)) if prelude else None,
            facts,
            [job[0] for job in jobs],
            counts,
            paces,
        ),
        name=name,
        out_shape=tuple(shapes + out_shapes),
        in_specs=[hbm] * far + [vmem] * (len(operands) - far) + in_specs,
        out_specs=tuple([vmem] * len(shapes) + out_specs),
        scratch_shapes=scratch + job_scratch,
        compiler_params=pltpu.CompilerParams(
            collective_id=number, has_side_effects=True, vmem_limit_bytes=(40 if jobs else 60) * 2**20
        ),
        cost_estimate=pl.CostEstimate(flops=10**9, bytes_accessed=100 * 10**6, transcendentals=0),
    )(*operands, *sources)


def load_scratch(operands):
    return [pltpu.VMEM(operand.shape, operand.dtype) for operand in operands] + [
        pltpu.SemaphoreType.DMA((len(operands),))
    ]


def start_loads(sources, held, sems):
    copies = [pltpu.make_async_copy(source, ref, sems.at[i]) for i, (source, ref) in enumerate(zip(sources, held))]
    for copy in copies:
        copy.start()
    return copies


def work_kernel(kernel, n_in, n_out, n_scratch, kinds, counts, *refs):
    far, refs = take(refs, n_in)
    sources, refs = take(refs, len(kinds))
    outs, refs = take(refs, n_out)
    results, refs = take(refs, len(kinds))
    scratch, refs = take(refs, n_scratch)
    ins, refs = take(refs, n_in)
    (load_sems,), refs = take(refs, 1)
    loads = start_loads(far, ins, load_sems)
    if kinds:
        greet(*place())
    jobs = make_jobs(kinds, counts, sources, results, refs)
    for job in jobs:
        job.start()
    for copy in loads:
        copy.wait()
    kernel(*ins, *outs, *scratch)
    for job in jobs:
        for act in job.steps():
            act()
    for job in jobs:
        job.finish()


def work_call(kernel, name, number, operands, outs, scratch, jobs):
    vmem, hbm = pl.BlockSpec(memory_space=pltpu.VMEM), pl.BlockSpec(memory_space=pltpu.HBM)
    sources, in_specs, out_shapes, out_specs, job_scratch, counts = job_specs(jobs)
    results = pl.pallas_call(
        functools.partial(
            work_kernel, kernel, len(operands), len(outs), len(scratch), [job[0] for job in jobs], counts
        ),
        name=name,
        out_shape=tuple(list(outs) + out_shapes),
        in_specs=[hbm] * len(operands) + in_specs,
        out_specs=tuple([vmem] * len(outs) + out_specs),
        scratch_shapes=list(scratch) + load_scratch(operands) + job_scratch,
        compiler_params=pltpu.CompilerParams(
            collective_id=number if jobs else None, has_side_effects=bool(jobs), vmem_limit_bytes=60 * 2**20
        ),
        cost_estimate=pl.CostEstimate(flops=10**10, bytes_accessed=50 * 10**6, transcendentals=0),
    )(*operands, *sources)
    return take(results, len(outs))


def settle_forward(total, rows, ins, outs):
    residual_ref, gain_ref = ins
    value = residual_ref[rows] + depth_scale * total
    outs[0][rows] = value
    inverse = lax.rsqrt(jnp.mean(value * value, axis=-1, keepdims=True) + eps_norm)
    return (value * inverse * gain_ref[...]).astype(jnp.bfloat16)


def settle_last(total, rows, ins, outs):
    return (ins[0][rows] + depth_scale * total).astype(jnp.bfloat16)


def settle_backward(total, rows, ins, outs, more=True):
    values_ref, grad_ref, gain_ref = ins
    gain_grad = outs[0]
    value = values_ref[rows]
    inverse = lax.rsqrt(jnp.mean(value * value, axis=-1, keepdims=True) + eps_norm)
    scaled = value * inverse
    contribution = jnp.sum(total * scaled, axis=0, keepdims=True)

    first = rows.start == 0

    @pl.when(first)
    def _():
        gain_grad[...] = contribution

    @pl.when(jnp.logical_not(first))
    def _():
        gain_grad[...] += contribution

    grad_scaled = total * gain_ref[...]
    grad = grad_ref[rows] + inverse * (
        grad_scaled - scaled * jnp.mean(grad_scaled * scaled, axis=-1, keepdims=True)
    )
    if not more:
        return grad.astype(jnp.bfloat16)
    outs[1][rows] = grad
    return (depth_scale * grad).astype(jnp.bfloat16)


class LineComm:
    def __init__(self):
        self.number = 0

    def next_number(self):
        self.number += 1
        return self.number

    def moves(self, *jobs, urgent=0):
        return jobs_call(self.next_number(), jobs, urgent)

    def own_rows(self, whole):
        block = whole.shape[0] // 4
        _, c, t = place()
        return lax.dynamic_slice_in_dim(whole, (jnp.where(c >= 2, 2, 0) + t) * block, block, 0)

    def forward(self, partial_sum, residual, gain, jobs, prelude=None):
        outs = line_call(
            "forward_line",
            self.next_number(),
            [(settle_forward, True, partial_sum, [residual, gain], [jax.ShapeDtypeStruct(residual.shape, jnp.float32)])],
            jobs,
            prelude,
        )
        made, (value, normed, *moved) = take(outs, len(prelude[2]) if prelude else 0)
        return value, normed, moved, made

    def last(self, partial_sum, residual, jobs):
        output, *moved = line_call(
            "last_line", self.next_number(), [(settle_last, False, partial_sum, [residual], [])], jobs
        )
        return output, moved

    def backward(self, partial_sum, values, grad_rows, gain, jobs, last=None):
        lines = [
            (
                settle_backward,
                True,
                partial_sum,
                [values, grad_rows, gain],
                [jax.ShapeDtypeStruct(gain.shape, jnp.float32), jax.ShapeDtypeStruct(values.shape, jnp.float32)],
            )
        ]
        if last:
            lines.append((settle_last, False, last[0], [last[1]], []))
        gain_grad, grad, gathered, *moved = line_call("backward_line", self.next_number(), lines, jobs)
        if last:
            return grad, gain_grad, gathered, moved[1:], moved[0]
        return grad, gain_grad, gathered, moved, None

    def backward_last(self, partial_sum, values, grad_rows, gain, jobs):
        gain_grad, own, *moved = line_call(
            "backward_last_line",
            self.next_number(),
            [
                (
                    functools.partial(settle_backward, more=False),
                    False,
                    partial_sum,
                    [values, grad_rows, gain],
                    [jax.ShapeDtypeStruct(gain.shape, jnp.float32)],
                )
            ],
            jobs,
        )
        return own, gain_grad, moved

    def sum_gains(self, gain_grads, jobs):
        gain_blocks, *moved = self.moves((GainScatter, gain_grads), *jobs)
        return jnp.sum(gain_blocks, axis=0)[: gain_grads.shape[0], : gain_grads.shape[1] // 16], moved

    def return_grads(self, full):
        return full.reshape(16, -1, full.shape[1])


class PlainComm:
    def moves(self, *jobs, urgent=0):
        moved = []
        for kind, source, *_ in jobs:
            if kind is Collect:
                moved.append(lax.all_gather(source, "ctx", axis=0, tiled=True))
                continue
            if kind is Return:
                source = reduce_grads(source, lax.axis_size("ctx"))
                moved.append(lax.all_to_all(source, "ctx", 0, 0, tiled=False))
                continue
            some = issubclass(kind, Exchange)
            if some:
                first, last = kind.rows(source)
                source = source[:, first:last]
            blocks = source if kind is Spread else lax.all_to_all(source, "ctx", 0, 0, tiled=False)
            moved.append(blocks if some else lax.all_gather(blocks, "dp", axis=0, tiled=True))
        return tuple(moved)

    def own_rows(self, whole):
        _, c, t = place()
        share = whole.shape[0] // (lax.axis_size("ctx") * lax.axis_size("tensor"))
        return lax.dynamic_slice_in_dim(whole, (c * lax.axis_size("tensor") + t) * share, share, 0)

    def forward(self, partial_sum, residual, gain, jobs, prelude=None):
        value = residual + depth_scale * scatter_rows(partial_sum)
        return value, gather_rows((rms_parts(value)[0] * gain).astype(jnp.bfloat16)), self.moves(*jobs), ()

    def deliver(self, rows):
        return lax.all_gather(rows.astype(jnp.bfloat16), "tensor", axis=0, tiled=True)

    def last(self, partial_sum, residual, jobs):
        return self.deliver(residual + depth_scale * scatter_rows(partial_sum)), self.moves(*jobs)

    def backward(self, partial_sum, values, grad_rows, gain, jobs, last=None):
        gain_grad, from_norm = norm_backward(values, gain, scatter_rows(partial_sum))
        grad = grad_rows + from_norm
        gathered = gather_rows((depth_scale * grad).astype(jnp.bfloat16))
        output = self.last(*last, [])[0] if last else None
        return grad, gain_grad, gathered, self.moves(*jobs), output

    def backward_last(self, partial_sum, values, grad_rows, gain, jobs):
        gain_grad, from_norm = norm_backward(values, gain, scatter_rows(partial_sum))
        return self.deliver(grad_rows + from_norm), gain_grad, self.moves(*jobs)

    def sum_gains(self, gain_grads, jobs):
        sums = lax.psum_scatter(gain_grads, ("dp", "ctx"), scatter_dimension=1, tiled=True)
        return lax.psum(sums, "tensor"), self.moves(*jobs)

    def return_grads(self, full):
        return full


def swap_halves(values):
    lane = lax.broadcasted_iota(jnp.int32, values.shape, 1)
    half = HEAD_DIM // 2
    width = values.shape[1]
    return jnp.where(lane % HEAD_DIM < half, pltpu.roll(values, width - half, 1), pltpu.roll(values, half, 1))


def head_scores(query, key, bias):
    return times_transposed(query, key) * score_scale + bias


def attend_kernel(heads, normed_ref, weight_ref, cosine_ref, sine_ref, bias_ref, partial_ref, mixed_ref, attended_ref, total_ref, wide):
    width = heads * HEAD_DIM
    lead = wide.shape[1] - width
    cosine, sine = cosine_ref[...], sine_ref[...]
    columns = mixed_ref.shape[1]
    normed = normed_ref[...]
    for first in range(0, columns, 2 * LANES):
        block = times(normed, weight_ref[:, first : first + 2 * LANES])
        for part in range(2):
            start = first + part * LANES
            tile = block[:, part * LANES : (part + 1) * LANES]
            if start < 2 * width:
                tile = tile * cosine + swap_halves(tile) * sine
            mixed_ref[:, start : start + LANES] = tile.astype(jnp.bfloat16)
    wide[:, :lead] = jnp.zeros((wide.shape[0], lead), jnp.bfloat16)
    for head in range(heads):
        low = head * HEAD_DIM
        query = mixed_ref[:, low : low + HEAD_DIM]
        key = mixed_ref[:, width + low : width + low + HEAD_DIM]
        value = mixed_ref[:, 2 * width + low : 2 * width + low + HEAD_DIM]
        scores = head_scores(query, key, bias_ref[...])
        top = jnp.max(scores, axis=-1, keepdims=True)
        terms = jnp.exp(scores - top)
        total = jnp.sum(terms, axis=-1, keepdims=True)
        probs = (terms / total).astype(jnp.bfloat16)
        wide[:, lead + low : lead + low + HEAD_DIM] = times(probs, value).astype(jnp.bfloat16)
        total_ref[:, head : head + 1] = top + jnp.log(total)
    attended_ref[...] = wide[:, lead:]
    attended = wide[...]
    for first in range(0, partial_ref.shape[1], 3 * LANES):
        partial_ref[:, first : first + 3 * LANES] = times_transposed(
            attended, weight_ref[first : first + 3 * LANES, 3 * width - lead :]
        ).astype(jnp.bfloat16)


def norm_attend_kernel(
    heads, inputs_ref, gain_ref, weight_ref, cosine_ref, sine_ref, bias_ref, partial_ref, mixed_ref, attended_ref, total_ref, normed_ref, wide
):
    rows = 128
    for first in range(0, inputs_ref.shape[0], rows):
        values = inputs_ref[first : first + rows].astype(jnp.float32)
        normed_ref[first : first + rows] = (rms_parts(values)[0] * gain_ref[...]).astype(jnp.bfloat16)
    attend_kernel(
        heads, normed_ref, weight_ref, cosine_ref, sine_ref, bias_ref, partial_ref, mixed_ref, attended_ref, total_ref, wide
    )


def attend_back_kernel(
    heads, grad_ref, weight_ref, mixed_ref, total_ref, cosine_ref, sine_ref, bias_ref, normed_ref, attended_ref, partial_ref, sums_ref, wide, turned, all_ref
):
    width = heads * HEAD_DIM
    lead = wide.shape[1] - width
    wide[...] = times(grad_ref[...], weight_ref[:, 3 * width - lead :]).astype(jnp.bfloat16)
    all_ref[:, 3 * width :] = jnp.zeros((all_ref.shape[0], all_ref.shape[1] - 3 * width), jnp.bfloat16)
    for head in range(heads):
        low = head * HEAD_DIM
        query = mixed_ref[:, low : low + HEAD_DIM]
        key = mixed_ref[:, width + low : width + low + HEAD_DIM]
        value = mixed_ref[:, 2 * width + low : 2 * width + low + HEAD_DIM]
        grad_out = wide[:, lead + low : lead + low + HEAD_DIM]
        scores = head_scores(query, key, bias_ref[...])
        probs = jnp.exp(scores - total_ref[:, head : head + 1])
        grad_probs = times_transposed(grad_out, value)
        delta = jnp.sum(probs * grad_probs, axis=-1, keepdims=True)
        grad_scores = (probs * (grad_probs - delta) * score_scale).astype(jnp.bfloat16)
        turned[:, low : low + HEAD_DIM] = times(grad_scores, key)
        turned[:, width + low : width + low + HEAD_DIM] = outer_rows(grad_scores, query)
        all_ref[:, 2 * width + low : 2 * width + low + HEAD_DIM] = outer_rows(
            probs.astype(jnp.bfloat16), grad_out
        ).astype(jnp.bfloat16)
    cosine, sine = cosine_ref[...], sine_ref[...]
    for start in range(0, 2 * width, LANES):
        tile = turned[:, start : start + LANES]
        all_ref[:, start : start + LANES] = (tile * cosine - swap_halves(tile) * sine).astype(jnp.bfloat16)
    grad_all = all_ref[...]
    for first in range(0, partial_ref.shape[1], 3 * LANES):
        partial_ref[:, first : first + 3 * LANES] = times_transposed(
            grad_all, weight_ref[first : first + 3 * LANES, : grad_all.shape[1]]
        ).astype(jnp.bfloat16)
    for first in range(0, sums_ref.shape[0], 2 * LANES):
        tile = slice(first, first + 2 * LANES)
        sums_ref[tile, : 3 * width] = outer_rows(normed_ref[:, tile], all_ref[:, : 3 * width]).astype(jnp.bfloat16)
        sums_ref[tile, 3 * width :] = outer_rows(grad_ref[:, tile], attended_ref[...]).astype(jnp.bfloat16)


def local_call(kernel, name, operands, outs, scratch, flops):
    vmem = pl.BlockSpec(memory_space=pltpu.VMEM)
    return pl.pallas_call(
        kernel,
        name=name,
        out_shape=tuple(outs),
        in_specs=[vmem] * len(operands),
        out_specs=tuple([vmem] * len(outs)),
        scratch_shapes=scratch,
        compiler_params=pltpu.CompilerParams(vmem_limit_bytes=48 * 2**20),
        cost_estimate=pl.CostEstimate(flops=flops, bytes_accessed=20 * 10**6, transcendentals=0),
    )(*operands)


def outer_kernel(*refs):
    out_ref, first = refs[-1], 0
    for left, right in zip(refs[:-1:2], refs[1:-1:2]):
        last = first + right.shape[1]
        out_ref[:, first:last] = outer_rows(left[...], right[...]).astype(out_ref.dtype)
        first = last


def outer_sums(*pairs):
    rows, width = pairs[0][0].shape
    columns = sum(right.shape[1] for _, right in pairs)
    tile = 256
    specs, operands = [], []
    for left, right in pairs:
        specs += [
            pl.BlockSpec((rows, tile), lambda i: (0, i)),
            pl.BlockSpec(right.shape, lambda i: (0, 0)),
        ]
        operands += [left, right]
    return pl.pallas_call(
        outer_kernel,
        name="outer_sums",
        grid=(width // tile,),
        out_shape=jax.ShapeDtypeStruct((width, columns), jnp.bfloat16),
        in_specs=specs,
        out_specs=pl.BlockSpec((tile, columns), lambda i: (i, 0)),
        compiler_params=pltpu.CompilerParams(vmem_limit_bytes=40 * 2**20),
        cost_estimate=pl.CostEstimate(
            flops=2 * rows * width * columns, bytes_accessed=2 * (rows + width) * columns, transcendentals=0
        ),
    )(*operands)


def attention_forward(query, key, value, bias):
    scores = jnp.einsum("qhd,khd->hqk", query, key, preferred_element_type=jnp.float32) * score_scale
    scores = scores + bias[None]
    top = jnp.max(scores, axis=-1, keepdims=True)
    terms = jnp.exp(scores - top)
    probs = terms / jnp.sum(terms, axis=-1, keepdims=True)
    attended = jnp.einsum(
        "hqk,khd->qhd", probs.astype(jnp.bfloat16), value, preferred_element_type=jnp.float32
    )
    return attended, probs


def attention_backward(query, key, value, probs, grad_out):
    grad_probs = jnp.einsum("qhd,khd->hqk", grad_out, value, preferred_element_type=jnp.float32)
    delta = jnp.sum(probs * grad_probs, axis=-1, keepdims=True)
    grad_scores = (probs * (grad_probs - delta) * score_scale).astype(jnp.bfloat16)
    grad_query = jnp.einsum("hqk,khd->qhd", grad_scores, key, preferred_element_type=jnp.float32)
    grad_key = jnp.einsum("hqk,qhd->khd", grad_scores, query, preferred_element_type=jnp.float32)
    grad_value = jnp.einsum(
        "hqk,qhd->khd", probs.astype(jnp.bfloat16), grad_out, preferred_element_type=jnp.float32
    )
    return grad_query, grad_key, grad_value


def lane_tables(tables):
    cosine, sine_table = tables[0][:, 0], tables[1][:, 0]
    return (
        jnp.concatenate([cosine] * (LANES // cosine.shape[1]), axis=1),
        jnp.concatenate([-sine_table, sine_table] * (LANES // HEAD_DIM), axis=1),
    )


def forward_attention(normed, weight, plan, bias, tables, kernels, gain):
    width = plan.head_width
    rows = normed.shape[0]
    if kernels:
        columns = (3 * width + LANES - 1) // LANES * LANES
        wide = (width + LANES - 1) // LANES * LANES
        sized = jax.ShapeDtypeStruct
        first = gain is not None
        return (
            functools.partial(norm_attend_kernel if first else attend_kernel, plan.head_count),
            [normed] + ([gain] if first else []) + [weight, *lane_tables(tables), bias],
            [
                sized((rows, columns), jnp.bfloat16),
                sized((rows, width), jnp.bfloat16),
                sized((rows, LANES), jnp.float32),
            ]
            + ([sized(normed.shape, jnp.bfloat16)] if first else []),
            [pltpu.VMEM((rows, wide), jnp.bfloat16)],
            (rows, weight.shape[0]),
        ), None
    head_shape = (rows, plan.head_count, HEAD_DIM)
    mixed = times(normed, weight[:, : 3 * width])
    query = rotate(mixed[:, :width].reshape(head_shape), tables, 1.0).astype(jnp.bfloat16)
    key = rotate(mixed[:, width : 2 * width].reshape(head_shape), tables, 1.0).astype(jnp.bfloat16)
    value = mixed[:, 2 * width :].reshape(head_shape).astype(jnp.bfloat16)
    attended, probs = attention_forward(query, key, value, bias)
    attended = attended.reshape(rows, width).astype(jnp.bfloat16)
    partial_sum = times_transposed(attended, weight[:, 3 * width :]).astype(jnp.bfloat16)
    return partial_sum, (normed, query, key, value, probs, attended)


def feed_kernel(normed_ref, gate_ref, up_ref, down_ref, partial_ref, gating_ref, upward_ref, activated_ref):
    normed = normed_ref[...]
    for first in range(0, gating_ref.shape[1], 2 * LANES):
        tile = slice(first, first + 2 * LANES)
        gating, upward = times(normed, gate_ref[:, tile]), times(normed, up_ref[:, tile])
        gating_ref[:, tile] = gating
        upward_ref[:, tile] = upward
        activated_ref[:, tile] = (jax.nn.silu(gating) * upward).astype(jnp.bfloat16)
    activated = activated_ref[...]
    for first in range(0, partial_ref.shape[1], 2 * LANES):
        tile = slice(first, first + 2 * LANES)
        partial_ref[:, tile] = times_transposed(activated, down_ref[tile, :]).astype(jnp.bfloat16)


def feed_prelude(normed, weights):
    rows, width = normed.shape
    units = weights[0].shape[1]
    sized = jax.ShapeDtypeStruct
    wide = sized((rows, units), jnp.float32)
    return (feed_kernel, [normed, *weights], [wide, wide, sized((rows, units), jnp.bfloat16)], [], (rows, width))


def forward_feed(normed, weights):
    gate_weight, up_weight, down_weight = weights
    gating, upward = times(normed, gate_weight), times(normed, up_weight)
    activated = (jax.nn.silu(gating) * upward).astype(jnp.bfloat16)
    partial_sum = times_transposed(activated, down_weight).astype(jnp.bfloat16)
    return partial_sum, (normed, gating, upward, activated)


def feed_back_kernel(
    grad_ref, normed_ref, gate_ref, up_ref, down_ref, gating_ref, upward_ref, activated_ref, partial_ref, sums_ref, gate_grad, up_grad
):
    units = gating_ref.shape[1]
    grad = grad_ref[...]
    for first in range(0, units, 2 * LANES):
        tile = slice(first, first + 2 * LANES)
        grad_act = times(grad, down_ref[:, tile])
        gating, upward = gating_ref[:, tile], upward_ref[:, tile]
        sigmoid_gate = jax.nn.sigmoid(gating)
        gate_grad[:, tile] = (grad_act * upward * sigmoid_gate * (1.0 + gating * (1.0 - sigmoid_gate))).astype(
            jnp.bfloat16
        )
        up_grad[:, tile] = (grad_act * gating * sigmoid_gate).astype(jnp.bfloat16)
    for first in range(0, partial_ref.shape[1], 2 * LANES):
        tile = slice(first, first + 2 * LANES)
        partial_ref[:, tile] = (
            times_transposed(gate_grad[...], gate_ref[tile, :]) + times_transposed(up_grad[...], up_ref[tile, :])
        ).astype(jnp.bfloat16)
        normed = normed_ref[:, tile]
        sums_ref[tile, :units] = outer_rows(normed, gate_grad[...]).astype(jnp.bfloat16)
        sums_ref[tile, units : 2 * units] = outer_rows(normed, up_grad[...]).astype(jnp.bfloat16)
        sums_ref[tile, 2 * units :] = outer_rows(grad_ref[:, tile], activated_ref[...]).astype(jnp.bfloat16)


def feed_both_kernel(
    normed_ref, gate_ref, up_ref, down_ref, grad_ref, last_ref, partial_ref, sums_ref, gating, upward, activated, gate_grad, up_grad
):
    feed_kernel(normed_ref, gate_ref, up_ref, down_ref, last_ref, gating, upward, activated)
    feed_back_kernel(
        grad_ref, normed_ref, gate_ref, up_ref, down_ref, gating, upward, activated, partial_ref, sums_ref, gate_grad, up_grad
    )


def feed_both(normed, weights, down_grad):
    rows, width = normed.shape
    units = weights[0].shape[1]
    sized = jax.ShapeDtypeStruct
    partial_sum = sized((rows, width), jnp.bfloat16)
    outs, _ = work_call(
        feed_both_kernel,
        "feed_both",
        None,
        [normed, *weights, down_grad],
        [partial_sum, partial_sum, sized((width, 3 * units), jnp.bfloat16)],
        [pltpu.VMEM((rows, units), jnp.float32)] * 2 + [pltpu.VMEM((rows, units), jnp.bfloat16)] * 3,
        [],
    )
    return outs


def backward_feed_beside(down_grad, weights, record, number, jobs):
    normed, gating, upward, activated = record
    rows, width = down_grad.shape
    units = gating.shape[1]
    sized = jax.ShapeDtypeStruct
    return work_call(
        feed_back_kernel,
        "feed_back",
        number,
        [down_grad, normed, *weights, gating, upward, activated],
        [sized((rows, width), jnp.bfloat16), sized((width, 3 * units), jnp.bfloat16)],
        [pltpu.VMEM((rows, units), jnp.bfloat16)] * 2,
        jobs,
    )


def backward_feed(down_grad, weights, record):
    gate_weight, up_weight, down_weight = weights
    normed, gating, upward, activated = record
    grad_act = times(down_grad, down_weight)
    sigmoid_gate = jax.nn.sigmoid(gating)
    grad_gating = (grad_act * upward * sigmoid_gate * (1.0 + gating * (1.0 - sigmoid_gate))).astype(jnp.bfloat16)
    grad_upward = (grad_act * gating * sigmoid_gate).astype(jnp.bfloat16)
    partial_sum = (times_transposed(grad_gating, gate_weight) + times_transposed(grad_upward, up_weight)).astype(
        jnp.bfloat16
    )
    return partial_sum, ((normed, grad_gating), (normed, grad_upward), (down_grad, activated))


def backward_attention(branch_grad, weight, record, plan, bias, tables, kernels, jobs):
    width = plan.head_width
    rows = branch_grad.shape[0]
    if kernels:
        normed, mixed, attended, total = record
        wide = (width + LANES - 1) // LANES * LANES
        sized = jax.ShapeDtypeStruct
        (partial_sum, sums), moved = work_call(
            functools.partial(attend_back_kernel, plan.head_count),
            "attend_back",
            kernels.next_number() if jobs else None,
            [branch_grad, weight, mixed, total, *lane_tables(tables), bias, normed, attended],
            [sized((rows, weight.shape[0]), jnp.bfloat16), sized((weight.shape[0], 4 * width), jnp.bfloat16)],
            [
                pltpu.VMEM((rows, wide), jnp.bfloat16),
                pltpu.VMEM((rows, 2 * width), jnp.float32),
                pltpu.VMEM(mixed.shape, jnp.bfloat16),
            ],
            jobs,
        )
        return partial_sum, sums, moved
    normed, query, key, value, probs, attended = record
    grad_mixed = times(branch_grad, weight[:, 3 * width :]).astype(jnp.bfloat16)
    grad_query, grad_key, grad_value = attention_backward(
        query, key, value, probs, grad_mixed.reshape(query.shape)
    )
    grad_all = jnp.concatenate(
        [
            rotate(grad_query, tables, -1.0).reshape(rows, width),
            rotate(grad_key, tables, -1.0).reshape(rows, width),
            grad_value.reshape(rows, width),
        ],
        axis=1,
    ).astype(jnp.bfloat16)
    partial_sum = times_transposed(grad_all, weight[:, : 3 * width]).astype(jnp.bfloat16)
    return partial_sum, outer_sums((normed, grad_all), (branch_grad, attended)), None


def body(
    inputs,
    cotangent,
    lengths,
    dealing,
    span_table,
    prenorm_gain,
    query_weight,
    keys_weight,
    values_weight,
    project_weight,
    postnorm_gain,
    gating_weight,
    upward_weight,
    downward_weight,
):
    n_dp, n_ctx, n_ten = lax.axis_size("dp"), lax.axis_size("ctx"), lax.axis_size("tensor")
    plan = Plan(n_dp, n_ctx, query_weight.shape[2], gating_weight.shape[2])
    own_rows = inputs.shape[0]
    half_span = own_rows // 2
    share = own_rows // n_ten
    group_index = lax.axis_index("dp")
    core = lax.axis_index("tensor")
    seq_count = lengths.shape[0] // n_dp
    starts, seq_lens = group_layout(lengths, dealing, group_index, seq_count)
    span_row = lax.dynamic_index_in_dim(span_table, group_index, 0, keepdims=False)
    facts = slot_facts(slots_for(own_rows * n_ctx, span_row, half_span), starts, seq_lens)
    tables = rope_tables(facts[2], HEAD_DIM // 2)
    bias = jnp.where(allowed(facts, facts), 0.0, masked_score)

    kernels = (n_dp, n_ctx, n_ten) == (4, 4, 2)
    comm = LineComm() if kernels else PlainComm()
    head_cuts = [cut * HEAD_DIM for cut in plan.head_cuts]

    attention_stack = [query_weight, keys_weight, values_weight, project_weight.transpose(0, 2, 1)]
    feed_stack = [gating_weight, upward_weight, downward_weight.transpose(0, 2, 1)]

    def windows(layer):
        attention = [cut_windows(weight[layer], head_cuts, plan.head_width) for weight in attention_stack]
        feed = [cut_windows(weight[layer], plan.unit_cuts, plan.unit_width) for weight in feed_stack]
        return [jnp.concatenate(attention, axis=2)] + feed

    def joined(blocks):
        return blocks.reshape(-1, blocks.shape[-1])

    if kernels:
        later_windows, moved = start_call(
            plan, comm.next_number(), attention_stack + feed_stack, prenorm_gain, postnorm_gain, inputs
        )
        inputs_whole, attention_blocks, gain_blocks, gate, up, down = moved
        gains = gain_blocks[:, : 2 * LAYERS, : prenorm_gain.shape[1]].transpose(1, 0, 2).reshape(2 * LAYERS, -1)
    else:
        attention_windows, gate, up, down = windows(0)
        later_windows = [windows(layer) for layer in range(1, LAYERS)]
        attention_blocks, inputs_whole, gate, up, down = comm.moves(
            (Fetch, attention_windows), (Collect, inputs), (Fetch, gate), (Exchange, up), (Exchange, down)
        )
        gains = lax.all_gather(
            jnp.concatenate([prenorm_gain, postnorm_gain], axis=0), ("dp", "ctx"), axis=1, tiled=True
        )
    gains = gains.astype(jnp.float32)
    front = [gains[layer : layer + 1] for layer in range(LAYERS)]
    behind = [gains[LAYERS + layer : LAYERS + layer + 1] for layer in range(LAYERS)]
    attention_weights, feed_weights = [None] * LAYERS, [None] * LAYERS
    attention_records, feed_records, middles = [None] * LAYERS, [None] * LAYERS, [None] * LAYERS
    starts_of = [None] * LAYERS

    attention_weights[0] = joined(attention_blocks)
    residual = comm.own_rows(inputs_whole).astype(jnp.float32)
    normed = inputs_whole
    if not kernels:
        normed = (rms_parts(inputs_whole.astype(jnp.float32))[0] * front[0]).astype(jnp.bfloat16)
    for layer in range(LAYERS):
        starts_of[layer] = residual
        more = layer + 1 < LAYERS
        partial_sum, attention_records[layer] = forward_attention(
            normed, attention_weights[layer], plan, bias, tables, kernels, None if layer else front[0]
        )
        prelude = partial_sum if kernels else None
        jobs = [(Spread, up, 6, 2), (Spread, down, 14, 2)]
        if more:
            next_windows = later_windows[layer]
            jobs += [(Exchange, next_windows[0]), (Exchange, next_windows[1])]
        else:
            jobs += [(Collect, cotangent, 5, 4)]
        hidden, normed_two, (up, down, *moved), made = comm.forward(
            None if kernels else partial_sum, residual, behind[layer], jobs, prelude
        )
        if kernels:
            attention_records[layer] = (made[3] if layer == 0 else normed, *made[:3])
        normed = normed_two
        feed_weights[layer] = [joined(blocks) for blocks in (gate, up, down)]
        middles[layer] = hidden
        if more:
            jobs = [
                (Spread, moved[0], 8, 3),
                (Spread, moved[1], 19, 2),
                (Exchange, next_windows[2]),
                (Exchange, next_windows[3]),
            ]
            prelude, partial_sum = None, None
            if kernels:
                prelude = feed_prelude(normed, feed_weights[layer])
            else:
                partial_sum, feed_records[layer] = forward_feed(normed, feed_weights[layer])
            residual, normed_next, moved, made = comm.forward(partial_sum, hidden, front[layer + 1], jobs, prelude)
            if kernels:
                feed_records[layer] = (normed, *made)
            normed = normed_next
            attention_weights[layer + 1] = joined(moved[0])
            gate, up, down = moved[1:]
        else:
            if kernels:
                feed_records[layer] = (normed,)
            else:
                last_sum, feed_records[layer] = forward_feed(normed, feed_weights[layer])
            cotangent_whole = moved[0]

    grad_rows = comm.own_rows(cotangent_whole).astype(jnp.float32)
    down_grad = (depth_scale * cotangent_whole.astype(jnp.float32)).astype(jnp.bfloat16)
    gain_fronts, gain_backs, attention_parts, feed_parts = [[None] * LAYERS for _ in range(4)]
    for layer in reversed(range(LAYERS)):
        more, last_layer = layer > 0, layer + 1 == LAYERS
        own_width = query_weight.shape[1]
        cut_feed, cut_attention = own_width * 5 // 9 // 16 * 16, own_width // 2 // 16 * 16

        def two(whole, cut):
            if last_layer:
                return [], []
            return [(exchange_rows(0, cut), whole)], [(exchange_rows(cut, own_width), whole)]

        beside, in_line = two(feed_parts[layer + 1] if not last_layer else None, cut_feed)
        if kernels and last_layer:
            last_sum, partial_sum, sums = feed_both(feed_records[layer][0], feed_weights[layer], down_grad)
        elif kernels:
            (partial_sum, sums), upper = backward_feed_beside(
                down_grad, feed_weights[layer], feed_records[layer], comm.next_number(), beside
            )
        else:
            partial_sum, pairs = backward_feed(down_grad, feed_weights[layer], feed_records[layer])
            sums = outer_sums(*pairs)
            upper = comm.moves(*beside) if beside else ()
        partial_sum, sums = lax.optimization_barrier((partial_sum, sums))
        feed_sums = reduce_grads(sums, n_ctx)
        grad_rows, gain_backs[layer], branch_grad, lower, last_output = comm.backward(
            partial_sum,
            middles[layer],
            grad_rows,
            behind[layer],
            in_line,
            None if more else (last_sum, middles[LAYERS - 1]),
        )
        if beside:
            feed_parts[layer + 1] = [upper[0], lower[0]]
        if not more:
            output = last_output
        beside, in_line = two(attention_parts[layer + 1] if not last_layer else None, cut_attention)
        partial_sum, sums, upper = backward_attention(
            branch_grad,
            attention_weights[layer],
            attention_records[layer],
            plan,
            bias,
            tables,
            comm if kernels else None,
            beside,
        )
        if beside and upper is None:
            upper = comm.moves(*beside)
        partial_sum, sums = lax.optimization_barrier((partial_sum, sums))
        attention_sums = reduce_grads(sums, n_ctx)
        if more:
            grad_rows, gain_fronts[layer], down_grad, lower, _ = comm.backward(
                partial_sum, starts_of[layer], grad_rows, front[layer], in_line
            )
        else:
            grad_inputs, gain_fronts[layer], lower = comm.backward_last(
                partial_sum, starts_of[layer], grad_rows, front[layer], in_line
            )
        if beside:
            attention_parts[layer + 1] = [upper[0], lower[0]]
        feed_parts[layer], attention_parts[layer] = feed_sums, attention_sums
    feed_parts[0], grad_inputs = lax.optimization_barrier((feed_parts[0], grad_inputs))
    feed_parts[0] = comm.moves((Exchange, feed_parts[0]))
    attention_parts[0], feed_parts[0] = lax.optimization_barrier((attention_parts[0], feed_parts[0]))
    gain_sums, attention_parts[0] = comm.sum_gains(
        jnp.concatenate(gain_fronts + gain_backs, axis=0), [(Exchange, attention_parts[0])]
    )
    grad_inputs = grad_inputs.astype(jnp.float32)

    if kernels:
        joins = join_layers(plan, attention_parts, feed_parts)
    else:

        def spread(parts, index, width, cuts):
            return jnp.stack(
                [
                    join_windows(jnp.concatenate(part, axis=1)[:, :, index * width : (index + 1) * width], cuts)
                    for part in parts
                ]
            ).astype(jnp.float32)

        joins = [spread(attention_parts, i, plan.head_width, head_cuts) for i in range(4)]
        joins += [spread(feed_parts, i, plan.unit_width, plan.unit_cuts) for i in range(3)]
    query_out, keys_out, values_out, project_out, gating_out, upward_out, downward_out = joins
    return (
        output,
        grad_inputs,
        gain_sums[:LAYERS],
        query_out,
        keys_out,
        values_out,
        project_out.transpose(0, 2, 1),
        gain_sums[LAYERS:],
        gating_out,
        upward_out,
        downward_out.transpose(0, 2, 1),
    )


def solution(mesh):
    rows = P(("dp", "ctx"), None)
    gain = P(None, ("dp", "ctx"))
    wide = P(None, ("dp", "ctx"), "tensor")
    tall = P(None, "tensor", ("dp", "ctx"))
    weights = (gain, wide, wide, wide, tall, gain, wide, wide, tall)
    return jax.shard_map(
        body,
        mesh=mesh,
        in_specs=(rows, rows, P(), P(), P()) + weights,
        out_specs=(rows, rows) + weights,
        check_vma=False,
    )
```
